32 devices in a mesh: batch: 4 (over z), fsdp: 8 (over y, x, core).
Axes of the slice: x: 2, y: 2, z: 4, core: 2. Of those that a mesh axis runs over, the one named last changes fastest.
Arguments:
- tokens: bfloat16 [64, 512, 768], P(('batch', 'fsdp')), may hold values from -6 to 6
- seg_ids: int32 [64, 512], P(('batch', 'fsdp')), may hold values from 0 to 7, never falling along the last dimension, each value on 1 to 128 neighbouring positions
- positive: int32 [512], P(('batch', 'fsdp')), may hold values from 0 to 511, as said below
- out_grad: bfloat16 [64, 512, 768], P(('batch', 'fsdp')), may hold values from -6 to 6
- w_qkv: bfloat16 [768, 2304], P('fsdp'), may hold values from -0.3125 to 0.3125
- b_qv: bfloat16 [1536], P('fsdp'), may hold values from -3 to 3
- w_out: bfloat16 [768, 768], P('fsdp'), may hold values from -0.875 to 0.875
- b_out: bfloat16 [768], P('fsdp'), may hold values from -3 to 3
- norm1_gain: bfloat16 [768], P('fsdp'), may hold values from 0.25 to 1.75
- norm1_shift: bfloat16 [768], P('fsdp'), may hold values from -3 to 3
- w_up: bfloat16 [768, 3072], P('fsdp'), may hold values from -0.21875 to 0.21875
- b_up: bfloat16 [3072], P('fsdp'), may hold values from -3 to 3
- w_down: bfloat16 [3072, 768], P('fsdp'), may hold values from -0.15625 to 0.15625
- b_down: bfloat16 [768], P('fsdp'), may hold values from -3 to 3
- norm2_gain: bfloat16 [768], P('fsdp'), may hold values from 0.25 to 1.75
- norm2_shift: bfloat16 [768], P('fsdp'), may hold values from -3 to 3
Outputs:
- result_out: bfloat16 [64, 512, 768], P(('batch', 'fsdp'))
- pair_loss: float32 [512], P(('batch', 'fsdp'))
- grad_tokens: float32 [64, 512, 768], P(('batch', 'fsdp'))
- grad_wqkv: float32 [768, 2304], P('fsdp')
- grad_bqv: float32 [1536], P('fsdp')
- grad_wout: float32 [768, 768], P('fsdp')
- grad_bout: float32 [768], P('fsdp')
- grad_gain1: float32 [768], P('fsdp')
- grad_shift1: float32 [768], P('fsdp')
- grad_wup: float32 [768, 3072], P('fsdp')
- grad_bup: float32 [3072], P('fsdp')
- grad_wdown: float32 [3072, 768], P('fsdp')
- grad_bdown: float32 [768], P('fsdp')
- grad_gain2: float32 [768], P('fsdp')
- grad_shift2: float32 [768], P('fsdp')
The draws below stay inside these ranges and needn't reach their ends.
Inputs may be any that keep to these rules, and one draw needn't show every extreme that they name: `positive`: a permutation of the 512 segments in one cycle: no segment is its own partner.
All inputs are finite; a program needn't handle non-finite values.
Results may differ from the reference program's by a relative error of at most 0.013.
Values may be sent and summed in bfloat16 or wider, within the bound.
No kernel may reach another device: no remote copies, remote signals or barrier semaphores. Data moves between devices by JAX's collectives and lax.ppermute only.
A program may use at most 192 MiB of HBM per device.

```python
import math
import jax
import jax.numpy as jnp
import numpy as np
from jax import lax

D = 768
HEADS = 12
HEAD = 64
FF = 3072
LEN = 512
SEGS = 8
MOST = 128
ROWS = 64
SEGMENTS = 512


def draw_positive(key, part):
    key = jax.random.fold_in(key, 11)
    ordering = jax.random.permutation(key, SEGMENTS)
    position = jnp.argsort(ordering)
    return jnp.roll(ordering, -1)[position].astype(jnp.int32)


def shard_levels(stream_key, dims, cuts, smallest, top_value):
    def one(dim, parts):
        heights = jax.random.uniform(jax.random.fold_in(jax.random.fold_in(stream_key, 6), dim), (parts,), jnp.float32, smallest / len(cuts), top_value / len(cuts))
        return jnp.repeat(jnp.exp(heights), dims[dim] // parts).reshape((-1,) + (1,) * (len(dims) - dim - 1))

    factor_of = one(*cuts[0])
    for cut in cuts[1:]:
        factor_of = factor_of * one(*cut)
    return factor_of


def length_profile(count, total, bound, slope):
    weights = [(1 << 20) // math.isqrt(standing ** slope) + 1 for standing in range(2, count + 1)]
    spare, holding = total - bound - (count - 1), [1] * (count - 1)
    while spare > 0:
        free = [i for i in range(count - 1) if holding[i] < bound]
        mass, left = sum([weights[i] for i in free]), spare
        for i in free:
            more = min(bound - holding[i], max(1, left * weights[i] // mass), spare)
            holding[i] = holding[i] + more
            spare = spare - more
    return np.array([bound] + holding)


def uneven_parts(own_key, amount, total, most, lean):
    if amount == 2:
        one = jax.random.randint(own_key, (), max(1, total - most), min(most, total - 1) + 1)
        return jnp.stack([one, total - one])
    lengths = jnp.asarray(length_profile(amount, total, most, lean), jnp.int32)
    pairs = (amount - 1) // 2
    donor, taker = lengths[1:1 + 2 * pairs:2], lengths[2:2 + 2 * pairs:2]
    margin = jnp.minimum(donor - 1, most - taker)
    moved = jax.random.randint(jax.random.fold_in(own_key, 1), (pairs,), 0, 1 << 20) % (margin + 1)
    lengths = lengths.at[1:1 + 2 * pairs:2].set(donor - moved).at[2:2 + 2 * pairs:2].set(taker + moved)
    return lengths[jax.random.permutation(jax.random.fold_in(own_key, 2), amount)]


def noise(key, extent, scale, bound, split=(), kind=jnp.bfloat16):
    level = shard_levels(key, extent, split, -0.22, 0.18) if split else 1.0
    drawn = jax.random.normal(key, extent, jnp.float32) * scale * level
    return jnp.minimum(jnp.maximum(drawn, -bound), bound).astype(kind)


def setup_inputs(seed: int = 0) -> dict:
    seeds = jax.random.split(jax.random.key(seed), 17)
    tokens = noise(seeds[0], (ROWS, LEN, D), 1.0, 6.0, ((0, 32),))
    seg_ids = jax.vmap(lambda own: jnp.searchsorted(jnp.cumsum(uneven_parts(own, SEGS, LEN, MOST, 1)), jnp.arange(LEN), side="right"))(jax.random.split(seeds[1], ROWS)).reshape((ROWS, LEN)).astype(jnp.int32)
    positive = draw_positive(jax.random.fold_in(seeds[16], 71), 0)
    out_grad = noise(seeds[3], (ROWS, LEN, D), 1.0, 6.0, ((0, 32),))
    w_qkv = noise(seeds[4], (D, 3 * D), (D // 2) ** -0.5, 0.3125, ((0, 8),))
    b_qv = noise(seeds[5], (2 * D,), 0.5, 3.0, ((0, 8),))
    w_out = noise(seeds[6], (D, D), (D // 16) ** -0.5, 0.875, ((0, 8),))
    b_out = noise(seeds[7], (D,), 0.5, 3.0, ((0, 8),))
    norm1_gain = jnp.clip(1.0 + 0.15 * jax.random.normal(seeds[8], (D,), jnp.float32), 0.25, 1.75).astype(jnp.bfloat16)
    norm1_shift = noise(seeds[9], (D,), 0.5, 3.0, ((0, 8),))
    w_up = noise(seeds[10], (D, FF), D ** -0.5, 0.21875, ((0, 8),))
    b_up = noise(seeds[11], (FF,), 0.5, 3.0, ((0, 8),))
    w_down = noise(seeds[12], (FF, D), (FF // 2) ** -0.5, 0.15625, ((0, 8),))
    b_down = noise(seeds[13], (D,), 0.5, 3.0, ((0, 8),))
    norm2_gain = jnp.clip(1.0 + 0.15 * jax.random.normal(seeds[14], (D,), jnp.float32), 0.25, 1.75).astype(jnp.bfloat16)
    norm2_shift = noise(seeds[15], (D,), 0.5, 3.0, ((0, 8),))
    return dict(tokens=tokens, seg_ids=seg_ids, positive=positive, out_grad=out_grad, w_qkv=w_qkv, b_qv=b_qv, w_out=w_out, b_out=b_out, norm1_gain=norm1_gain, norm1_shift=norm1_shift, w_up=w_up, b_up=b_up, w_down=w_down, b_down=b_down, norm2_gain=norm2_gain, norm2_shift=norm2_shift)


@jax.custom_vjp
def low(v):
    return lax.optimization_barrier(v.astype(jnp.bfloat16)).astype(jnp.float32)

@jax.custom_vjp
def low_back(v):
    return v

def low_keep(v):
    return (low(v), None)

def low_pass(kept, grad):
    return (grad,)

def back_keep(v):
    return (v, None)

def back_low(kept, grad):
    return (low(grad),)
low.defvjp(low_keep, low_pass)
low_back.defvjp(back_keep, back_low)
norm_eps = 1e-06
pool_eps = 1e-06
score_scale = 50.0
pair_weight = 256.0
masked_value = -1000000000.0

def matmul_exact(left, right):
    return jnp.dot(left, right, precision=lax.Precision.HIGHEST, preferred_element_type=jnp.float32)

def scale_rows(values):
    row_mean = lax.optimization_barrier(jnp.mean(values, axis=-1, keepdims=True))
    centred = values - row_mean
    spread = lax.optimization_barrier(jnp.mean(centred * centred, axis=-1, keepdims=True))
    return centred * lax.rsqrt(spread + norm_eps)

def layer_norm(values, gain, shift):
    return scale_rows(values) * gain + shift

def attend_row(pieces):
    queries, key_rows, values, row_ids = pieces
    inv_root = 1.0 / math.sqrt(HEAD)
    scores = jnp.einsum('qhd,khd->hqk', queries, key_rows, precision=lax.Precision.HIGHEST) * inv_root
    scores = low_back(scores)
    same_seg = row_ids[:, None] == row_ids[None, :]
    scores = jnp.where(same_seg[None], scores, masked_value)
    row_max = lax.optimization_barrier(jnp.max(scores, axis=-1, keepdims=True))
    exp_terms = jnp.exp(scores - row_max)
    attn_probs = low(exp_terms / lax.optimization_barrier(jnp.sum(exp_terms, axis=-1, keepdims=True)))
    return jnp.einsum('hqk,khd->qhd', attn_probs, values, precision=lax.Precision.HIGHEST)

def forward(tokens, w_qkv, b_qv, w_out, b_out, gain_one, shift_one, w_up, b_up, w_down, b_down, gain_two, shift_two, seg_ids, positive):
    token_rows = tokens.reshape(ROWS * LEN, D)
    zero_bias = jnp.zeros((D,), jnp.float32)
    qkv_bias = jnp.concatenate([b_qv[:D], zero_bias, b_qv[D:]])
    qkv_rows = low_back(low(matmul_exact(token_rows, w_qkv) + qkv_bias))
    qkv_split = qkv_rows.reshape(ROWS, LEN, 3, HEADS, HEAD)
    context = lax.map(jax.checkpoint(attend_row), (qkv_split[:, :, 0], qkv_split[:, :, 1], qkv_split[:, :, 2], seg_ids))
    context_b = low_back(low(context.reshape(ROWS * LEN, D)))
    attn_out = low_back(matmul_exact(context_b, w_out) + b_out)
    hidden = layer_norm(token_rows + attn_out, gain_one, shift_one)
    up_pre = low_back(matmul_exact(low(hidden), w_up) + b_up)
    activated = low(jax.nn.gelu(up_pre, approximate=False))
    down_out = low_back(matmul_exact(activated, w_down) + b_down)
    result = layer_norm(hidden + down_out, gain_two, shift_two)
    grid_rows = result.reshape(ROWS, LEN, D)
    member = (seg_ids[:, None, :] == jnp.arange(SEGS, dtype=jnp.int32)[None, :, None]).astype(jnp.float32)
    sums = jnp.einsum('rsl,rld->rsd', member, grid_rows, precision=lax.Precision.HIGHEST)
    pooled = (sums / lax.optimization_barrier(jnp.sum(member, axis=-1, keepdims=True))).reshape(SEGMENTS, D)
    embedding = low(pooled * lax.rsqrt(lax.optimization_barrier(jnp.mean(pooled * pooled, axis=-1, keepdims=True)) + pool_eps))
    logits = low_back(matmul_exact(embedding, embedding.T) * (score_scale / D))
    seg_index = jnp.arange(SEGMENTS, dtype=jnp.int32)
    logits = jnp.where(seg_index[:, None] == seg_index[None, :], masked_value, logits)
    row_max = lax.optimization_barrier(jnp.max(logits, axis=-1, keepdims=True))
    log_total = row_max[:, 0] + jnp.log(lax.optimization_barrier(jnp.sum(jnp.exp(logits - row_max), axis=-1)))
    picked = jnp.take_along_axis(logits, positive[:, None].astype(jnp.int32), axis=1)[:, 0]
    return (result.reshape(ROWS, LEN, D), log_total - picked)

def reference(tokens, seg_ids, positive, out_grad, w_qkv, b_qv, w_out, b_out, norm1_gain, norm1_shift, w_up, b_up, w_down, b_down, norm2_gain, norm2_shift):

    def objective(a0, a1, a2, a3, a4, a5, a6, a7, a8, a9, a10, a11, a12):
        return forward(a0, a1, a2, a3, a4, a5, a6, a7, a8, a9, a10, a11, a12, seg_ids, positive)
    (result, pair_loss), pull = jax.vjp(objective, tokens.astype(jnp.float32), w_qkv.astype(jnp.float32), b_qv.astype(jnp.float32), w_out.astype(jnp.float32), b_out.astype(jnp.float32), norm1_gain.astype(jnp.float32), norm1_shift.astype(jnp.float32), w_up.astype(jnp.float32), b_up.astype(jnp.float32), w_down.astype(jnp.float32), b_down.astype(jnp.float32), norm2_gain.astype(jnp.float32), norm2_shift.astype(jnp.float32))
    grads = pull((out_grad.astype(jnp.float32), jnp.full(pair_loss.shape, pair_weight, jnp.float32)))
    return (result.astype(jnp.bfloat16), pair_loss, grads[0], grads[1], grads[2], grads[3], grads[4], grads[5], grads[6], grads[7], grads[8], grads[9], grads[10], grads[11], grads[12])
```

```python
import functools
import math

import jax
import jax.numpy as jnp
from jax import lax
from jax.experimental import pallas as pl
from jax.experimental.pallas import tpu as pltpu
from jax.sharding import PartitionSpec as P

HEADS = 12
SEGS = 8

norm_eps = 1e-06
pool_eps = 1e-06
score_scale = 50.0
pair_weight = 256.0
masked_value = -1000000000.0

BLOCKS = 8
TILE = 128
TAIL = 128
BASE = 64

bf16 = jnp.bfloat16
f32 = jnp.float32
ANY = pl.BlockSpec(memory_space=pl.ANY)
VMEM_BYTES = 56 * 1024 * 1024


def dot(left, right):
    return jnp.dot(left, right, preferred_element_type=f32)


def dot_nt(left, right):
    return lax.dot_general(left, right, (((1,), (1,)), ((), ())), preferred_element_type=f32)


def whole(shape):
    return pl.BlockSpec(shape, lambda *_: (0,) * len(shape))


def call(kernel, grid, in_specs, out_specs, out_shape, scratch, flops, moved, special=0):
    return pl.pallas_call(
        kernel,
        out_shape=out_shape,
        grid_spec=pltpu.PrefetchScalarGridSpec(
            num_scalar_prefetch=1,
            grid=grid,
            in_specs=in_specs,
            out_specs=out_specs,
            scratch_shapes=scratch,
        ),
        compiler_params=pltpu.CompilerParams(vmem_limit_bytes=VMEM_BYTES),
        cost_estimate=pl.CostEstimate(
            flops=int(flops), bytes_accessed=int(moved), transcendentals=int(special)
        ),
    )


def shaped(shape, dtype):
    return jax.ShapeDtypeStruct(shape, dtype)


def swap(value, axis, size, bit):
    return lax.ppermute(value, axis, [(i, i ^ bit) for i in range(size)])


def fsdp_swap(value, bit):
    return swap(value, "fsdp", BLOCKS, bit)


def gather_first(shard):
    return fsdp_swap(shard, 2), fsdp_swap(shard, 4)


def gather_second(shard, over_x, over_y):
    rows = shard.shape[0]
    half = rows // 2
    far_top = fsdp_swap(over_y[:half], 2)
    far_low = fsdp_swap(over_x[half:], 4)
    mine = [
        (shard, 0, 0),
        (over_x, 2, 0),
        (over_y, 4, 0),
        (far_top, 6, 0),
        (far_low, 6, half),
    ]
    theirs = [(fsdp_swap(value, 1), place ^ 1, off) for value, place, off in mine]
    return mine + theirs


def gather_whole(shard):
    full = lax.all_gather(shard, "fsdp", axis=0, tiled=True)
    rows = full.shape[0] // BLOCKS
    return [(full[i * rows : (i + 1) * rows], i, 0) for i in range(BLOCKS)]


def meta_of(pieces):
    return tuple((place, off, value.shape[0]) for value, place, off in pieces)


def arrays_of(pieces):
    return [value for value, _, _ in pieces]


def load(meta, rows, refs, target, sems, index):
    copies = []
    for number, ((place, off, count), ref) in enumerate(zip(meta, refs)):
        start = pl.multiple_of((index ^ place) * rows + off, 16)
        copies.append(pltpu.make_async_copy(ref, target.at[pl.ds(start, count)], sems.at[number]))
    for copy in copies:
        copy.start()
    return copies


def fill_mask(seg_row, mask_ref):
    length = seg_row.shape[1]
    keys = jnp.broadcast_to(seg_row, (TILE, length)).T
    for lo, hi, at in bands(length):
        same = keys[lo:hi] == seg_row[:, at : at + TILE]
        mask_ref[lo:hi, at : at + TILE] = jnp.where(same, 0.0, masked_value)


def bands(length):
    out = []
    for at in range(0, length, TILE):
        out.append((max(at - TILE, 0), min(at + 2 * TILE, length), at))
    return out


def two_heads(pair):
    lane = lax.broadcasted_iota(jnp.int32, (1, pair.shape[1]), 1)
    first = (lane < pair.shape[1] // 2).astype(f32).astype(bf16)
    return jnp.concatenate([pair * first, pair * (1.0 - first)], axis=0)


def twice(value):
    return jnp.concatenate([value, value], axis=1)


def attend_kernel(meta, index_ref, tok_ref, bias_ref, seg_ref, *rest):
    pieces, rest = rest[: len(meta)], rest[len(meta) :]
    qkv_ref, ctx_ref, lse_ref, w_ref, vt_ref, ct_ref, mask_ref, sems = rest
    width = tok_ref.shape[1]
    length = tok_ref.shape[0]
    pairs = HEADS // 2
    lanes = width // pairs
    half = lanes // 2

    @pl.when(pl.program_id(0) == 0)
    def _():
        for copy in load(meta, width // BLOCKS, pieces, w_ref, sems, index_ref[0]):
            copy.wait()

    fill_mask(seg_ref[0].astype(f32), mask_ref)
    inv_root = 1.0 / math.sqrt(half)
    for part in range(3):
        cols = slice(part * width, (part + 1) * width)
        value = dot(tok_ref[...], w_ref[:, cols]) + bias_ref[:, cols]
        if part == 0:
            value = value * inv_root
        qkv_ref[:, cols] = value.astype(bf16)
    vt_ref[...] = qkv_ref[:, 2 * width :].T

    def one_pair(pair, carry):
        at_q = pl.multiple_of(pair * lanes, lanes)
        at_k = pl.multiple_of(width + pair * lanes, lanes)
        for lo, hi, at in bands(length):
            queries = two_heads(qkv_ref[at : at + TILE, pl.ds(at_q, lanes)])
            scores = dot_nt(qkv_ref[lo:hi, pl.ds(at_k, lanes)], queries)
            scores = scores + twice(mask_ref[lo:hi, at : at + TILE])
            top = jnp.max(scores, axis=0, keepdims=True)
            terms = jnp.exp(scores - top)
            total = jnp.sum(terms, axis=0, keepdims=True)
            probs = (terms * (1.0 / total)).astype(bf16)
            context = dot(vt_ref[pl.ds(at_q, lanes), lo:hi], probs)
            lse = top + jnp.log(total)
            for head in range(2):
                rows = pl.ds(pl.multiple_of(at_q + head * half, half), half)
                part = context[head * half : (head + 1) * half, head * TILE : (head + 1) * TILE]
                ct_ref[rows, at : at + TILE] = part.astype(bf16)
                lse_ref[0, pair, head : head + 1, at : at + TILE] = lse[
                    :, head * TILE : (head + 1) * TILE
                ]
        return carry

    lax.fori_loop(0, pairs, one_pair, 0)
    ctx_ref[...] = ct_ref[...].T


def attend(index, tokens, bias, seg_rows, pieces):
    count, width = tokens.shape
    rows, _, length = seg_rows.shape
    pairs = HEADS // 2
    meta = meta_of(pieces)
    return call(
        functools.partial(attend_kernel, meta),
        (rows,),
        [
            pl.BlockSpec((length, width), lambda i, s: (i, 0)),
            whole((1, 3 * width)),
            pl.BlockSpec((1, 1, length), lambda i, s: (i, 0, 0)),
        ]
        + [ANY] * len(meta),
        [
            pl.BlockSpec((length, 3 * width), lambda i, s: (i, 0)),
            pl.BlockSpec((length, width), lambda i, s: (i, 0)),
            pl.BlockSpec((1, pairs, 2, length), lambda i, s: (i, 0, 0, 0)),
        ],
        [
            shaped((count, 3 * width), bf16),
            shaped((count, width), bf16),
            shaped((rows, pairs, 2, length), f32),
        ],
        [
            pltpu.VMEM((width, 3 * width), bf16),
            pltpu.VMEM((width, length), bf16),
            pltpu.VMEM((width, length), bf16),
            pltpu.VMEM((length, length), f32),
            pltpu.SemaphoreType.DMA((len(meta),)),
        ],
        count * width * width * 6 + count * length * width * 4,
        count * width * 10 + width * width * 6,
        count * length * HEADS * 5 // 8,
    )(index, tokens, bias, seg_rows, *arrays_of(pieces))


def row_stats(values):
    mean = jnp.mean(values, axis=-1, keepdims=True)
    centred = values - mean
    spread = jnp.mean(centred * centred, axis=-1, keepdims=True)
    return centred, lax.rsqrt(spread + norm_eps)


def project_kernel(meta, index_ref, ctx_ref, tok_ref, vec_ref, *rest):
    pieces, rest = rest[: len(meta)], rest[len(meta) :]
    norm_ref, root_ref, hid_ref, w_ref, sems = rest

    @pl.when(pl.program_id(0) == 0)
    def _():
        rows = w_ref.shape[0] // BLOCKS
        for copy in load(meta, rows, pieces, w_ref, sems, index_ref[0]):
            copy.wait()

    summed = tok_ref[...].astype(f32) + (dot(ctx_ref[...], w_ref[...]) + vec_ref[0:1])
    centred, root = row_stats(summed)
    normed = centred * root
    norm_ref[...] = normed
    root_ref[...] = root
    hid_ref[...] = (normed * vec_ref[1:2] + vec_ref[2:3]).astype(bf16)


def project(index, context, tokens, vectors, pieces, step=256):
    count, width = tokens.shape
    meta = meta_of(pieces)
    rows = pl.BlockSpec((step, width), lambda i, s: (i, 0))
    return call(
        functools.partial(project_kernel, meta),
        (count // step,),
        [rows, rows, whole(vectors.shape)] + [ANY] * len(meta),
        [rows, pl.BlockSpec((step, 1), lambda i, s: (i, 0)), rows],
        [shaped((count, width), f32), shaped((count, 1), f32), shaped((count, width), bf16)],
        [pltpu.VMEM((width, width), bf16), pltpu.SemaphoreType.DMA((len(meta),))],
        count * width * width * 2,
        count * width * 10 + width * width * 2,
    )(index, context, tokens, vectors, *arrays_of(pieces))


def up_kernel(meta, index_ref, hid_ref, bias_ref, *rest):
    pieces, rest = rest[: len(meta)], rest[len(meta) :]
    act_ref, slope_ref, w_ref, sems = rest
    step = act_ref.shape[1]
    col = pl.program_id(1)

    @pl.when((pl.program_id(0) == 0) & (col == 0))
    def _():
        rows = w_ref.shape[0] // BLOCKS
        for copy in load(meta, rows, pieces, w_ref, sems, index_ref[0]):
            copy.wait()

    cols = pl.ds(pl.multiple_of(col * step, step), step)
    value = dot(hid_ref[...], w_ref[:, cols]) + bias_ref[...]
    share = 0.5 * (1.0 + lax.erf(value * math.sqrt(0.5)))
    density = jnp.exp(value * value * -0.5) * (1.0 / math.sqrt(2.0 * math.pi))
    act_ref[...] = (value * share).astype(bf16)
    slope_ref[...] = (share + value * density).astype(bf16)


def up(index, hidden, bias, pieces, step=256, tile=768):
    count, width = hidden.shape
    inner = bias.shape[1]
    meta = meta_of(pieces)
    out = pl.BlockSpec((step, tile), lambda i, j, s: (i, j))
    return call(
        functools.partial(up_kernel, meta),
        (count // step, inner // tile),
        [
            pl.BlockSpec((step, width), lambda i, j, s: (i, 0)),
            pl.BlockSpec((1, tile), lambda i, j, s: (0, j)),
        ]
        + [ANY] * len(meta),
        [out, out],
        [shaped((count, inner), bf16), shaped((count, inner), bf16)],
        [pltpu.VMEM((width, inner), bf16), pltpu.SemaphoreType.DMA((len(meta),))],
        count * width * inner * 2,
        count * (width * 2 + inner * 4) + width * inner * 2,
        count * inner * 4,
    )(index, hidden, bias, *arrays_of(pieces))


def down_kernel(meta, index_ref, act_ref, norm_ref, vec_ref, seg_ref, pos_ref, *rest):
    pieces, rest = rest[: len(meta)], rest[len(meta) :]
    res_ref, norm2_ref, root_ref, pay_ref, pool_ref, stat_ref, w_ref, sum_ref, num_ref, sems = rest
    step = pl.program_id(0)
    steps = pl.num_programs(0)
    width = res_ref.shape[1]

    @pl.when(step == 0)
    def _():
        sum_ref[...] = jnp.zeros_like(sum_ref)
        num_ref[...] = jnp.zeros_like(num_ref)
        rows = w_ref.shape[0] // BLOCKS
        for copy in load(meta, rows, pieces, w_ref, sems, index_ref[0]):
            copy.wait()

    hidden = norm_ref[...] * vec_ref[1:2] + vec_ref[2:3]
    summed = hidden + (dot(act_ref[...], w_ref[...]) + vec_ref[3:4])
    centred, root = row_stats(summed)
    normed = centred * root
    result = normed * vec_ref[4:5] + vec_ref[5:6]
    norm2_ref[...] = normed
    root_ref[...] = root
    high = result.astype(bf16)
    res_ref[...] = high
    low = (result - high.astype(f32)).astype(bf16)
    seg = seg_ref[0]
    wanted = lax.broadcasted_iota(jnp.int32, (SEGS, seg.shape[1]), 0)
    member = (wanted == seg).astype(f32)
    member_b = member.astype(bf16)
    own = pl.ds(pl.multiple_of(step // (steps * SEGS // sum_ref.shape[0]) * SEGS, SEGS), SEGS)
    sum_ref[own] += dot(member_b, high) + dot(member_b, low)
    num_ref[own] += jnp.broadcast_to(jnp.sum(member, axis=1, keepdims=True), (SEGS, TAIL))

    @pl.when(step == steps - 1)
    def _():
        counts = num_ref[:, 0:1]
        pooled = sum_ref[...] / counts
        scale = lax.rsqrt(jnp.mean(pooled * pooled, axis=-1, keepdims=True) + pool_eps)
        pool_ref[...] = pooled
        lane = lax.broadcasted_iota(jnp.int32, (pooled.shape[0], TAIL), 1)
        stat_ref[...] = jnp.where(lane == 0, scale, counts)
        pay_ref[:, :width] = (pooled * scale).astype(bf16)
        partner = pos_ref[...]
        digit = jnp.where(lane == 0, partner // BASE, partner % BASE)
        pay_ref[:, width:] = jnp.where(lane < 2, digit, 0).astype(f32).astype(bf16)


def down(index, activated, normed, vectors, seg_rows, positive, pieces, step=256):
    count, width = normed.shape
    inner = activated.shape[1]
    rows, _, length = seg_rows.shape
    own = rows * SEGS
    per_row = length // step
    meta = meta_of(pieces)
    block = pl.BlockSpec((step, width), lambda i, s: (i, 0))
    return call(
        functools.partial(down_kernel, meta),
        (count // step,),
        [
            pl.BlockSpec((step, inner), lambda i, s: (i, 0)),
            block,
            whole(vectors.shape),
            pl.BlockSpec((1, 1, step), lambda i, s: (i // per_row, 0, i % per_row)),
            whole((own, 1)),
        ]
        + [ANY] * len(meta),
        [
            block,
            block,
            pl.BlockSpec((step, 1), lambda i, s: (i, 0)),
            whole((own, width + TAIL)),
            whole((own, width)),
            whole((own, TAIL)),
        ],
        [
            shaped((count, width), bf16),
            shaped((count, width), f32),
            shaped((count, 1), f32),
            shaped((own, width + TAIL), bf16),
            shaped((own, width), f32),
            shaped((own, TAIL), f32),
        ],
        [
            pltpu.VMEM((inner, width), bf16),
            pltpu.VMEM((own, width), f32),
            pltpu.VMEM((own, TAIL), f32),
            pltpu.SemaphoreType.DMA((len(meta),)),
        ],
        count * width * inner * 2,
        count * (width * 10 + inner * 2) + width * inner * 2,
    )(index, activated, normed, vectors, seg_rows, positive, *arrays_of(pieces))


def contrast_kernel(place_ref, all_ref, own_ref, pos_ref, pool_ref, stat_ref, loss_ref, grad_ref):
    total = all_ref.shape[0]
    own, width = pool_ref.shape
    factor = score_scale / width
    block = min(total, 512)
    flip, first = place_ref[0], place_ref[1]
    mine = own_ref[:, :width]
    mine_id = lax.broadcasted_iota(jnp.int32, (own, total), 0) + first
    other_id = lax.broadcasted_iota(jnp.int32, (own, total), 1) ^ flip
    logits = dot_nt(mine, all_ref[:, :width]) * factor
    logits = jnp.where(mine_id == other_id, masked_value, logits)
    top = jnp.max(logits, axis=1, keepdims=True)
    log_own = top + jnp.log(jnp.sum(jnp.exp(logits - top), axis=1, keepdims=True))
    is_positive = other_id == pos_ref[...]
    picked = jnp.sum(jnp.where(is_positive, logits, 0.0), axis=1, keepdims=True)
    loss_ref[...] = log_own - picked
    d_logits = pair_weight * (jnp.exp(logits - log_own) - is_positive.astype(f32))
    d_emb = dot(d_logits.astype(bf16), all_ref[:, :width])
    lane = lax.broadcasted_iota(jnp.int32, (SEGS, TAIL), 1)
    digits = jnp.where(lane == 0, float(BASE), jnp.where(lane == 1, 1.0, 0.0)).astype(bf16)
    for at in range(0, total, block):
        rows = slice(at, at + block)
        table = dot_nt(all_ref[:, :width], all_ref[rows, :width]) * factor
        left = lax.broadcasted_iota(jnp.int32, (total, block), 0)
        right = lax.broadcasted_iota(jnp.int32, (total, block), 1) + at
        table = jnp.where(left == right, masked_value, table)
        top = jnp.max(table, axis=0, keepdims=True)
        log_all = top + jnp.log(jnp.sum(jnp.exp(table - top), axis=0, keepdims=True))
        partner = dot_nt(digits, all_ref[rows, width:])[0:1].astype(jnp.int32)
        chosen = partner == mine_id[:, rows]
        back = pair_weight * (jnp.exp(logits[:, rows] - log_all) - chosen.astype(f32))
        d_emb += dot(back.astype(bf16), all_ref[rows, :width])
    d_emb = d_emb * factor
    scale, counts = stat_ref[:, 0:1], stat_ref[:, 1:2]
    pooled = pool_ref[...]
    along = jnp.mean(d_emb * pooled, axis=-1, keepdims=True)
    grad_ref[...] = (d_emb * scale - pooled * (scale * scale * scale * along)) / counts


def contrast(place, everyone, payload, positive, pooled, stats):
    own, width = pooled.shape
    total = everyone.shape[0]
    return call(
        contrast_kernel,
        (1,),
        [whole(v.shape) for v in (everyone, payload, positive, pooled, stats)],
        [whole((own, 1)), whole((own, width))],
        [shaped((own, 1), f32), shaped((own, width), f32)],
        [],
        total * total * width * 2,
        total * width * 2,
        total * total,
    )(place, everyone, payload, positive, pooled, stats)


def norm_back(d_out, normed, root, gain):
    scaled = d_out * gain
    mean = jnp.mean(scaled, axis=-1, keepdims=True)
    along = jnp.mean(scaled * normed, axis=-1, keepdims=True)
    return root * (scaled - mean - normed * along)


def column_sum(values):
    return jnp.sum(values, axis=0, keepdims=True)


def rank_of(step):
    return jnp.where(step < 4, 2 * step + 1, 2 * (step - 4))


def norm2_kernel(index_ref, og_ref, norm_ref, root_ref, seg_ref, gain_ref, dp_ref, act_ref, *rest):
    dsum_ref, ddown_ref, vec_ref, keep_ref, send_ref, dt_ref = rest
    step = pl.program_id(0)
    count, width = og_ref.shape
    own = dp_ref.shape[0]
    per_row = count * SEGS // own

    @pl.when(step == 0)
    def _():
        vec_ref[...] = jnp.zeros_like(vec_ref)
        chunk = 256
        pad = jnp.zeros((TILE - 3 * SEGS, width), bf16)
        for at in range(0, count, chunk):
            row = at // per_row
            pool = dp_ref[row * SEGS : (row + 1) * SEGS]
            high = pool.astype(bf16)
            left = pool - high.astype(f32)
            mid = left.astype(bf16)
            low = (left - mid.astype(f32)).astype(bf16)
            table = jnp.concatenate([high, mid, low, pad], axis=0)
            lane = lax.broadcasted_iota(jnp.int32, (chunk, TILE), 1)
            here = slice(at, at + chunk)
            member = (lane % SEGS == seg_ref[here]).astype(f32).astype(bf16)
            d_res = og_ref[here].astype(f32) + dot(member, table)
            normed = norm_ref[here]
            d_sum = norm_back(d_res, normed, root_ref[here], gain_ref[...])
            d_down = d_sum.astype(bf16)
            dsum_ref[here] = d_sum
            ddown_ref[here] = d_down
            dt_ref[:, here] = d_down.T
            vec_ref[0:1] += column_sum(d_res * normed)
            vec_ref[1:2] += column_sum(d_res)
            vec_ref[2:3] += column_sum(d_down.astype(f32))

    grad = dot(dt_ref[...], act_ref[...]).astype(bf16)

    @pl.when(step < 4)
    def _():
        send_ref[0] = grad

    @pl.when(step >= 4)
    def _():
        keep_ref[0] = grad


def norm2(index, out_grad, normed, root, seg_col, gain, d_pool, activated):
    count, width = out_grad.shape
    inner = activated.shape[1]
    tile = inner // BLOCKS
    own = d_pool.shape[0]
    return call(
        norm2_kernel,
        (BLOCKS,),
        [
            whole((count, width)),
            whole((count, width)),
            whole((count, 1)),
            whole((count, 1)),
            whole((1, width)),
            whole((own, width)),
            pl.BlockSpec((count, tile), lambda i, s: (0, s[0] ^ rank_of(i))),
        ],
        [
            whole((count, width)),
            whole((count, width)),
            whole((SEGS, width)),
            pl.BlockSpec((1, width, tile), lambda i, s: (jnp.maximum(i - 4, 0), 0, 0)),
            pl.BlockSpec((1, width, tile), lambda i, s: (jnp.minimum(i, 3), 0, 0)),
        ],
        [
            shaped((count, width), f32),
            shaped((count, width), bf16),
            shaped((SEGS, width), f32),
            shaped((4, width, tile), bf16),
            shaped((4, width, tile), bf16),
        ],
        [pltpu.VMEM((width, count), bf16)],
        count * width * inner * 2,
        count * (width * 12 + inner * 2) + width * inner * 2,
    )(index, out_grad, normed, root, seg_col, gain, d_pool, activated)


def put_turned(source_ref, target_ref, turn_ref, index):
    turn_ref[...] = source_ref[...].T
    rows = turn_ref.shape[0] // BLOCKS
    for place in range(BLOCKS):
        block = index ^ ((place % 4) * 2 + place // 4)
        start = pl.multiple_of(block * rows, 16)
        target_ref[place * rows : (place + 1) * rows] = turn_ref[pl.ds(start, rows)]


def up_back_kernel(
    down_meta, up_meta, index_ref, ddown_ref, slope_ref, hid_ref, *rest
):
    low_pieces, rest = rest[: len(down_meta)], rest[len(down_meta) :]
    up_pieces, rest = rest[: len(up_meta)], rest[len(up_meta) :]
    dhid_ref, bias_ref, keep_ref, send_ref, wd_ref, wu_ref, turn_ref, ht_ref, sems, up_sems = rest
    step = pl.program_id(0)
    tile = slope_ref.shape[1]
    width = ht_ref.shape[0]

    @pl.when(step == 0)
    def _():
        index = index_ref[0]
        first = load(down_meta, tile, low_pieces, wd_ref, sems, 0)
        second = load(up_meta, width // BLOCKS, up_pieces, wu_ref, up_sems, index)
        put_turned(hid_ref, ht_ref, turn_ref, index)
        for copy in first + second:
            copy.wait()
        dhid_ref[...] = jnp.zeros_like(dhid_ref)

    rows = pl.ds(pl.multiple_of(step * tile, tile), tile)
    cols = pl.ds(pl.multiple_of((index_ref[0] ^ step) * tile, tile), tile)
    d_act = dot_nt(ddown_ref[...], wd_ref[rows])
    d_up = (d_act * slope_ref[...].astype(f32)).astype(bf16)
    bias_ref[...] = column_sum(d_up.astype(f32))
    grad = dot(ht_ref[...], d_up).astype(bf16)
    half = width // 2
    keep_ref[...] = grad[:half].reshape(keep_ref.shape)
    send_ref[...] = grad[half:].reshape(send_ref.shape)
    dhid_ref[...] += dot_nt(d_up, wu_ref[:, cols])


def up_back(index, d_down, slope, hidden, down_pieces, up_pieces):
    count, width = d_down.shape
    inner = slope.shape[1]
    tile = inner // BLOCKS
    part = width // BLOCKS
    down_meta, up_meta = meta_of(down_pieces), meta_of(up_pieces)
    grads = pl.BlockSpec((4, part, tile), lambda i, s: (0, 0, s[0] ^ i))
    return call(
        functools.partial(up_back_kernel, down_meta, up_meta),
        (BLOCKS,),
        [
            whole((count, width)),
            pl.BlockSpec((count, tile), lambda i, s: (0, s[0] ^ i)),
            whole((count, width)),
        ]
        + [ANY] * (len(down_meta) + len(up_meta)),
        [
            whole((count, width)),
            pl.BlockSpec((1, tile), lambda i, s: (0, s[0] ^ i)),
            grads,
            grads,
        ],
        [
            shaped((count, width), f32),
            shaped((1, inner), f32),
            shaped((4, part, inner), bf16),
            shaped((4, part, inner), bf16),
        ],
        [
            pltpu.VMEM((inner, width), bf16),
            pltpu.VMEM((width, inner), bf16),
            pltpu.VMEM((width, count), bf16),
            pltpu.VMEM((width, count), bf16),
            pltpu.SemaphoreType.DMA((len(down_meta),)),
            pltpu.SemaphoreType.DMA((len(up_meta),)),
        ],
        count * width * inner * 6,
        count * (width * 8 + inner * 2) + width * inner * 6,
    )(index, d_down, slope, hidden, *arrays_of(down_pieces), *arrays_of(up_pieces))


def norm1_kernel(meta, index_ref, dhid_ref, dsum_ref, norm_ref, root_ref, gain_ref, ctx_ref, *rest):
    pieces, rest = rest[: len(meta)], rest[len(meta) :]
    dattn_ref, dctx_ref, vec_ref, keep_ref, send_ref, w_ref, acc_ref, sems = rest
    step = pl.program_id(0)
    rows = w_ref.shape[0] // BLOCKS

    @pl.when(step == 0)
    def _():
        copies = load(meta, rows, pieces, w_ref, sems, index_ref[0])
        vec_ref[...] = jnp.zeros_like(vec_ref)
        acc_ref[...] = jnp.zeros_like(acc_ref)
        for copy in copies:
            copy.wait()

    d_hid = dsum_ref[...] + dhid_ref[...]
    normed = norm_ref[...]
    d_sum = norm_back(d_hid, normed, root_ref[...], gain_ref[...])
    d_attn = d_sum.astype(bf16)
    dattn_ref[...] = d_sum
    vec_ref[0:1] += column_sum(d_hid * normed)
    vec_ref[1:2] += column_sum(d_hid)
    vec_ref[2:3] += column_sum(d_attn.astype(f32))
    dctx_ref[...] = dot_nt(d_attn, w_ref[...]).astype(bf16)
    acc_ref[...] += dot(ctx_ref[...].T, d_attn)

    @pl.when(step == pl.num_programs(0) - 1)
    def _():
        for place in range(4):
            for target, core in ((keep_ref, 0), (send_ref, 1)):
                start = pl.multiple_of((index_ref[0] ^ (2 * place + core)) * rows, 16)
                target[place] = acc_ref[pl.ds(start, rows)].astype(bf16)


def norm1(index, d_hidden, d_summed, normed, root, gain, context, pieces, step=256):
    count, width = d_hidden.shape
    meta = meta_of(pieces)
    part = width // BLOCKS
    block = pl.BlockSpec((step, width), lambda i, s: (i, 0))
    return call(
        functools.partial(norm1_kernel, meta),
        (count // step,),
        [
            block,
            block,
            block,
            pl.BlockSpec((step, 1), lambda i, s: (i, 0)),
            whole((1, width)),
            block,
        ]
        + [ANY] * len(meta),
        [
            block,
            block,
            whole((SEGS, width)),
            whole((4, part, width)),
            whole((4, part, width)),
        ],
        [
            shaped((count, width), f32),
            shaped((count, width), bf16),
            shaped((SEGS, width), f32),
            shaped((4, part, width), bf16),
            shaped((4, part, width), bf16),
        ],
        [
            pltpu.VMEM((width, width), bf16),
            pltpu.VMEM((width, width), f32),
            pltpu.SemaphoreType.DMA((len(meta),)),
        ],
        count * width * width * 4,
        count * width * 20 + width * width * 4,
    )(index, d_hidden, d_summed, normed, root, gain, context, *arrays_of(pieces))


def attend_back_kernel(index_ref, q_ref, k_ref, v_ref, dctx_ref, lse_ref, seg_ref, tok_ref, *rest):
    dq_ref, dk_ref, dv_ref, bias_ref, keep_ref, send_ref = rest[:6]
    mask_ref, turn_ref, tt_ref, dk_acc, dv_acc, both_ref = rest[6:]
    rows, _, length = seg_ref.shape
    lanes = q_ref.shape[1]
    half = lanes // 2
    inv_root = 1.0 / math.sqrt(half)

    @pl.when(pl.program_id(0) == 0)
    def _():
        put_turned(tok_ref, tt_ref, turn_ref, index_ref[0])
        for row in range(rows):
            fill_mask(seg_ref[row].astype(f32), mask_ref.at[row])

    for row in range(rows):
        base = row * length
        here = slice(base, base + length)
        kt = k_ref[here].T
        dk_acc[...] = jnp.zeros_like(dk_acc)
        dv_acc[...] = jnp.zeros_like(dv_acc)
        for lo, hi, at in bands(length):
            tile = slice(base + at, base + at + TILE)
            keys = k_ref[base + lo : base + hi]
            values = v_ref[base + lo : base + hi]
            queries = two_heads(q_ref[tile])
            d_context = two_heads(dctx_ref[tile])
            lse = jnp.concatenate(
                [lse_ref[row, 0, head : head + 1, at : at + TILE] for head in range(2)], axis=1
            )
            scores = dot_nt(keys, queries) + twice(mask_ref[row, lo:hi, at : at + TILE])
            probs = jnp.exp(scores - lse)
            d_probs = dot_nt(values, d_context)
            inner = jnp.sum(d_probs * probs, axis=0, keepdims=True)
            d_scores = (probs * (d_probs - inner)).astype(bf16)
            dv_acc[lo:hi] += dot(probs.astype(bf16), d_context)
            dk_acc[lo:hi] += dot(d_scores, queries)
            dq = dot(kt[:, lo:hi], d_scores) * inv_root
            dq = jnp.concatenate([dq[:half, :TILE], dq[half:, TILE:]], axis=0)
            both_ref[tile, :lanes] = dq.T.astype(bf16)
        both_ref[here, lanes : 2 * lanes] = dk_acc[...].astype(bf16)
        both_ref[here, 2 * lanes :] = dv_acc[...].astype(bf16)
    both = both_ref[...]
    dq_ref[...] = both[:, :lanes]
    dk_ref[...] = both[:, lanes : 2 * lanes]
    dv_ref[...] = both[:, 2 * lanes :]
    bias_ref[0, 0:1] = column_sum(both.astype(f32))
    grad = dot(tt_ref[...], both).astype(bf16)
    middle = grad.shape[0] // 2
    keep_ref[...] = grad[:middle].reshape(keep_ref.shape)
    send_ref[...] = grad[middle:].reshape(send_ref.shape)


def attend_back(index, qkv, d_context, lse, seg_rows, tokens, first, pairs):
    count, width = tokens.shape
    rows, _, length = seg_rows.shape
    every = HEADS // 2
    lanes = width // every
    part = width // BLOCKS
    column = lambda place: pl.BlockSpec((count, lanes), lambda i, s: (0, place + i))
    out = pl.BlockSpec((count, lanes), lambda i, s: (0, i))
    grads = pl.BlockSpec((4, part, 3 * lanes), lambda i, s: (0, 0, i))
    return call(
        attend_back_kernel,
        (pairs,),
        [
            column(first),
            column(every + first),
            column(2 * every + first),
            column(first),
            pl.BlockSpec((rows, 1, 2, length), lambda i, s: (0, first + i, 0, 0)),
            whole((rows, 1, length)),
            whole((count, width)),
        ],
        [
            out,
            out,
            out,
            pl.BlockSpec((1, SEGS, 3 * lanes), lambda i, s: (i, 0, 0)),
            grads,
            grads,
        ],
        [
            shaped((count, pairs * lanes), bf16),
            shaped((count, pairs * lanes), bf16),
            shaped((count, pairs * lanes), bf16),
            shaped((pairs, SEGS, 3 * lanes), f32),
            shaped((4, part, pairs * 3 * lanes), bf16),
            shaped((4, part, pairs * 3 * lanes), bf16),
        ],
        [
            pltpu.VMEM((rows, length, length), f32),
            pltpu.VMEM((width, count), bf16),
            pltpu.VMEM((width, count), bf16),
            pltpu.VMEM((length, lanes), f32),
            pltpu.VMEM((length, lanes), f32),
            pltpu.VMEM((count, 3 * lanes), bf16),
        ],
        count * pairs * lanes * (width * 6 + length * 6),
        count * pairs * lanes * 14 + count * width * 2,
        count * length * pairs * 5 // 4,
    )(index, qkv, qkv, qkv, d_context, lse, seg_rows, tokens)


def input_kernel(meta, parts, index_ref, dattn_ref, *rest):
    grads, rest = rest[: 3 * parts], rest[3 * parts :]
    pieces, rest = rest[: len(meta)], rest[len(meta) :]
    out_ref, w_ref, sems = rest
    width = out_ref.shape[1]
    step = width // parts

    @pl.when(pl.program_id(0) == 0)
    def _():
        rows = w_ref.shape[0] // BLOCKS
        for copy in load(meta, rows, pieces, w_ref, sems, index_ref[0]):
            copy.wait()

    total = dattn_ref[...]
    for kind in range(3):
        for part in range(parts):
            at = kind * width + part * step
            total += dot_nt(grads[kind * parts + part][...], w_ref[:, at : at + step])
    out_ref[...] = total


def input_grad(index, d_attn, grads, pieces, step=256):
    count, width = d_attn.shape
    meta = meta_of(pieces)
    parts = len(grads) // 3
    block = pl.BlockSpec((step, width), lambda i, s: (i, 0))
    return call(
        functools.partial(input_kernel, meta, parts),
        (count // step,),
        [block]
        + [pl.BlockSpec((step, g.shape[1]), lambda i, s: (i, 0)) for g in grads]
        + [ANY] * len(meta),
        block,
        shaped((count, width), f32),
        [pltpu.VMEM((width, 3 * width), bf16), pltpu.SemaphoreType.DMA((len(meta),))],
        count * width * width * 6,
        count * width * 14 + width * width * 6,
    )(index, d_attn, *grads, *arrays_of(pieces))


def rounded(value):
    return lax.optimization_barrier(value.astype(bf16))


def add(*values):
    total = values[0].astype(f32)
    for value in values[1:]:
        total = total + value.astype(f32)
    return total


def reduce_blocks(blocks):
    mine, over_x, over_y, far = blocks
    half = far.shape[0] // 2
    top = fsdp_swap(far[:half], 2)
    low = fsdp_swap(far[half:], 4)
    over_x = jnp.concatenate([over_x[:half], add(over_x[half:], low).astype(bf16)], axis=0)
    over_y = jnp.concatenate([add(over_y[:half], top).astype(bf16), over_y[half:]], axis=0)
    from_x = fsdp_swap(over_x, 2)
    from_y = fsdp_swap(over_y, 4)
    return rounded(add(mine, from_x, from_y))


def reduce_planes(value, planes):
    value = rounded(add(value, swap(value, "batch", planes, 1)))
    return add(value, swap(value, "batch", planes, 2))


def reduce_shard(keep, send, planes):
    other = fsdp_swap(send, 1)
    blocks = [rounded(add(keep[i], other[i])) for i in range(4)]
    return reduce_planes(reduce_blocks(blocks), planes)


def reduce_general(keep, send):
    full = jnp.stack([keep, send], axis=1)
    total = lax.psum(full, "batch")
    total = total.reshape((BLOCKS,) + keep.shape[1:])
    return total


def layer(
    planes,
    ring,
    tokens,
    seg_ids,
    positive,
    out_grad,
    w_qkv,
    b_qv,
    w_out,
    b_out,
    norm1_gain,
    norm1_shift,
    w_up,
    b_up,
    w_down,
    b_down,
    norm2_gain,
    norm2_shift,
):
    paired = ring == BLOCKS and planes == 4
    row_count, row_length, width = tokens.shape
    count = row_count * row_length
    inner = b_up.shape[0] * ring
    own = row_count * SEGS
    token_rows = tokens.reshape(count, width)
    seg_rows = seg_ids.reshape(row_count, 1, row_length)
    seg_col = seg_ids.reshape(count, 1)
    pos_col = positive.reshape(own, 1)
    fsdp = lax.axis_index("fsdp")
    me = lax.axis_index("batch") * ring + fsdp
    index = (fsdp if paired else jnp.zeros_like(fsdp)).reshape(1).astype(jnp.int32)

    weights = (w_qkv, w_out, w_up, w_down)
    if paired:
        firsts = [gather_first(w) for w in weights]
        qkv_pieces, out_pieces, up_pieces, down_pieces = [
            gather_second(w, *first) for w, first in zip(weights, firsts)
        ]
    else:
        qkv_pieces, out_pieces, up_pieces, down_pieces = [gather_whole(w) for w in weights]

    small = (b_qv, b_out, norm1_gain, norm1_shift, b_up, b_down, norm2_gain, norm2_shift)
    sizes = [value.shape[0] for value in small]
    table = lax.all_gather(jnp.concatenate(small)[None], "fsdp", axis=0, tiled=True).astype(f32)
    vectors, at = [], 0
    for size in sizes:
        vectors.append(table[:, at : at + size].reshape(1, ring * size))
        at += size
    bias_qv, bias_out, gain1, shift1, bias_up, bias_down, gain2, shift2 = vectors
    bias_qkv = jnp.concatenate(
        [bias_qv[:, :width], jnp.zeros((1, width), f32), bias_qv[:, width:]], axis=1
    )
    rows = jnp.concatenate(
        [bias_out, gain1, shift1, bias_down, gain2, shift2, jnp.zeros((2, width), f32)], axis=0
    )

    qkv, context, lse = attend(index, token_rows, bias_qkv, seg_rows, qkv_pieces)
    normed1, root1, hidden = project(index, context, token_rows, rows, out_pieces)
    activated, slope = up(index, hidden, bias_up, up_pieces)
    result, normed2, root2, payload, pooled, stats = down(
        index, activated, normed1, rows, seg_rows, pos_col, down_pieces
    )

    if paired:
        everyone = payload
        for bit in (1, 2, 4):
            everyone = jnp.concatenate([everyone, fsdp_swap(everyone, bit)], axis=0)
        for bit in (1, 2):
            everyone = jnp.concatenate([everyone, swap(everyone, "batch", planes, bit)], axis=0)
        flip = me * own
    else:
        everyone = lax.all_gather(payload, ("batch", "fsdp"), axis=0, tiled=True)
        flip = jnp.zeros_like(me)
    place = jnp.stack([flip, me * own]).astype(jnp.int32)
    pair_loss, d_pool = contrast(place, everyone, payload, pos_col, pooled, stats)

    d_summed, d_down, sums2, keep_down, send_down = norm2(
        index, out_grad.reshape(count, width), normed2, root2, seg_col, gain2, d_pool, activated
    )
    d_hidden, sums_up, keep_up, send_up = up_back(
        index, d_down, slope, hidden, down_pieces, up_pieces
    )
    d_attn, d_context, sums1, keep_out, send_out = norm1(
        index, d_hidden, d_summed, normed1, root1, gain1, context, out_pieces
    )
    pairs = HEADS // 2
    cuts = 2
    backs = [
        attend_back(
            index, qkv, d_context, lse, seg_rows, token_rows, i * pairs // cuts, pairs // cuts
        )
        for i in range(cuts)
    ]
    grads = [backs[cut][kind] for kind in range(3) for cut in range(cuts)]
    grad_tokens = input_grad(index, d_attn, grads, qkv_pieces)

    lanes = width // pairs
    sums_qkv = jnp.concatenate([back[3][:, 0] for back in backs], axis=0).reshape(pairs, 3, lanes)
    sums_qv = jnp.concatenate([sums_qkv[:, 0].reshape(-1), sums_qkv[:, 2].reshape(-1)])
    sums = (sums_qv, sums1[2], sums1[0], sums1[1], sums_up[0], sums2[2], sums2[0], sums2[1])

    if paired:
        vector = jnp.concatenate([v.reshape(ring, -1) for v in sums], axis=1)
        order = [2 * (i % 4) + i // 4 for i in range(BLOCKS)]
        vector = vector[jnp.array(order, jnp.int32) ^ fsdp].astype(bf16)
        vector = jnp.pad(vector[:, None], ((0, 0), (0, 15), (0, 0)))
        grad_down = reduce_shard(keep_down, send_down, planes).T
        grad_up = reduce_shard(keep_up, send_up, planes)
        grad_out = reduce_shard(keep_out, send_out, planes)
        shards = []
        for cut, back in enumerate(backs):
            keep, send = back[4], back[5]
            if cut == cuts - 1:
                keep = jnp.concatenate([keep, vector[:4]], axis=1)
                send = jnp.concatenate([send, vector[4:]], axis=1)
            shards.append(reduce_shard(keep, send, planes))
        part = width // BLOCKS
        line = shards[-1][part]
        shards = [shard[:part] for shard in shards]
        own_vectors, at = [], 0
        for size in sizes:
            own_vectors.append(line[at : at + size])
            at += size
    else:
        scatter = lambda value: lax.psum_scatter(value, "fsdp", scatter_dimension=0, tiled=True)
        joined = lambda value: value.reshape((-1,) + value.shape[2:])
        grad_down = scatter(joined(reduce_general(keep_down, send_down).transpose(0, 2, 1)))
        grad_up = scatter(joined(reduce_general(keep_up, send_up)))
        grad_out = scatter(joined(reduce_general(keep_out, send_out)))
        grad_down, grad_up, grad_out = [add(g) for g in (grad_down, grad_up, grad_out)]
        shards = [add(scatter(joined(reduce_general(back[4], back[5])))) for back in backs]
        own_vectors = [
            lax.psum_scatter(lax.psum(v, "batch"), "fsdp", scatter_dimension=0, tiled=True)
            for v in sums
        ]

    grad_qkv = jnp.concatenate(shards, axis=1)
    depth = grad_qkv.shape[0]
    grad_qkv = grad_qkv.reshape(depth, pairs, 3, lanes).transpose(0, 2, 1, 3)
    grad_qkv = grad_qkv.reshape(depth, 3 * width)
    return (
        result.reshape(tokens.shape),
        pair_loss.reshape(own),
        grad_tokens.reshape(tokens.shape),
        grad_qkv,
        own_vectors[0],
        grad_out,
        own_vectors[1],
        own_vectors[2],
        own_vectors[3],
        grad_up,
        own_vectors[4],
        grad_down,
        own_vectors[5],
        own_vectors[6],
        own_vectors[7],
    )


def solution(mesh):
    rows = P(("batch", "fsdp"), None, None)
    matrix = P("fsdp", None)
    vector = P("fsdp")
    placed = (
        rows,
        P(("batch", "fsdp"), None),
        P(("batch", "fsdp")),
        rows,
        matrix,
        vector,
        matrix,
        vector,
        vector,
        vector,
        matrix,
        vector,
        matrix,
        vector,
        vector,
        vector,
    )
    given = (
        rows,
        P(("batch", "fsdp")),
        rows,
        matrix,
        vector,
        matrix,
        vector,
        vector,
        vector,
        matrix,
        vector,
        matrix,
        vector,
        vector,
        vector,
    )
    return jax.shard_map(
        functools.partial(layer, mesh.shape["batch"], mesh.shape["fsdp"]),
        mesh=mesh,
        in_specs=placed,
        out_specs=given,
        check_vma=False,
    )
```

```python
import functools
import math

import jax
import jax.numpy as jnp
from jax import lax
from jax.experimental import pallas as pl
from jax.experimental.pallas import tpu as pltpu
from jax.sharding import PartitionSpec as P

HEADS = 12
SEGS = 8

norm_eps = 1e-06
pool_eps = 1e-06
score_scale = 50.0
pair_weight = 256.0
masked_value = -1000000000.0

BLOCKS = 8
TILE = 128
TAIL = 128
BASE = 64

bf16 = jnp.bfloat16
f32 = jnp.float32
ANY = pl.BlockSpec(memory_space=pl.ANY)
VMEM_BYTES = 32 * 1024 * 1024


def dot(left, right):
    return jnp.dot(left, right, preferred_element_type=f32)


def dot_nt(left, right):
    return lax.dot_general(left, right, (((1,), (1,)), ((), ())), preferred_element_type=f32)


def whole(shape):
    return pl.BlockSpec(shape, lambda *_: (0,) * len(shape))


def call(
    kernel,
    grid,
    in_specs,
    out_specs,
    out_shape,
    scratch,
    flops,
    moved,
    special=0,
    after=(),
    alias=None,
    near=(),
    room=VMEM_BYTES,
):
    given, extra = len(in_specs) + 1, len(after)

    def body(*refs):
        kernel(*refs[:given], *refs[given + extra :])

    single = not isinstance(out_shape, list)
    shapes = [out_shape] if single else out_shape
    shapes = [
        shape if -1 - number in near else pltpu.HBM(shape.shape, shape.dtype)
        for number, shape in enumerate(shapes)
    ]
    run = pl.pallas_call(
        body,
        out_shape=shapes[0] if single else shapes,
        grid_spec=pltpu.PrefetchScalarGridSpec(
            num_scalar_prefetch=1,
            grid=grid,
            in_specs=in_specs + [ANY] * extra,
            out_specs=out_specs,
            scratch_shapes=scratch,
        ),
        input_output_aliases=alias or {},
        compiler_params=pltpu.CompilerParams(vmem_limit_bytes=room),
        cost_estimate=pl.CostEstimate(
            flops=int(flops), bytes_accessed=int(moved), transcendentals=int(special)
        ),
    )

    def apply(index, *operands):
        placed = [
            value if 1 + number in near else pltpu.with_memory_space_constraint(value, pltpu.HBM)
            for number, value in enumerate(operands)
        ]
        return run(index, *placed, *after)

    return apply


def shaped(shape, dtype):
    return jax.ShapeDtypeStruct(shape, dtype)


def swap(value, axis, size, bit):
    return lax.ppermute(value, axis, [(i, i ^ bit) for i in range(size)])


def fsdp_swap(value, bit):
    return swap(value, "fsdp", BLOCKS, bit)


def middle(shard):
    return shard.shape[0] // 32 * 16


def first_stage(shard):
    return fsdp_swap(shard, 2), fsdp_swap(shard, 4)


def second_stage(shard, over_x, over_y):
    half = middle(shard)
    return fsdp_swap(over_y[:half], 2), fsdp_swap(over_x[half:], 4)


def all_pieces(shard, over_x, over_y, far_top, far_low):
    half = middle(shard)
    mine = [
        (shard, 0, 0),
        (over_x, 2, 0),
        (over_y, 4, 0),
        (far_top, 6, 0),
        (far_low, 6, half),
    ]
    return mine + [(fsdp_swap(value, 1), place ^ 1, off) for value, place, off in mine]


def gather_whole(shard):
    full = lax.all_gather(shard, "fsdp", axis=0, tiled=True)
    rows = full.shape[0] // BLOCKS
    return [full[i * rows : (i + 1) * rows] for i in range(BLOCKS)]


def meta_of(pieces):
    return tuple((place, off, value.shape[0]) for value, place, off in pieces)


def arrays_of(pieces):
    return [value for value, _, _ in pieces]


def copies_of(meta, rows, refs, target, sems, index, source=None, place=None):
    copies = []
    for number, ((block, off, count), ref) in enumerate(zip(meta, refs)):
        start = pl.multiple_of((index ^ block) * rows + off, 16)
        here = pl.ds(start, count)
        copies.append(
            pltpu.make_async_copy(
                ref if source is None else ref.at[:, source],
                target.at[here] if place is None else target.at[here, place],
                sems.at[number],
            )
        )
    return copies


def start_all(copies):
    for copy in copies:
        copy.start()


def wait_all(copies):
    for copy in copies:
        copy.wait()


def columns(number, size, base=0):
    return pl.ds(pl.multiple_of(base + number * size, TILE), size)


def fill_mask(seg_row, mask_ref):
    length = seg_row.shape[1]
    keys = jnp.broadcast_to(seg_row, (TILE, length)).T
    for lo, hi, at in bands(length):
        same = keys[lo:hi] == seg_row[:, at : at + TILE]
        mask_ref[lo:hi, at : at + TILE] = jnp.where(same, 0.0, masked_value)


def bands(length):
    out = []
    for at in range(0, length, TILE):
        out.append((max(at - TILE, 0), min(at + 2 * TILE, length), at))
    return out


def two_heads(pair):
    lane = lax.broadcasted_iota(jnp.int32, (1, pair.shape[1]), 1)
    first = (lane < pair.shape[1] // 2).astype(f32).astype(bf16)
    return jnp.concatenate([pair * first, pair * (1.0 - first)], axis=0)


def twice(value):
    return jnp.concatenate([value, value], axis=1)


def pack_small(small):
    line = jnp.concatenate([jnp.pad(v, (0, -v.shape[0] % TILE)) for v in small])
    return jnp.pad(line[None], ((0, 15), (0, 0)))


def spread(table, at, size):
    count = table.shape[0]
    padded = size + -size % TILE
    block = table[:, at : at + padded].astype(bf16)
    col = lax.broadcasted_iota(jnp.int32, (1, count * size), 1)
    owner = col // size
    place = lax.broadcasted_iota(jnp.int32, (padded, count * size), 0) == col - owner * size
    value = dot(block, place.astype(f32).astype(bf16))
    keep = lax.broadcasted_iota(jnp.int32, value.shape, 0) == owner
    return jnp.sum(jnp.where(keep, value, 0.0), axis=0, keepdims=True), at + padded


def qkv_kernel(meta, small_meta, size, index_ref, tok_ref, *rest):
    pieces, rest = rest[: len(meta)], rest[len(meta) :]
    lines, rest = rest[: len(small_meta)], rest[len(small_meta) :]
    qkv_ref, table_ref, w_ref, small_ref, bias_ref, sems, small_sems = rest
    width = tok_ref.shape[1]
    part = pl.program_id(0)

    def weights(number):
        cols = columns(number, width)
        rows = width // BLOCKS
        return copies_of(meta, rows, pieces, w_ref, sems.at[number], index_ref[0], cols, cols)

    @pl.when(part == 0)
    def _():
        small = copies_of(small_meta, 16, lines, small_ref, small_sems, index_ref[0])
        start_all(small)
        for number in range(3):
            start_all(weights(number))
        wait_all(small)
        line = lax.broadcasted_iota(jnp.int32, (BLOCKS, 16 * BLOCKS), 0) * 16
        pick = line == lax.broadcasted_iota(jnp.int32, (BLOCKS, 16 * BLOCKS), 1)
        table_ref[...] = dot(pick.astype(f32).astype(bf16), small_ref[...])
        bias, _ = spread(table_ref[...], 0, size)
        bias_ref[0] = bias[:, :width]
        bias_ref[1] = jnp.zeros((1, width), f32)
        bias_ref[2] = bias[:, width:]

    wait_all(weights(part))
    scale = jnp.where(part == 0, 1.0 / math.sqrt(width // HEADS), 1.0)
    value = dot(tok_ref[...], w_ref[:, columns(part, width)]) + bias_ref[part]
    qkv_ref[...] = (value * scale).astype(bf16)


def project_qkv(index, tokens, pieces, lines, size):
    count, width = tokens.shape
    meta, small_meta = meta_of(pieces), meta_of(lines)
    used = lines[0][0].shape[1]
    return call(
        functools.partial(qkv_kernel, meta, small_meta, size),
        (3,),
        [whole((count, width))] + [ANY] * len(meta + small_meta),
        [pl.BlockSpec((count, width), lambda i, s: (0, i)), whole((BLOCKS, used))],
        [shaped((count, 3 * width), bf16), shaped((BLOCKS, used), f32)],
        [
            pltpu.VMEM((width, 3 * width), bf16),
            pltpu.VMEM((16 * BLOCKS, used), bf16),
            pltpu.VMEM((3, 1, width), f32),
            pltpu.SemaphoreType.DMA((3, len(meta))),
            pltpu.SemaphoreType.DMA((len(small_meta),)),
        ],
        count * width * width * 6,
        count * width * 8 + width * width * 6,
    )(index, tokens, *arrays_of(pieces), *arrays_of(lines))


def attend_kernel(index_ref, qkv_ref, seg_ref, *rest):
    ctx_ref, lse_ref, vt_ref, ct_ref, mask_ref = rest[-5:]
    length, width = ctx_ref.shape
    pairs = HEADS // 2
    lanes = width // pairs
    half = lanes // 2
    fill_mask(seg_ref[0].astype(f32), mask_ref)
    vt_ref[...] = qkv_ref[:, 2 * width :].T

    tiles = [(pair, band) for pair in range(pairs) for band in bands(length)]

    def scores_of(tile):
        pair, (lo, hi, at) = tile
        queries = two_heads(qkv_ref[at : at + TILE, pair * lanes : (pair + 1) * lanes])
        keys = qkv_ref[lo:hi, width + pair * lanes : width + (pair + 1) * lanes]
        return dot_nt(keys, queries)

    def probs_of(tile, scores):
        pair, (lo, hi, at) = tile
        scores = scores + twice(mask_ref[lo:hi, at : at + TILE])
        top = jnp.max(scores, axis=0, keepdims=True)
        terms = jnp.exp(scores - top)
        total = jnp.sum(terms, axis=0, keepdims=True)
        lse = top + jnp.log(total)
        for head in range(2):
            lse_ref[0, pair, head : head + 1, at : at + TILE] = lse[:, head * TILE : (head + 1) * TILE]
        return (terms * (1.0 / total)).astype(bf16)

    def put_context(tile, probs):
        pair, (lo, hi, at) = tile
        context = dot(vt_ref[pair * lanes : (pair + 1) * lanes, lo:hi], probs)
        for head in range(2):
            rows = slice(pair * lanes + head * half, pair * lanes + (head + 1) * half)
            part = context[head * half : (head + 1) * half, head * TILE : (head + 1) * TILE]
            ct_ref[rows, at : at + TILE] = part.astype(bf16)

    ready = {}
    probs = {}
    for step in range(len(tiles) + 2):
        if step < len(tiles):
            ready[step] = scores_of(tiles[step])
        if 0 <= step - 1 < len(tiles):
            probs[step - 1] = probs_of(tiles[step - 1], ready.pop(step - 1))
        if 0 <= step - 2:
            put_context(tiles[step - 2], probs.pop(step - 2))
    ctx_ref[...] = ct_ref[...].T


def attend(index, qkv, seg_rows, row, before=(), after=()):
    count, width = qkv.shape[0], qkv.shape[1] // 3
    rows, _, length = seg_rows.shape
    pairs = HEADS // 2
    return call(
        attend_kernel,
        (1,),
        [
            pl.BlockSpec((length, 3 * width), lambda i, s: (row, 0)),
            pl.BlockSpec((1, 1, length), lambda i, s: (row, 0, 0)),
        ]
        + [ANY] * len(before),
        [
            pl.BlockSpec((length, width), lambda i, s: (row, 0)),
            pl.BlockSpec((1, pairs, 2, length), lambda i, s: (row, 0, 0, 0)),
        ],
        [shaped((count, width), bf16), shaped((rows, pairs, 2, length), f32)],
        [
            pltpu.VMEM((width, length), bf16),
            pltpu.VMEM((width, length), bf16),
            pltpu.VMEM((length, length), f32),
        ],
        length * length * width * 4,
        length * width * 8,
        length * length * HEADS * 5 // 8,
        after,
        {3 + i: i for i in range(len(before))},
    )(index, qkv, seg_rows, *before)


def row_stats(values):
    mean = jnp.mean(values, axis=-1, keepdims=True)
    centred = values - mean
    spread = jnp.mean(centred * centred, axis=-1, keepdims=True)
    return centred, lax.rsqrt(spread + norm_eps)


def project_kernel(meta, sizes, index_ref, ctx_ref, tok_ref, table_ref, *rest):
    pieces, rest = rest[: len(meta)], rest[len(meta) :]
    norm_ref, root_ref, hid_ref, vec_ref, up_ref, w_ref, sems = rest
    width = w_ref.shape[0]

    @pl.when(pl.program_id(0) == 0)
    def _():
        rows = width // BLOCKS
        here = slice(0, width)
        copies = copies_of(meta, rows, pieces, w_ref, sems, index_ref[0], here, here)
        start_all(copies)
        at = sizes[0] + -sizes[0] % TILE
        line = 0
        vec_ref[...] = jnp.zeros_like(vec_ref)
        for size in sizes[1:]:
            value, at = spread(table_ref[...], at, size)
            if value.shape[1] == width:
                vec_ref[line : line + 1] = value
                line += 1
            else:
                up_ref[...] = value
        wait_all(copies)

    def finish(here, product):
        summed = tok_ref[here].astype(f32) + (product + vec_ref[0:1])
        centred, root = row_stats(summed)
        normed = centred * root
        norm_ref[here] = normed
        root_ref[here] = root
        hid_ref[here] = (normed * vec_ref[1:2] + vec_ref[2:3]).astype(bf16)

    in_turn(ctx_ref.shape[0], lambda here: dot(ctx_ref[here], w_ref[...]), finish)


def in_turn(count, begin, finish, size=2 * TILE):
    last = None
    for at in range(0, count, size):
        here = slice(at, at + size)
        value = begin(here)
        if last is not None:
            finish(*last)
        last = (here, value)
    finish(*last)


def project(index, context, tokens, table, pieces, sizes, step=512):
    count, width = tokens.shape
    inner = 4 * width
    meta = meta_of(pieces)
    rows = pl.BlockSpec((step, width), lambda i, s: (i, 0))
    return call(
        functools.partial(project_kernel, meta, sizes),
        (count // step,),
        [rows, rows, whole(table.shape)] + [ANY] * len(meta),
        [
            rows,
            pl.BlockSpec((step, 1), lambda i, s: (i, 0)),
            rows,
            whole((SEGS, width)),
            whole((1, inner)),
        ],
        [
            shaped((count, width), f32),
            shaped((count, 1), f32),
            shaped((count, width), bf16),
            shaped((SEGS, width), f32),
            shaped((1, inner), f32),
        ],
        [pltpu.VMEM((width, width), bf16), pltpu.SemaphoreType.DMA((len(meta),))],
        count * width * width * 2,
        count * width * 10 + width * width * 2,
    )(index, context, tokens, table, *arrays_of(pieces))


def gelu_parts(value):
    share = 0.5 * lax.erf(value * math.sqrt(0.5)) + 0.5
    bell = jnp.exp2(value * value * (-0.5 / math.log(2.0)))
    return value * share, share + value * bell * (1.0 / math.sqrt(2.0 * math.pi))


def up_kernel(meta, index_ref, hid_ref, bias_ref, *rest):
    pieces, rest = rest[: len(meta)], rest[len(meta) :]
    act_ref, slope_ref, w_ref, sems = rest
    tile = act_ref.shape[1]
    width = w_ref.shape[0]
    step = pl.program_id(0)

    def weights(number):
        source, place = columns(number, tile, width), columns(number, tile)
        rows = width // BLOCKS
        return copies_of(meta, rows, pieces, w_ref, sems.at[number], index_ref[0], source, place)

    @pl.when(step == 0)
    def _():
        for number in range(sems.shape[0]):
            start_all(weights(number))

    wait_all(weights(step))
    wide = 256

    def begin(cols):
        w = w_ref[:, columns(step, tile)] if wide == tile else w_ref[:, pl.ds(
            pl.multiple_of(step * tile + cols.start, wide), wide
        )]
        return dot(hid_ref[...], w) + bias_ref[:, cols]

    def finish(cols, value):
        act, slope = gelu_parts(value)
        act_ref[:, cols] = act.astype(bf16)
        slope_ref[:, cols] = slope.astype(bf16)

    in_turn(tile, begin, finish, wide)


def up(index, hidden, bias, pieces, after=(), tile=768):
    count, width = hidden.shape
    inner = bias.shape[1]
    meta = meta_of(pieces)
    out = pl.BlockSpec((count, tile), lambda i, s: (0, i))
    return call(
        functools.partial(up_kernel, meta),
        (inner // tile,),
        [whole((count, width)), pl.BlockSpec((1, tile), lambda i, s: (0, i))] + [ANY] * len(meta),
        [out, out],
        [shaped((count, inner), bf16), shaped((count, inner), bf16)],
        [
            pltpu.VMEM((width, inner), bf16),
            pltpu.SemaphoreType.DMA((inner // tile, len(meta))),
        ],
        count * width * inner * 2,
        count * (width * 2 + inner * 4) + width * inner * 2,
        count * inner * 4,
        after,
    )(index, hidden, bias, *arrays_of(pieces))


def down_kernel(meta, index_ref, act_ref, norm_ref, vec_ref, seg_ref, pos_ref, *rest):
    pieces, rest = rest[: len(meta)], rest[len(meta) :]
    res_ref, norm2_ref, root_ref, pay_ref, pool_ref, stat_ref, w_ref, sum_ref, num_ref, sems = rest
    step = pl.program_id(0)
    steps = pl.num_programs(0)
    width = res_ref.shape[1]
    inner = w_ref.shape[0]
    copies = copies_of(meta, inner // BLOCKS, pieces, w_ref, sems, index_ref[0])

    @pl.when(step == 0)
    def _():
        start_all(copies)
        sum_ref[...] = jnp.zeros_like(sum_ref)
        num_ref[...] = jnp.zeros_like(num_ref)
        wait_all(copies)

    seg = seg_ref[0]
    wanted = lax.broadcasted_iota(jnp.int32, (SEGS, seg.shape[1]), 0)
    member = (wanted == seg).astype(f32)
    member_b = member.astype(bf16)
    own = pl.ds(pl.multiple_of(step // (steps * SEGS // sum_ref.shape[0]) * SEGS, SEGS), SEGS)
    num_ref[own] += jnp.broadcast_to(jnp.sum(member, axis=1, keepdims=True), (SEGS, TAIL))

    def finish(here, product):
        hidden = norm_ref[here] * vec_ref[1:2] + vec_ref[2:3]
        summed = hidden + (product + vec_ref[3:4])
        centred, root = row_stats(summed)
        normed = centred * root
        result = normed * vec_ref[4:5] + vec_ref[5:6]
        norm2_ref[here] = normed
        root_ref[here] = root
        high = result.astype(bf16)
        res_ref[here] = high
        low = (result - high.astype(f32)).astype(bf16)
        sum_ref[own] += dot(member_b[:, here], high) + dot(member_b[:, here], low)

    in_turn(act_ref.shape[0], lambda here: dot(act_ref[here], w_ref[...]), finish)

    @pl.when(step == steps - 1)
    def _():
        counts = num_ref[:, 0:1]
        pooled = sum_ref[...] / counts
        scale = lax.rsqrt(jnp.mean(pooled * pooled, axis=-1, keepdims=True) + pool_eps)
        pool_ref[...] = pooled
        lane = lax.broadcasted_iota(jnp.int32, (pooled.shape[0], TAIL), 1)
        stat_ref[...] = jnp.where(lane == 0, scale, counts)
        pay_ref[:, :width] = (pooled * scale).astype(bf16)
        partner = pos_ref[...]
        digit = jnp.where(lane == 0, partner // BASE, partner % BASE)
        pay_ref[:, width:] = jnp.where(lane < 2, digit, 0).astype(f32).astype(bf16)


def down(index, activated, normed, vectors, seg_rows, positive, pieces, step=512):
    count, width = normed.shape
    inner = activated.shape[1]
    rows, _, length = seg_rows.shape
    own = rows * SEGS
    per_row = length // step
    meta = meta_of(pieces)
    block = pl.BlockSpec((step, width), lambda i, s: (i, 0))
    return call(
        functools.partial(down_kernel, meta),
        (count // step,),
        [
            pl.BlockSpec((step, inner), lambda i, s: (i, 0)),
            block,
            whole(vectors.shape),
            pl.BlockSpec((1, 1, step), lambda i, s: (i // per_row, 0, i % per_row)),
            whole((own, 1)),
        ]
        + [ANY] * len(meta),
        [
            block,
            block,
            pl.BlockSpec((step, 1), lambda i, s: (i, 0)),
            whole((own, width + TAIL)),
            whole((own, width)),
            whole((own, TAIL)),
        ],
        [
            shaped((count, width), bf16),
            shaped((count, width), f32),
            shaped((count, 1), f32),
            shaped((own, width + TAIL), bf16),
            shaped((own, width), f32),
            shaped((own, TAIL), f32),
        ],
        [
            pltpu.VMEM((inner, width), bf16),
            pltpu.VMEM((own, width), f32),
            pltpu.VMEM((own, TAIL), f32),
            pltpu.SemaphoreType.DMA((len(meta),)),
        ],
        count * width * inner * 2,
        count * (width * 10 + inner * 2) + width * inner * 2,
        near=(3, 5, -4, -5, -6),
    )(index, activated, normed, vectors, seg_rows, positive, *arrays_of(pieces))


def segment_of(row, own, cores, chips, planes):
    block = row // own
    plane, chip, core = block % planes, block // planes % chips, block // (planes * chips)
    return ((plane * chips + chip) * cores + core) * own + row % own


def contrast_kernel(layout, place_ref, own_ref, pos_ref, pool_ref, stat_ref, *rest):
    pieces, (loss_ref, grad_ref, all_ref, sems) = rest[:-4], rest[-4:]
    copies, at = [], 0
    for number, piece in enumerate(pieces):
        here = all_ref.at[at : at + piece.shape[0]]
        copies.append(pltpu.make_async_copy(piece, here, sems.at[number]))
        at += piece.shape[0]
    for copy in copies:
        copy.start()
    for copy in copies:
        copy.wait()
    total = all_ref.shape[0]
    own, width = pool_ref.shape
    factor = score_scale / width
    block = min(total, 512)
    flip, first = place_ref[0], place_ref[1]
    mine = own_ref[:, :width]
    mine_id = lax.broadcasted_iota(jnp.int32, (own, total), 0) + first
    other_id = segment_of(lax.broadcasted_iota(jnp.int32, (1, total), 1), own, *layout) ^ flip
    logits = dot_nt(mine, all_ref[:, :width]) * factor
    logits = jnp.where(mine_id == other_id, masked_value, logits)
    top = jnp.max(logits, axis=1, keepdims=True)
    log_own = top + jnp.log(jnp.sum(jnp.exp(logits - top), axis=1, keepdims=True))
    is_positive = other_id == pos_ref[...]
    picked = jnp.sum(jnp.where(is_positive, logits, 0.0), axis=1, keepdims=True)
    loss_ref[...] = log_own - picked
    d_logits = pair_weight * (jnp.exp(logits - log_own) - is_positive.astype(f32))
    d_emb = dot(d_logits.astype(bf16), all_ref[:, :width])
    lane = lax.broadcasted_iota(jnp.int32, (SEGS, TAIL), 1)
    digits = jnp.where(lane == 0, float(BASE), jnp.where(lane == 1, 1.0, 0.0)).astype(bf16)
    for at in range(0, total, block):
        rows = slice(at, at + block)
        table = dot_nt(all_ref[:, :width], all_ref[rows, :width]) * factor
        left = lax.broadcasted_iota(jnp.int32, (total, block), 0)
        right = lax.broadcasted_iota(jnp.int32, (total, block), 1) + at
        table = jnp.where(left == right, masked_value, table)
        top = jnp.max(table, axis=0, keepdims=True)
        log_all = top + jnp.log(jnp.sum(jnp.exp(table - top), axis=0, keepdims=True))
        partner = dot_nt(digits, all_ref[rows, width:])[0:1].astype(jnp.int32)
        chosen = partner == mine_id[:, rows]
        back = pair_weight * (jnp.exp(logits[:, rows] - log_all) - chosen.astype(f32))
        d_emb += dot(back.astype(bf16), all_ref[rows, :width])
    d_emb = d_emb * factor
    scale, counts = stat_ref[:, 0:1], stat_ref[:, 1:2]
    pooled = pool_ref[...]
    along = jnp.mean(d_emb * pooled, axis=-1, keepdims=True)
    grad_ref[...] = (d_emb * scale - pooled * (scale * scale * scale * along)) / counts


def contrast(place, layout, everyone, payload, positive, pooled, stats):
    own, width = pooled.shape
    total = sum(v.shape[0] for v in everyone)
    return call(
        functools.partial(contrast_kernel, layout),
        (1,),
        [whole(v.shape) for v in (payload, positive, pooled, stats)] + [ANY] * len(everyone),
        [whole((own, 1)), whole((own, width))],
        [shaped((own, 1), f32), shaped((own, width), f32)],
        [
            pltpu.VMEM((total, width + TAIL), bf16),
            pltpu.SemaphoreType.DMA((len(everyone),)),
        ],
        total * total * width * 2,
        total * width * 2,
        total * total,
        near=(1, 2, 3, 4, -1, -2),
    )(place, payload, positive, pooled, stats, *everyone)


def norm_back(d_out, normed, root, gain):
    scaled = d_out * gain
    mean = jnp.mean(scaled, axis=-1, keepdims=True)
    along = jnp.mean(scaled * normed, axis=-1, keepdims=True)
    return root * (scaled - mean - normed * along)


def column_sum(values):
    return jnp.sum(values, axis=0, keepdims=True)


def norm2_kernel(turns, index_ref, og_ref, norm_ref, root_ref, seg_ref, gain_ref, dp_ref, *rest):
    act_ref, dsum_ref, ddown_ref, vec_ref, keep_ref, send_ref, dt_ref = rest
    step = pl.program_id(0)
    chunk, width = og_ref.shape
    own = dp_ref.shape[0]

    @pl.when(step == 0)
    def _():
        vec_ref[...] = jnp.zeros_like(vec_ref)

    @pl.when(step < turns)
    def _():
        row = step // (turns * SEGS // own)
        pool = dp_ref[pl.ds(pl.multiple_of(row * SEGS, SEGS), SEGS)]
        high = pool.astype(bf16)
        left = pool - high.astype(f32)
        mid = left.astype(bf16)
        low = (left - mid.astype(f32)).astype(bf16)
        pad = jnp.zeros((TILE - 3 * SEGS, width), bf16)
        table = jnp.concatenate([high, mid, low, pad], axis=0)
        lane = lax.broadcasted_iota(jnp.int32, (TILE, TILE), 1)

        def begin(here):
            member = (lane % SEGS == seg_ref[here]).astype(f32).astype(bf16)
            return dot(member, table)

        def finish(here, shared):
            d_res = og_ref[here].astype(f32) + shared
            normed = norm_ref[here]
            d_sum = norm_back(d_res, normed, root_ref[here], gain_ref[...])
            d_down = d_sum.astype(bf16)
            dsum_ref[here] = d_sum
            ddown_ref[here] = d_down
            dt_ref[:, columns(step, chunk) if chunk == TILE else pl.ds(
                pl.multiple_of(step * chunk + here.start, TILE), TILE
            )] = d_down.T
            vec_ref[0:1] += column_sum(d_down.astype(f32))
            vec_ref[1:2] += column_sum(d_res * normed)
            vec_ref[2:3] += column_sum(d_res)

        in_turn(chunk, begin, finish, TILE)

    @pl.when(step >= turns)
    def _():
        grad = dot(dt_ref[...], act_ref[...]).astype(bf16)
        half = grad.shape[1] // 2
        odd = index_ref[0] % 2 == 1
        keep_ref[0] = jnp.where(odd, grad[:, half:], grad[:, :half])
        send_ref[0] = jnp.where(odd, grad[:, :half], grad[:, half:])


def norm2(index, out_grad, normed, root, seg_col, gain, d_pool, activated, turns=4):
    count, width = out_grad.shape
    inner = activated.shape[1]
    tile = inner // 4
    own = d_pool.shape[0]
    first = lambda i: jnp.minimum(i, turns - 1)
    then = lambda i: jnp.maximum(i - turns, 0)
    block = pl.BlockSpec((count // turns, width), lambda i, s: (first(i), 0))
    column = pl.BlockSpec((count // turns, 1), lambda i, s: (first(i), 0))
    grads = pl.BlockSpec((1, width, tile // 2), lambda i, s: (then(i), 0, 0))
    return call(
        functools.partial(norm2_kernel, turns),
        (turns + 4,),
        [
            block,
            block,
            column,
            column,
            whole((1, width)),
            whole((own, width)),
            pl.BlockSpec((count, tile), lambda i, s: (0, (s[0] // 2) ^ then(i))),
        ],
        [block, block, whole((SEGS, width)), grads, grads],
        [
            shaped((count, width), f32),
            shaped((count, width), bf16),
            shaped((SEGS, width), f32),
            shaped((4, width, tile // 2), bf16),
            shaped((4, width, tile // 2), bf16),
        ],
        [pltpu.VMEM((width, count), bf16)],
        count * width * inner * 2,
        count * (width * 12 + inner * 2) + width * inner * 2,
        near=(5, 6, -1, -2, -3, -4, -5),
    )(index, out_grad, normed, root, seg_col, gain, d_pool, activated)


def put_turned(source_ref, target_ref, turn_ref, index):
    turn_ref[...] = source_ref[...].T
    rows = turn_ref.shape[0] // BLOCKS
    for place in range(BLOCKS):
        block = index ^ ((place % 4) * 2 + place // 4)
        start = pl.multiple_of(block * rows, 16)
        target_ref[place * rows : (place + 1) * rows] = turn_ref[pl.ds(start, rows)]


def up_back_kernel(
    down_meta, up_meta, first, before, index_ref, ddown_ref, slope_ref, hid_ref, *rest
):
    low_pieces, rest = rest[: len(down_meta)], rest[len(down_meta) :]
    up_pieces, rest = rest[: len(up_meta)], rest[len(up_meta) + before :]
    dhid_ref, bias_ref, keep_ref, send_ref, wd_ref, wu_ref, turn_ref, ht_ref, sems, up_sems = rest
    step = pl.program_id(0)
    tile = slope_ref.shape[1]
    width = ht_ref.shape[0]
    index = index_ref[0]
    steps = sems.shape[0]

    def weights(number):
        copies = []
        here = wd_ref.at[pl.ds(pl.multiple_of(number * tile, tile), tile)]
        for piece, ((place, off, size), ref) in enumerate(zip(down_meta, low_pieces)):
            start = pl.multiple_of(((index ^ place) % 2) * (tile // 2) + off, 16)
            copies.append((place // 2 - first, ref, here.at[pl.ds(start, size)], sems.at[number, piece]))
        cols = columns((index // 2) ^ (number + first), tile, width)
        high = copies_of(
            up_meta, width // BLOCKS, up_pieces, wu_ref.at[number], up_sems.at[number], index, cols
        )
        return copies, high

    def rows_of(number):
        low, _ = weights(number)
        return [
            pltpu.make_async_copy(ref, here, sem) for place, ref, here, sem in low if place == number
        ]

    @pl.when(step == 0)
    def _():
        for number in range(steps):
            start_all(rows_of(number))
            start_all(weights(number)[1])
        put_turned(hid_ref, ht_ref, turn_ref, index)

    for number in range(steps):

        @pl.when(step == number)
        def _():
            wait_all(rows_of(number))

    wide = 256
    parts = []

    def begin(cols):
        rows = pl.ds(pl.multiple_of(step * tile + cols.start, wide), wide)
        return dot_nt(ddown_ref[...], wd_ref[rows])

    def finish(cols, d_act):
        d_up = (d_act * slope_ref[:, cols].astype(f32)).astype(bf16)
        bias_ref[:, cols] = column_sum(d_up.astype(f32))
        parts.append(d_up)

    in_turn(tile, begin, finish, wide)
    d_up = jnp.concatenate(parts, axis=1)
    grad = dot(ht_ref[...], d_up).astype(bf16)
    half = width // 2
    keep_ref[...] = grad[:half].reshape(keep_ref.shape)
    send_ref[...] = grad[half:].reshape(send_ref.shape)
    wait_all(weights(step)[1])
    share = dot_nt(d_up, wu_ref[step])

    @pl.when(step == 0)
    def _():
        dhid_ref[...] = share

    @pl.when(step > 0)
    def _():
        dhid_ref[...] += share


def up_back(index, d_down, slope, hidden, down_pieces, up_pieces, first, steps, before=(), after=()):
    count, width = d_down.shape
    inner = slope.shape[1]
    tile = inner // 4
    part = width // BLOCKS
    down_meta, up_meta = meta_of(down_pieces), meta_of(up_pieces)
    place = lambda i, s: (s[0] // 2) ^ (i + first)
    grads = pl.BlockSpec((4, part, tile), lambda i, s: (0, 0, place(i, s)))
    given = 4 + len(down_meta) + len(up_meta)
    return call(
        functools.partial(up_back_kernel, down_meta, up_meta, first, len(before)),
        (steps,),
        [
            whole((count, width)),
            pl.BlockSpec((count, tile), lambda i, s: (0, place(i, s))),
            whole((count, width)),
        ]
        + [ANY] * (len(down_meta) + len(up_meta) + len(before)),
        [
            whole((count, width)),
            pl.BlockSpec((1, tile), lambda i, s: (0, place(i, s))),
            grads,
            grads,
        ],
        [
            shaped((count, width), f32),
            shaped((1, inner), f32),
            shaped((4, part, inner), bf16),
            shaped((4, part, inner), bf16),
        ],
        [
            pltpu.VMEM((steps * tile, width), bf16),
            pltpu.VMEM((steps, width, tile), bf16),
            pltpu.VMEM((width, count), bf16),
            pltpu.VMEM((width, count), bf16),
            pltpu.SemaphoreType.DMA((steps, len(down_meta))),
            pltpu.SemaphoreType.DMA((steps, len(up_meta))),
        ],
        count * width * tile * 6 * steps,
        count * (width * 8 + inner) + width * inner * 6,
        0,
        after,
        {given + i: 1 + i for i in range(len(before))},
        (1, -1, -2, -3, -4) + tuple(range(given, given + len(before))),
        40 * 1024 * 1024,
    )(index, d_down, slope, hidden, *arrays_of(down_pieces), *arrays_of(up_pieces), *before)


def cut_vector(vector, size, index):
    width = vector.shape[1]
    owner = lax.broadcasted_iota(jnp.int32, (BLOCKS, width), 1) // size
    wanted = lax.broadcasted_iota(jnp.int32, (BLOCKS, width), 0) ^ index
    rows = jnp.where(owner == wanted, vector, 0.0).astype(bf16)
    source = lax.broadcasted_iota(jnp.int32, (width, 1), 0)
    place = source - source // size * size == lax.broadcasted_iota(jnp.int32, (width, TILE), 1)
    return dot(rows, place.astype(f32).astype(bf16))


def norm1_kernel(meta, parts, index_ref, *rest):
    dhids, rest = rest[:parts], rest[parts:]
    dsum_ref, norm_ref, root_ref, gain_ref, ctx_ref, other_ref, up_ref, *rest = rest
    pieces, rest = rest[: len(meta)], rest[len(meta) :]
    dattn_ref, dctx_ref, keep_ref, send_ref, w_ref, acc_ref, vec_ref, sems = rest
    step = pl.program_id(0)
    width = w_ref.shape[0]
    rows = width // BLOCKS

    @pl.when(step == 0)
    def _():
        here = slice(0, width)
        copies = copies_of(meta, rows, pieces, w_ref, sems, index_ref[0], here, here)
        start_all(copies)
        vec_ref[...] = jnp.zeros_like(vec_ref)
        acc_ref[...] = jnp.zeros_like(acc_ref)
        wait_all(copies)

    parts = []

    def begin(here):
        d_hid = dsum_ref[here]
        for dhid_ref in dhids:
            d_hid = d_hid + dhid_ref[here]
        normed = norm_ref[here]
        d_sum = norm_back(d_hid, normed, root_ref[here], gain_ref[...])
        d_attn = d_sum.astype(bf16)
        dattn_ref[here] = d_sum
        vec_ref[0:1] += column_sum(d_attn.astype(f32))
        vec_ref[1:2] += column_sum(d_hid * normed)
        vec_ref[2:3] += column_sum(d_hid)
        parts.append(d_attn)
        return d_attn

    def finish(here, d_attn):
        dctx_ref[here] = dot_nt(d_attn, w_ref[...]).astype(bf16)

    in_turn(dsum_ref.shape[0], begin, finish)
    acc_ref[...] += dot(ctx_ref[...].T, jnp.concatenate(parts, axis=0))

    @pl.when(step == pl.num_programs(0) - 1)
    def _():
        index = index_ref[0]
        vectors = [vec_ref[i : i + 1] for i in range(3)] + [other_ref[i : i + 1] for i in range(3)]
        top = [cut_vector(vector, rows, index) for vector in vectors]
        top = jnp.concatenate(top, axis=1)
        size = up_ref.shape[1] // BLOCKS
        line = lax.broadcasted_iota(jnp.int32, (16, width), 0)
        pad = jnp.zeros((1, width - size), f32)
        for place in range(4):
            for target, core in ((keep_ref, 0), (send_ref, 1)):
                number = 2 * place + core
                block = index ^ number
                start = pl.multiple_of(block * rows, 16)
                target[place, :rows] = acc_ref[pl.ds(start, rows)].astype(bf16)
                low = up_ref[:, pl.ds(pl.multiple_of(block * size, size), size)]
                low = jnp.concatenate([low, pad], axis=1)
                extra = jnp.where(line == 0, top[number : number + 1], 0.0)
                extra = jnp.where(line == 1, low, extra)
                target[place, rows:] = extra.astype(bf16)


def norm1(
    index, d_hiddens, d_summed, normed, root, gain, context, sums, sums_up, pieces, after=(), step=512
):
    count, width = d_summed.shape
    meta = meta_of(pieces)
    part = width // BLOCKS + 16
    block = pl.BlockSpec((step, width), lambda i, s: (i, 0))
    return call(
        functools.partial(norm1_kernel, meta, len(d_hiddens)),
        (count // step,),
        [block] * len(d_hiddens)
        + [
            block,
            block,
            pl.BlockSpec((step, 1), lambda i, s: (i, 0)),
            whole((1, width)),
            block,
            whole(sums.shape),
            whole(sums_up.shape),
        ]
        + [ANY] * len(meta),
        [block, block, whole((4, part, width)), whole((4, part, width))],
        [
            shaped((count, width), f32),
            shaped((count, width), bf16),
            shaped((4, part, width), bf16),
            shaped((4, part, width), bf16),
        ],
        [
            pltpu.VMEM((width, width), bf16),
            pltpu.VMEM((width, width), f32),
            pltpu.VMEM((SEGS, width), f32),
            pltpu.SemaphoreType.DMA((len(meta),)),
        ],
        count * width * width * 4,
        count * width * 20 + width * width * 4,
        0,
        after,
        near=tuple(range(1, 2 + len(d_hiddens))) + (-1, -2, -3, -4),
    )(
        index, *d_hiddens, d_summed, normed, root, gain, context, sums, sums_up, *arrays_of(pieces)
    )


def attend_back_kernel(
    first, index_ref, q_ref, k_ref, v_ref, dctx_ref, lse_ref, seg_ref, tok_ref, *rest
):
    dq_ref, dk_ref, dv_ref, keep_ref, send_ref = rest[:5]
    mask_ref, turn_ref, tt_ref, kt_ref, two_ref, pt_ref, both_ref = rest[5:]
    rows, _, length = seg_ref.shape
    lanes = 2 * tok_ref.shape[1] // HEADS
    half = lanes // 2
    group = q_ref.shape[1] // lanes
    inv_root = 1.0 / math.sqrt(half)

    @pl.when(pl.program_id(0) == 0)
    def _():
        put_turned(tok_ref, tt_ref, turn_ref, index_ref[0])
        for row in range(rows):
            fill_mask(seg_ref[row].astype(f32), mask_ref.at[row])

    tiles = [
        (pair, row, band) for pair in range(group) for row in range(rows) for band in bands(length)
    ]
    for pair in range(group):
        for row in range(rows):
            here = slice(row * length, (row + 1) * length)
            kt_ref[pair, row] = k_ref[here, pair * lanes : (pair + 1) * lanes].T

    def begin(tile):
        pair, row, (lo, hi, at) = tile
        cols = slice(pair * lanes, (pair + 1) * lanes)
        base = row * length
        queries = two_heads(q_ref[base + at : base + at + TILE, cols])
        d_context = two_heads(dctx_ref[base + at : base + at + TILE, cols])
        two_ref[0, pair, row, 2 * at : 2 * at + 2 * TILE] = queries
        two_ref[1, pair, row, 2 * at : 2 * at + 2 * TILE] = d_context
        scores = dot_nt(k_ref[base + lo : base + hi, cols], queries)
        return scores, dot_nt(v_ref[base + lo : base + hi, cols], d_context)

    def middle_part(tile, scores, d_probs):
        pair, row, (lo, hi, at) = tile
        lse = jnp.concatenate(
            [lse_ref[row, pair, head : head + 1, at : at + TILE] for head in range(2)], axis=1
        )
        probs = jnp.exp(scores + twice(mask_ref[row, lo:hi, at : at + TILE]) - lse)
        inner = jnp.sum(d_probs * probs, axis=0, keepdims=True)
        d_scores = (probs * (d_probs - inner)).astype(bf16)
        pt_ref[0, pair, row, lo:hi, 2 * at : 2 * at + 2 * TILE] = d_scores
        pt_ref[1, pair, row, lo:hi, 2 * at : 2 * at + 2 * TILE] = probs.astype(bf16)
        return d_scores

    def put(tile, kind, value):
        pair, row, (_, _, at) = tile
        here = slice(row * length + at, row * length + at + TILE)
        cols = slice((3 * pair + kind) * lanes, (3 * pair + kind + 1) * lanes)
        both_ref[here, cols] = value.astype(bf16)

    def end(tile, d_scores):
        pair, row, (lo, hi, at) = tile
        dq = dot(kt_ref[pair, row, :, lo:hi], d_scores) * inv_root
        dq = jnp.concatenate([dq[:half, :TILE], dq[half:, TILE:]], axis=0)
        put(tile, 0, dq.T)

    def end_keys(tile):
        pair, row, (lo, hi, at) = tile
        cols = slice(2 * lo, 2 * hi)
        for kind in range(2):
            value = dot(
                pt_ref[kind, pair, row, at : at + TILE, cols], two_ref[kind, pair, row, cols]
            )
            put(tile, 1 + kind, value)

    ready = {}
    done = {}
    for step in range(len(tiles) + 3):
        if step < len(tiles):
            ready[step] = begin(tiles[step])
        if 0 <= step - 1 < len(tiles):
            done[step - 1] = middle_part(tiles[step - 1], *ready.pop(step - 1))
        if 0 <= step - 2 < len(tiles):
            end(tiles[step - 2], done.pop(step - 2))
        if 0 <= step - 3 < len(tiles):
            end_keys(tiles[step - 3])
    both = both_ref[...]
    for pair in range(group):
        for kind, target in enumerate((dq_ref, dk_ref, dv_ref)):
            cols = slice((3 * pair + kind) * lanes, (3 * pair + kind + 1) * lanes)
            target[:, pair * lanes : (pair + 1) * lanes] = both[:, cols]
    grad = dot(tt_ref[...], both).astype(bf16)
    width = grad.shape[0]
    part = width // BLOCKS
    span = both.shape[1]
    col = lax.broadcasted_iota(jnp.int32, (1, span), 1)
    kind = col // lanes % 3
    place = (pl.program_id(0) * group + first + col // (3 * lanes)) * lanes + col % lanes
    owner = jnp.where(kind == 1, -1, (place + jnp.where(kind == 2, width, 0)) // (2 * part))
    sums = column_sum(both.astype(f32))
    line = lax.broadcasted_iota(jnp.int32, (16, span), 0)
    for block in range(BLOCKS):
        target, core = (keep_ref, 0) if block < 4 else (send_ref, 1)
        target[block % 4, :part] = grad[block * part : (block + 1) * part]
        here = owner == (index_ref[0] ^ (2 * (block % 4) + core))
        extra = jnp.where(line == 0, jnp.where(here, sums, 0.0), 0.0)
        target[block % 4, part:] = extra.astype(bf16)


def attend_back(
    index, qkv, d_context, lse, seg_rows, tokens, first, pairs, after=(), group=2
):
    count, width = tokens.shape
    rows, _, length = seg_rows.shape
    every = HEADS // 2
    lanes = width // every
    part = width // BLOCKS + 16
    wide = group * lanes
    column = lambda place: pl.BlockSpec((count, wide), lambda i, s: (0, place // group + i))
    out = pl.BlockSpec((count, wide), lambda i, s: (0, i))
    grads = pl.BlockSpec((4, part, 3 * wide), lambda i, s: (0, 0, i))
    return call(
        functools.partial(attend_back_kernel, first),
        (pairs // group,),
        [
            column(first),
            column(every + first),
            column(2 * every + first),
            column(first),
            pl.BlockSpec((rows, group, 2, length), lambda i, s: (0, first // group + i, 0, 0)),
            whole((rows, 1, length)),
            whole((count, width)),
        ],
        [out, out, out, grads, grads],
        [
            shaped((count, pairs * lanes), bf16),
            shaped((count, pairs * lanes), bf16),
            shaped((count, pairs * lanes), bf16),
            shaped((4, part, pairs * 3 * lanes), bf16),
            shaped((4, part, pairs * 3 * lanes), bf16),
        ],
        [
            pltpu.VMEM((rows, length, length), f32),
            pltpu.VMEM((width, count), bf16),
            pltpu.VMEM((width, count), bf16),
            pltpu.VMEM((group, rows, lanes, length), bf16),
            pltpu.VMEM((2, group, rows, 2 * length, lanes), bf16),
            pltpu.VMEM((2, group, rows, length, 2 * length), bf16),
            pltpu.VMEM((count, 3 * wide), bf16),
        ],
        count * pairs * lanes * (width * 6 + length * 6),
        count * pairs * lanes * 14 + count * width * 2,
        count * length * pairs * 5 // 4,
        after,
        near=(4, -1, -2, -3, -4, -5),
    )(index, qkv, qkv, qkv, d_context, lse, seg_rows, tokens)


def input_kernel(meta, parts, index_ref, dattn_ref, *rest):
    grads, rest = rest[: 3 * parts], rest[3 * parts :]
    pieces, rest = rest[: len(meta)], rest[len(meta) :]
    out_ref, w_ref, sems = rest
    width = out_ref.shape[1]
    step = width // parts
    first = pl.program_id(0) == 0

    def weights(kind):
        cols = columns(kind, width)
        rows = width // BLOCKS
        return copies_of(meta, rows, pieces, w_ref, sems.at[kind], index_ref[0], cols, cols)

    @pl.when(first)
    def _():
        for kind in range(3):
            start_all(weights(kind))

    total = dattn_ref[...]
    for kind in range(3):

        @pl.when(first)
        def _():
            wait_all(weights(kind))

        for part in range(parts):
            at = kind * width + part * step
            total += dot_nt(grads[kind * parts + part][...], w_ref[:, at : at + step])
    out_ref[...] = total


def input_grad(index, d_attn, grads, pieces, after=(), step=512):
    count, width = d_attn.shape
    meta = meta_of(pieces)
    parts = len(grads) // 3
    block = pl.BlockSpec((step, width), lambda i, s: (i, 0))
    return call(
        functools.partial(input_kernel, meta, parts),
        (count // step,),
        [block]
        + [pl.BlockSpec((step, g.shape[1]), lambda i, s: (i, 0)) for g in grads]
        + [ANY] * len(meta),
        block,
        shaped((count, width), f32),
        [pltpu.VMEM((width, 3 * width), bf16), pltpu.SemaphoreType.DMA((3, len(meta)))],
        count * width * width * 6,
        count * width * 14 + width * width * 6,
        0,
        after,
        near=tuple(range(1, 2 + len(grads))),
    )(index, d_attn, *grads, *arrays_of(pieces))


def rounded(value):
    return lax.optimization_barrier(value.astype(bf16))


def add(*values):
    total = values[0].astype(f32)
    for value in values[1:]:
        total = total + value.astype(f32)
    return total


def along_z(value, pairs):
    return lax.ppermute(value, "batch", pairs)


class Sum:
    def __init__(self, planes, keeps, sends, line):
        self.planes, self.keeps, self.line = planes, keeps, line
        self.arrived = [fsdp_swap(send, 1) for send in sends]
        self.stages = [self.over_core, self.over_far, self.over_chips, self.over_z, self.over_middle]

    def next(self, clock):
        if clock is not None:
            *self.arrived, _ = lax.optimization_barrier((*self.arrived, clock))
        return self.stages.pop(0)(*self.arrived)

    def over_core(self, *others):
        rows = self.keeps[0].shape[1]
        half = rows // 32 * 16
        cuts = [(0, 0, rows), (1, 0, rows), (2, 0, rows), (3, 0, half), (3, half, rows)]
        self.blocks = []
        for place, lo, hi in cuts:
            sums = [
                add(keep[place, lo:hi], other[place, lo:hi]).astype(bf16)
                for keep, other in zip(self.keeps, others)
            ]
            self.blocks.append(rounded(jnp.concatenate(sums, axis=1)))
        self.half = half
        self.arrived = [fsdp_swap(self.blocks[3], 2), fsdp_swap(self.blocks[4], 4)]
        return self.blocks[3:]

    def over_far(self, top, low):
        _, over_x, over_y, _, _ = self.blocks
        half = self.half
        over_x = over_x.at[half:].set(add(over_x[half:], low).astype(bf16))
        over_y = over_y.at[:half].set(add(over_y[:half], top).astype(bf16))
        self.arrived = [fsdp_swap(over_x, 2), fsdp_swap(over_y, 4)]
        return [over_x, over_y]

    def over_chips(self, from_x, from_y):
        self.total = rounded(add(self.blocks[0], from_x, from_y))
        pairs = [(0, 1), (3, 2)] if self.line else [(0, 1), (1, 0), (2, 3), (3, 2)]
        self.arrived = [along_z(self.total, pairs)]
        return [self.total]

    def over_z(self, other):
        self.total = rounded(add(self.total, other))
        pairs = [(1, 2), (2, 1)] if self.line else [(0, 2), (2, 0), (1, 3), (3, 1)]
        self.arrived = [along_z(self.total, pairs)]
        return [self.total]

    def over_middle(self, other):
        if self.line:
            self.total = rounded(add(self.total, other))
            self.arrived = [along_z(self.total, [(1, 0), (2, 3)])]
        return [self.total]

    def result(self):
        other = self.arrived[0]
        if not self.line:
            return add(self.total, other)
        plane = lax.axis_index("batch")
        inside = (plane == 1) | (plane == 2)
        return jnp.where(inside, self.total, other).astype(f32)


def layer(
    planes,
    ring,
    tokens,
    seg_ids,
    positive,
    out_grad,
    w_qkv,
    b_qv,
    w_out,
    b_out,
    norm1_gain,
    norm1_shift,
    w_up,
    b_up,
    w_down,
    b_down,
    norm2_gain,
    norm2_shift,
):
    paired = ring == BLOCKS and planes == 4
    row_count, row_length, width = tokens.shape
    count = row_count * row_length
    own = row_count * SEGS
    token_rows = tokens.reshape(count, width)
    seg_rows = seg_ids.reshape(row_count, 1, row_length)
    seg_col = seg_ids.reshape(count, 1)
    pos_col = positive.reshape(own, 1)
    fsdp = lax.axis_index("fsdp")
    me = lax.axis_index("batch") * ring + fsdp
    index = (fsdp if paired else jnp.zeros_like(fsdp)).reshape(1).astype(jnp.int32)
    tie = lax.optimization_barrier

    small = (b_qv, b_out, norm1_gain, norm1_shift, b_down, norm2_gain, norm2_shift, b_up)
    sizes = [value.shape[0] * ring // BLOCKS for value in small]
    join = lambda left, right: jnp.concatenate([left, right], axis=1)
    if paired:
        first_xy = first_stage(w_qkv)
        line = tie(pack_small(small))
        lines = [(line, 0, 0)] + [(fsdp_swap(line, bit), bit, 0) for bit in (2, 4, 6)]
        lines = lines + [(fsdp_swap(value, 1), bit ^ 1, 0) for value, bit, _ in lines]
        first_xy = list(first_xy)
        *first_xy, line, second = tie((*first_xy, line, join(w_out, w_up)))
        first_far = second_stage(w_qkv, *first_xy)
        second, *_ = tie((second, *first_far))
        second_xy = first_stage(second)
        qkv_pieces = all_pieces(w_qkv, *first_xy, *first_far)
    else:
        blocks = [gather_whole(value) for value in (w_qkv, w_out, w_up, w_down, *small)]
        lines = [(pack_small(b[4:]), i, 0) for i, b in enumerate(zip(*blocks))]
        qkv_pieces = [(b[0], i, 0) for i, b in enumerate(zip(*blocks))]
        mid_pieces = [(join(b[1], b[2]), i, 0) for i, b in enumerate(zip(*blocks))]
        down_pieces = [(b[3], i, 0) for i, b in enumerate(zip(*blocks))]

    qkv, table = project_qkv(index, token_rows, qkv_pieces, lines, sizes[0])
    attended = ()
    for row in range(row_count):
        late = ()
        if paired and row == row_count - 1:
            *attended, over_x, over_y, third = tie((*attended, *second_xy, w_down))
            second_far = second_stage(second, over_x, over_y)
            third_xy = first_stage(third)
            late = (over_x, over_y)
        attended = attend(index, qkv, seg_rows, row, attended, late)
    context, lse = attended
    if paired:
        mid_pieces = all_pieces(second, over_x, over_y, *second_far)
    normed1, root1, hidden, rows, bias_up = project(
        index, context, token_rows, table, mid_pieces, sizes
    )
    late = ()
    if paired:
        hidden, *third_xy = tie((hidden, *third_xy))
        third_far = second_stage(w_down, *third_xy)
        down_pieces = all_pieces(w_down, *third_xy, *third_far)
        late = tuple(third_xy)
    activated, slope = up(index, hidden, bias_up, mid_pieces, late)
    result, normed2, root2, payload, pooled, stats = down(
        index, activated, normed1, rows, seg_rows, pos_col, down_pieces
    )

    if paired:
        line = [payload] + [swap(payload, "batch", planes, bit) for bit in (1, 2, 3)]
        line = jnp.concatenate(line, axis=0)
        plane = [line] + [fsdp_swap(line, bit) for bit in (2, 4, 6)]
        plane = jnp.concatenate(plane, axis=0)
        everyone = [plane, fsdp_swap(plane, 1)]
        layout = (2, ring // 2, planes)
        flip = me * own
    else:
        everyone = [lax.all_gather(payload, ("batch", "fsdp"), axis=0, tiled=True)]
        layout = (1, planes * ring, 1)
        flip = jnp.zeros_like(me)
    place = jnp.stack([flip, me * own]).astype(jnp.int32)
    pair_loss, d_pool = contrast(place, layout, everyone, payload, pos_col, pooled, stats)

    def start(keeps, sends, line):
        return Sum(planes, keeps, sends, line) if paired else None

    def go(clock, *sums):
        sent = []
        for one in sums:
            if one is not None:
                sent += one.next(clock)
        return tuple(sent)

    gain1, gain2 = rows[1:2], rows[4:5]
    d_summed, d_down, sums2, keep_down, send_down = norm2(
        index, out_grad.reshape(count, width), normed2, root2, seg_col, gain2, d_pool, activated
    )
    sum_down = start([keep_down], [send_down], True)
    halves = [up_back(index, d_down, slope, hidden, down_pieces, mid_pieces, 0, 2)]
    sent = go(halves[0][0], sum_down)
    before = tuple(halves[0][1:])
    halves.append(
        up_back(index, d_down, slope, hidden, down_pieces, mid_pieces, 2, 2, before, sent)
    )
    _, sums_up, keep_up, send_up = halves[1]
    sum_up = start([keep_up], [send_up], True)
    sent = go(halves[1][0], sum_down)
    d_attn, d_context, keep_out, send_out = norm1(
        index,
        [half[0] for half in halves],
        d_summed,
        normed1,
        root1,
        gain1,
        context,
        sums2,
        sums_up,
        mid_pieces,
        sent,
    )
    sent = go(d_context, sum_up)
    pairs = HEADS // 2
    cuts = 3
    backs = []
    for cut in range(cuts):
        backs.append(
            attend_back(
                index,
                qkv,
                d_context,
                lse,
                seg_rows,
                token_rows,
                cut * pairs // cuts,
                pairs // cuts,
                sent,
            )
        )
        if cut == 0:
            sum_left = start([keep_out, backs[0][3]], [send_out, backs[0][4]], True)
            sent = go(backs[0][0], sum_down, sum_up)
        if cut == 1:
            sent = go(backs[1][0], sum_down, sum_left)
    sum_right = start([backs[1][3], backs[2][3]], [backs[1][4], backs[2][4]], False)
    sent = go(backs[2][0], sum_down, sum_up, sum_left)
    grads = [backs[cut][kind] for kind in range(3) for cut in range(cuts)]
    grad_tokens = input_grad(index, d_attn, grads, qkv_pieces, sent)
    lanes = width // pairs

    part = width // BLOCKS
    if paired:
        go(None, sum_right)
        go(None, sum_left, sum_up)
        go(None, sum_right)
        go(None, sum_left, sum_up)
        go(None, sum_right)
        go(None, sum_left)
        go(None, sum_right)
        go(None, sum_right)
        grad_down, grad_up = sum_down.result().T, sum_up.result()
        left, right = sum_left.result(), sum_right.result()
        grad_out = left[:part, :width]
        grad_qkv = jnp.concatenate([left[:part, width:], right[:part]], axis=1)
        vector = jnp.concatenate([left[part, width:], right[part]])
        own_vectors = [left[part, i * TILE : i * TILE + part] for i in range(6)]
        own_vectors.append(left[part + 1, : sizes[-1]])
    else:

        def scatter(keep, send):
            full = lax.psum(jnp.stack([keep, send], axis=1).astype(f32), "batch")
            return full.reshape((BLOCKS,) + full.shape[2:])

        def own_rows(full):
            full = full.reshape((-1,) + full.shape[2:])
            return lax.psum_scatter(full, "fsdp", scatter_dimension=0, tiled=True)

        def own_values(full):
            return lax.psum_scatter(full.reshape(-1), "fsdp", scatter_dimension=0, tiled=True)

        grad_down = own_rows(scatter(keep_down, send_down).transpose(0, 2, 1))
        grad_up = own_rows(scatter(keep_up, send_up))
        left = scatter(keep_out, send_out)
        grad_out = own_rows(left[:, :part])
        own_vectors = [own_values(left[:, part, i * TILE : i * TILE + part]) for i in range(6)]
        own_vectors.append(own_values(left[:, part + 1, : sizes[-1]]))
        wide = jnp.concatenate([scatter(back[3], back[4]) for back in backs], axis=2)
        grad_qkv = own_rows(wide[:, :part])
        vector = lax.psum(jnp.sum(wide[:, part], axis=0), "fsdp")

    depth = grad_qkv.shape[0]
    grad_qkv = grad_qkv.reshape(depth, pairs, 3, lanes).transpose(0, 2, 1, 3)
    grad_qkv = grad_qkv.reshape(depth, 3 * width)
    vector = vector.reshape(pairs, 3, lanes)
    vector = jnp.concatenate([vector[:, 0].reshape(-1), vector[:, 2].reshape(-1)])
    shard = vector.shape[0] // ring
    grad_bqv = lax.dynamic_slice(vector, (fsdp * shard,), (shard,))
    grad_bout, grad_g1, grad_s1, grad_bdown, grad_g2, grad_s2, grad_bup = own_vectors
    return (
        result.reshape(tokens.shape),
        pair_loss.reshape(own),
        grad_tokens.reshape(tokens.shape),
        grad_qkv,
        grad_bqv,
        grad_out,
        grad_bout,
        grad_g1,
        grad_s1,
        grad_up,
        grad_bup,
        grad_down,
        grad_bdown,
        grad_g2,
        grad_s2,
    )


def solution(mesh):
    rows = P(("batch", "fsdp"), None, None)
    matrix = P("fsdp", None)
    vector = P("fsdp")
    placed = (
        rows,
        P(("batch", "fsdp"), None),
        P(("batch", "fsdp")),
        rows,
        matrix,
        vector,
        matrix,
        vector,
        vector,
        vector,
        matrix,
        vector,
        matrix,
        vector,
        vector,
        vector,
    )
    given = (
        rows,
        P(("batch", "fsdp")),
        rows,
        matrix,
        vector,
        matrix,
        vector,
        vector,
        vector,
        matrix,
        vector,
        matrix,
        vector,
        vector,
        vector,
    )
    return jax.shard_map(
        functools.partial(layer, mesh.shape["batch"], mesh.shape["fsdp"]),
        mesh=mesh,
        in_specs=placed,
        out_specs=given,
        check_vma=False,
    )
```

```python
import functools
import math

import jax
import jax.numpy as jnp
from jax import lax
from jax.experimental import pallas as pl
from jax.experimental.pallas import tpu as pltpu
from jax.sharding import PartitionSpec as P

HEADS = 12
SEGS = 8

norm_eps = 1e-06
pool_eps = 1e-06
score_scale = 50.0
pair_weight = 256.0
masked_value = -1000000000.0

BLOCKS = 8
TILE = 128
TAIL = 128
BASE = 64

bf16 = jnp.bfloat16
f32 = jnp.float32
ANY = pl.BlockSpec(memory_space=pl.ANY)
HELD = pl.BlockSpec(memory_space=pltpu.VMEM)
VMEM_BYTES = 24 * 1024 * 1024


def dot(left, right):
    return jnp.dot(left, right, preferred_element_type=f32)


def dot_nt(left, right):
    return lax.dot_general(left, right, (((1,), (1,)), ((), ())), preferred_element_type=f32)


def whole(shape):
    return pl.BlockSpec(shape, lambda *_: (0,) * len(shape))


def call(
    kernel,
    grid,
    in_specs,
    out_specs,
    out_shape,
    scratch,
    flops,
    moved,
    special=0,
    after=(),
    alias=None,
    near=(),
    room=VMEM_BYTES,
):
    given, extra = len(in_specs) + 1, len(after)
    last = given + extra + len(out_shape)

    def body(*refs):
        refs[last][...] = jnp.zeros_like(refs[last])
        kernel(*refs[:given], *refs[given + extra : last], *refs[last + 1 :])

    shapes = [
        shape if -1 - number in near else pltpu.HBM(shape.shape, shape.dtype)
        for number, shape in enumerate(out_shape)
    ]
    shapes.append(shaped((8, TILE), f32))
    run = pl.pallas_call(
        body,
        out_shape=shapes,
        grid_spec=pltpu.PrefetchScalarGridSpec(
            num_scalar_prefetch=1,
            grid=grid,
            in_specs=in_specs + [ANY] * extra,
            out_specs=out_specs + [whole((8, TILE))],
            scratch_shapes=scratch,
        ),
        input_output_aliases=alias or {},
        compiler_params=pltpu.CompilerParams(vmem_limit_bytes=room),
        cost_estimate=pl.CostEstimate(
            flops=int(flops), bytes_accessed=int(moved), transcendentals=int(special)
        ),
    )

    def apply(index, *operands):
        placed = [
            value if 1 + number in near else pltpu.with_memory_space_constraint(value, pltpu.HBM)
            for number, value in enumerate(operands)
        ]
        return run(index, *placed, *after)

    return apply


def shaped(shape, dtype):
    return jax.ShapeDtypeStruct(shape, dtype)


def swap(value, axis, size, bit):
    return lax.ppermute(value, axis, [(i, i ^ bit) for i in range(size)])


def fsdp_swap(value, bit):
    return swap(value, "fsdp", BLOCKS, bit)


def middle(shard):
    return shard.shape[0] // 32 * 16


def first_stage(shard):
    return fsdp_swap(shard, 2), fsdp_swap(shard, 4)


def second_stage(shard, over_x, over_y):
    half = middle(shard)
    return fsdp_swap(over_y[:half], 2), fsdp_swap(over_x[half:], 4)


def own_pieces(shard, over_x, over_y):
    return [(shard, 0, 0), (over_x, 2, 0), (over_y, 4, 0)]


def far_pieces(shard, far_top, far_low):
    return [(far_top, 6, 0), (far_low, 6, middle(shard))]


def both_cores(pieces):
    return pieces + [(fsdp_swap(value, 1), place ^ 1, off) for value, place, off in pieces]


def gather_whole(shard):
    full = lax.all_gather(shard, "fsdp", axis=0, tiled=True)
    rows = full.shape[0] // BLOCKS
    return [full[i * rows : (i + 1) * rows] for i in range(BLOCKS)]


def meta_of(pieces):
    return tuple((place, off, value.shape[0]) for value, place, off in pieces)


def arrays_of(pieces):
    return [value for value, _, _ in pieces]


def copies_of(
    meta, rows, refs, target, sems, index, source=None, place=None, first=0
):
    copies = []
    for number, ((block, off, count), ref) in enumerate(zip(meta, refs)):
        low, high = max(off, first), min(off + count, first + rows)
        if low >= high:
            continue
        here = pl.ds(pl.multiple_of((index ^ block) * rows + low - first, 16), high - low)
        part = ref.at[low - off : high - off]
        copies.append(
            pltpu.make_async_copy(
                part if source is None else part.at[:, source],
                target.at[here] if place is None else target.at[here, place],
                sems.at[number],
            )
        )
    return copies


def pair_copies(meta, size, refs, target, sems, index, chip):
    copies = []
    for number, ((block, off, count), ref) in enumerate(zip(meta, refs)):
        if block // 2 == chip:
            start = pl.multiple_of((index ^ block) * size + off, 16)
            copies.append(
                pltpu.make_async_copy(ref, target.at[pl.ds(start, count)], sems.at[number])
            )
    return copies


def start_all(copies):
    for copy in copies:
        copy.start()


def wait_all(copies):
    for copy in copies:
        copy.wait()


def columns(number, size, base=0):
    return pl.ds(pl.multiple_of(base + number * size, TILE), size)


def fill_mask(seg_row, mask_ref):
    length = seg_row.shape[1]
    keys = jnp.broadcast_to(seg_row, (TILE, length)).T
    for lo, hi, at in bands(length):
        same = keys[lo:hi] == seg_row[:, at : at + TILE]
        mask_ref[lo:hi, at : at + TILE] = jnp.where(same, 0.0, masked_value)


def bands(length):
    out = []
    for at in range(0, length, TILE):
        out.append((max(at - TILE, 0), min(at + 2 * TILE, length), at))
    return out


def two_heads(pair):
    lane = lax.broadcasted_iota(jnp.int32, (1, pair.shape[1]), 1)
    first = (lane < pair.shape[1] // 2).astype(f32).astype(bf16)
    return jnp.concatenate([pair * first, pair * (1.0 - first)], axis=0)


def twice(value):
    return jnp.concatenate([value, value], axis=1)


def pack_line(vectors, width):
    line = jnp.concatenate([jnp.pad(v, (0, -v.shape[0] % TILE)) for v in vectors])
    return jnp.pad(line[None], ((0, 15), (0, width - line.shape[0])))


def pack_first(w_qkv, b_qv):
    return jnp.concatenate([w_qkv, pack_line([b_qv], w_qkv.shape[1])], axis=0)


def pack_second(w_out, w_up, *vectors):
    both = jnp.concatenate([w_out, w_up], axis=1)
    return jnp.concatenate([both, pack_line(vectors, both.shape[1])], axis=0)


def table_of(lines):
    line = lax.broadcasted_iota(jnp.int32, (BLOCKS, 16 * BLOCKS), 0) * 16
    pick = line == lax.broadcasted_iota(jnp.int32, (BLOCKS, 16 * BLOCKS), 1)
    return dot(pick.astype(f32).astype(bf16), lines)


def spread(table, at, size):
    count = table.shape[0]
    padded = size + -size % TILE
    block = table[:, at : at + padded].astype(bf16)
    col = lax.broadcasted_iota(jnp.int32, (1, count * size), 1)
    owner = col // size
    place = lax.broadcasted_iota(jnp.int32, (padded, count * size), 0) == col - owner * size
    value = dot(block, place.astype(f32).astype(bf16))
    keep = lax.broadcasted_iota(jnp.int32, value.shape, 0) == owner
    return jnp.sum(jnp.where(keep, value, 0.0), axis=0, keepdims=True), at + padded


def qkv_kernel(meta, size, index_ref, tok_ref, *rest):
    pieces, rest = rest[: len(meta)], rest[len(meta) :]
    qkv_ref, w_ref, small_ref, bias_ref, sems, small_sems = rest
    width = tok_ref.shape[1]
    rows = width // BLOCKS
    part = pl.program_id(0)
    index = index_ref[0]

    def weights(number):
        cols = columns(number, width)
        return copies_of(meta, rows, pieces, w_ref, sems.at[number], index, cols, cols)

    @pl.when(part == 0)
    def _():
        here = slice(0, small_ref.shape[1])
        small = copies_of(meta, 16, pieces, small_ref, small_sems, index, here, None, rows)
        start_all(small)
        for number in range(3):
            start_all(weights(number))
        wait_all(small)
        bias, _ = spread(table_of(small_ref[...]), 0, size)
        bias_ref[0] = bias[:, :width]
        bias_ref[1] = jnp.zeros((1, width), f32)
        bias_ref[2] = bias[:, width:]

    wait_all(weights(part))
    scale = jnp.where(part == 0, 1.0 / math.sqrt(width // HEADS), 1.0)
    value = dot(tok_ref[...], w_ref[:, columns(part, width)]) + bias_ref[part]
    qkv_ref[...] = (value * scale).astype(bf16)


def project_qkv(index, tokens, pieces, size):
    count, width = tokens.shape
    meta = meta_of(pieces)
    out = pl.BlockSpec((count, width), lambda i, s: (0, i))
    return call(
        functools.partial(qkv_kernel, meta, size),
        (3,),
        [whole((count, width))] + [ANY] * len(meta),
        [out],
        [shaped((count, 3 * width), bf16)],
        [
            pltpu.VMEM((width, 3 * width), bf16),
            pltpu.VMEM((16 * BLOCKS, size + -size % TILE), bf16),
            pltpu.VMEM((3, 1, width), f32),
            pltpu.SemaphoreType.DMA((3, len(meta))),
            pltpu.SemaphoreType.DMA((len(meta),)),
        ],
        count * width * width * 6,
        count * width * 8 + width * width * 6,
        near=(-1,),
    )(index, tokens, *arrays_of(pieces))


def attend_kernel(index_ref, qkv_ref, seg_ref, *rest):
    ctx_ref, lse_ref, vt_ref, ct_ref, mask_ref = rest[-5:]
    length, width = ctx_ref.shape
    pairs = HEADS // 2
    lanes = width // pairs
    half = lanes // 2
    fill_mask(seg_ref[0].astype(f32), mask_ref)
    vt_ref[...] = qkv_ref[:, 2 * width :].T

    tiles = [(pair, band) for pair in range(pairs) for band in bands(length)]

    def scores_of(tile):
        pair, (lo, hi, at) = tile
        queries = two_heads(qkv_ref[at : at + TILE, pair * lanes : (pair + 1) * lanes])
        keys = qkv_ref[lo:hi, width + pair * lanes : width + (pair + 1) * lanes]
        return dot_nt(keys, queries)

    def probs_of(tile, scores):
        pair, (lo, hi, at) = tile
        scores = scores + twice(mask_ref[lo:hi, at : at + TILE])
        top = jnp.max(scores, axis=0, keepdims=True)
        terms = jnp.exp(scores - top)
        total = jnp.sum(terms, axis=0, keepdims=True)
        lse = top + jnp.log(total)
        for head in range(2):
            lse_ref[0, pair, head : head + 1, at : at + TILE] = lse[:, head * TILE : (head + 1) * TILE]
        return (terms * (1.0 / total)).astype(bf16)

    def put_context(tile, probs):
        pair, (lo, hi, at) = tile
        context = dot(vt_ref[pair * lanes : (pair + 1) * lanes, lo:hi], probs)
        for head in range(2):
            rows = slice(pair * lanes + head * half, pair * lanes + (head + 1) * half)
            part = context[head * half : (head + 1) * half, head * TILE : (head + 1) * TILE]
            ct_ref[rows, at : at + TILE] = part.astype(bf16)

    ready = {}
    probs = {}
    for step in range(len(tiles) + 2):
        if step < len(tiles):
            ready[step] = scores_of(tiles[step])
        if 0 <= step - 1 < len(tiles):
            probs[step - 1] = probs_of(tiles[step - 1], ready.pop(step - 1))
        if 0 <= step - 2:
            put_context(tiles[step - 2], probs.pop(step - 2))
    ctx_ref[...] = ct_ref[...].T


def attend(index, qkv, seg_rows, row, before=(), after=()):
    count, width = qkv.shape[0], qkv.shape[1] // 3
    rows, _, length = seg_rows.shape
    pairs = HEADS // 2
    return call(
        attend_kernel,
        (1,),
        [
            pl.BlockSpec((length, 3 * width), lambda i, s: (row, 0)),
            pl.BlockSpec((1, 1, length), lambda i, s: (row, 0, 0)),
        ]
        + [ANY] * len(before),
        [
            pl.BlockSpec((length, width), lambda i, s: (row, 0)),
            pl.BlockSpec((1, pairs, 2, length), lambda i, s: (row, 0, 0, 0)),
        ],
        [
            shaped((count, width), bf16),
            shaped((rows, pairs, 2, length), f32),
        ],
        [
            pltpu.VMEM((width, length), bf16),
            pltpu.VMEM((width, length), bf16),
            pltpu.VMEM((length, length), f32),
        ],
        length * length * width * 4,
        length * width * 8,
        length * length * HEADS * 5 // 8,
        after,
        {3 + i: i for i in range(len(before))},
        (1, -1, -2) + ((3, 4) if before else ()),
    )(index, qkv, seg_rows, *before)


def row_stats(values):
    mean = jnp.mean(values, axis=-1, keepdims=True)
    centred = values - mean
    spread = jnp.mean(centred * centred, axis=-1, keepdims=True)
    return centred, lax.rsqrt(spread + norm_eps)


def project_kernel(meta, sizes, index_ref, ctx_ref, tok_ref, *rest):
    pieces, rest = rest[: len(meta)], rest[len(meta) :]
    norm_ref, root_ref, hid_ref, vec_ref, up_ref, w_ref, small_ref, sems, small_sems = rest
    width = w_ref.shape[0]

    @pl.when(pl.program_id(0) == 0)
    def _():
        rows = width // BLOCKS
        here = slice(0, width)
        copies = copies_of(meta, rows, pieces, w_ref, sems, index_ref[0], here, here)
        line = slice(0, small_ref.shape[1])
        small = copies_of(meta, 16, pieces, small_ref, small_sems, index_ref[0], line, None, rows)
        start_all(small)
        start_all(copies)
        vec_ref[...] = jnp.zeros_like(vec_ref)
        wait_all(small)
        table = table_of(small_ref[...])
        line, at = 0, 0
        for size in sizes:
            value, at = spread(table, at, size)
            if value.shape[1] == width:
                vec_ref[line : line + 1] = value
                line += 1
            else:
                up_ref[...] = value
        wait_all(copies)

    def finish(here, product):
        summed = tok_ref[here].astype(f32) + (product + vec_ref[0:1])
        centred, root = row_stats(summed)
        normed = centred * root
        norm_ref[here] = normed
        root_ref[here] = root
        hid_ref[here] = (normed * vec_ref[1:2] + vec_ref[2:3]).astype(bf16)

    in_turn(ctx_ref.shape[0], lambda here: dot(ctx_ref[here], w_ref[...]), finish)


def in_turn(count, begin, finish, size=2 * TILE):
    last = None
    for at in range(0, count, size):
        here = slice(at, at + size)
        value = begin(here)
        if last is not None:
            finish(*last)
        last = (here, value)
    finish(*last)


def project(index, context, tokens, pieces, sizes, after=(), step=512):
    count, width = tokens.shape
    inner = 4 * width
    used = sum(size + -size % TILE for size in sizes)
    meta = meta_of(pieces)
    rows = pl.BlockSpec((step, width), lambda i, s: (i, 0))
    return call(
        functools.partial(project_kernel, meta, sizes),
        (count // step,),
        [rows, rows] + [ANY] * len(meta),
        [
            rows,
            pl.BlockSpec((step, 1), lambda i, s: (i, 0)),
            rows,
            whole((SEGS, width)),
            whole((1, inner)),
        ],
        [
            shaped((count, width), f32),
            shaped((count, 1), f32),
            shaped((count, width), bf16),
            shaped((SEGS, width), f32),
            shaped((1, inner), f32),
        ],
        [
            pltpu.VMEM((width, width), bf16),
            pltpu.VMEM((16 * BLOCKS, used), bf16),
            pltpu.SemaphoreType.DMA((len(meta),)),
            pltpu.SemaphoreType.DMA((len(meta),)),
        ],
        count * width * width * 2,
        count * width * 10 + width * width * 2,
        0,
        after,
        near=(1, -3, -4, -5),
    )(index, context, tokens, *arrays_of(pieces))


def gelu_parts(value):
    share = 0.5 * lax.erf(value * math.sqrt(0.5)) + 0.5
    bell = jnp.exp2(value * value * (-0.5 / math.log(2.0)))
    return value * share, share + value * bell * (1.0 / math.sqrt(2.0 * math.pi))


def up_kernel(meta, index_ref, hid_ref, bias_ref, *rest):
    pieces, rest = rest[: len(meta)], rest[len(meta) :]
    act_ref, slope_ref, w_ref, sems = rest
    tile = act_ref.shape[1]
    width = w_ref.shape[0]
    step = pl.program_id(0)

    def weights(number):
        source, place = columns(number, tile, width), columns(number, tile)
        rows = width // BLOCKS
        return copies_of(meta, rows, pieces, w_ref, sems.at[number], index_ref[0], source, place)

    @pl.when(step == 0)
    def _():
        for number in range(sems.shape[0]):
            start_all(weights(number))

    wait_all(weights(step))
    wide = 256

    def begin(cols):
        here = pl.ds(pl.multiple_of(step * tile + cols.start, wide), wide)
        return dot(hid_ref[...], w_ref[:, here]) + bias_ref[:, cols]

    def finish(cols, value):
        act, slope = gelu_parts(value)
        act_ref[:, cols] = act.astype(bf16)
        slope_ref[:, cols] = slope.astype(bf16)

    in_turn(tile, begin, finish, wide)


def up(index, hidden, bias, pieces, after=(), tile=768):
    count, width = hidden.shape
    inner = bias.shape[1]
    meta = meta_of(pieces)
    out = pl.BlockSpec((count, tile), lambda i, s: (0, i))
    return call(
        functools.partial(up_kernel, meta),
        (inner // tile,),
        [HELD, pl.BlockSpec((1, tile), lambda i, s: (0, i))] + [ANY] * len(meta),
        [out, out],
        [shaped((count, inner), bf16)] * 2,
        [
            pltpu.VMEM((width, inner), bf16),
            pltpu.SemaphoreType.DMA((inner // tile, len(meta))),
        ],
        count * width * inner * 2,
        count * (width * 2 + inner * 4) + width * inner * 2,
        count * inner * 4,
        after,
        near=(1, 2),
    )(index, hidden, bias, *arrays_of(pieces))


def down_kernel(meta, index_ref, act_ref, norm_ref, vec_ref, seg_ref, pos_ref, *rest):
    pieces, rest = rest[: len(meta)], rest[len(meta) :]
    res_ref, norm2_ref, root_ref, pay_ref, pool_ref, stat_ref, *rest = rest
    w_ref, held_ref, sum_ref, num_ref, sems, act_sems = rest
    step, steps = pl.program_id(0), pl.num_programs(0)
    length, width = res_ref.shape
    tile = w_ref.shape[0] // 4
    index = index_ref[0]

    def weights(chip):
        return pair_copies(meta, tile // 2, pieces, w_ref, sems, index, chip)

    def inputs(row, chip):
        rows = pl.ds(pl.multiple_of(row * length, length), length)
        source = act_ref.at[rows, columns((index // 2) ^ chip, tile)]
        return pltpu.make_async_copy(source, held_ref.at[row, chip], act_sems.at[row, chip])

    @pl.when(step == 0)
    def _():
        inputs(0, 0).start()
        start_all(weights(0))

    wanted = lax.broadcasted_iota(jnp.int32, (SEGS, length), 0)
    member = (wanted == seg_ref[0]).astype(f32)
    product = None
    for chip in range(4):
        inputs(step, chip).wait()

        @pl.when(step == 0)
        def _():
            wait_all(weights(chip))
            if chip < 3:
                inputs(0, chip + 1).start()
                start_all(weights(chip + 1))
            else:
                for other in range(4):
                    inputs(1, other).start()

        value = dot(held_ref[step, chip], w_ref[columns((index // 2) ^ chip, tile)])
        product = value if product is None else product + value
    hidden = norm_ref[...] * vec_ref[1:2] + vec_ref[2:3]
    summed = hidden + (product + vec_ref[3:4])
    centred, root = row_stats(summed)
    normed = centred * root
    result = normed * vec_ref[4:5] + vec_ref[5:6]
    norm2_ref[...] = normed
    root_ref[...] = root
    high = result.astype(bf16)
    res_ref[...] = high
    low = (result - high.astype(f32)).astype(bf16)
    own = pl.ds(pl.multiple_of(step * SEGS, SEGS), SEGS)
    member_b = member.astype(bf16)
    sum_ref[own] = dot(member_b, high) + dot(member_b, low)
    num_ref[own] = jnp.broadcast_to(jnp.sum(member, axis=1, keepdims=True), (SEGS, TAIL))

    @pl.when(step == steps - 1)
    def _():
        counts = num_ref[:, 0:1]
        pooled = sum_ref[...] / counts
        scale = lax.rsqrt(jnp.mean(pooled * pooled, axis=-1, keepdims=True) + pool_eps)
        pool_ref[...] = pooled
        lane = lax.broadcasted_iota(jnp.int32, (pooled.shape[0], TAIL), 1)
        stat_ref[...] = jnp.where(lane == 0, scale, counts)
        pay_ref[:, :width] = (pooled * scale).astype(bf16)
        partner = pos_ref[...]
        digit = jnp.where(lane == 0, partner // BASE, partner % BASE)
        pay_ref[:, width:] = jnp.where(lane < 2, digit, 0).astype(f32).astype(bf16)


def down(index, activated, normed, vectors, seg_rows, positive, pieces, after=()):
    count, width = normed.shape
    inner = activated.shape[1]
    rows, _, step = seg_rows.shape
    own = rows * SEGS
    meta = meta_of(pieces)
    block = pl.BlockSpec((step, width), lambda i, s: (i, 0))
    return call(
        functools.partial(down_kernel, meta),
        (count // step,),
        [
            ANY,
            block,
            whole(vectors.shape),
            pl.BlockSpec((1, 1, step), lambda i, s: (i, 0, 0)),
            whole((own, 1)),
        ]
        + [ANY] * len(meta),
        [
            block,
            block,
            pl.BlockSpec((step, 1), lambda i, s: (i, 0)),
            whole((own, width + TAIL)),
            whole((own, width)),
            whole((own, TAIL)),
        ],
        [
            shaped((count, width), bf16),
            shaped((count, width), f32),
            shaped((count, 1), f32),
            shaped((own, width + TAIL), bf16),
            shaped((own, width), f32),
            shaped((own, TAIL), f32),
        ],
        [
            pltpu.VMEM((inner, width), bf16),
            pltpu.VMEM((rows, 4, step, inner // 4), bf16),
            pltpu.VMEM((own, width), f32),
            pltpu.VMEM((own, TAIL), f32),
            pltpu.SemaphoreType.DMA((len(meta),)),
            pltpu.SemaphoreType.DMA((rows, 4)),
        ],
        count * width * inner * 2,
        count * (width * 10 + inner * 2) + width * inner * 2,
        after=after,
        near=(3, 5, -4, -5, -6),
    )(index, activated, normed, vectors, seg_rows, positive, *arrays_of(pieces))


def segment_of(row, own, cores, chips, planes):
    block = row // own
    plane, chip, core = block % planes, block // planes % chips, block // (planes * chips)
    return ((plane * chips + chip) * cores + core) * own + row % own


def contrast_kernel(layout, place_ref, own_ref, pos_ref, pool_ref, stat_ref, *rest):
    pieces, (loss_ref, grad_ref, all_ref, sems) = rest[:-4], rest[-4:]
    copies, at = [], 0
    for number, piece in enumerate(pieces):
        here = all_ref.at[at : at + piece.shape[0]]
        copies.append(pltpu.make_async_copy(piece, here, sems.at[number]))
        at += piece.shape[0]
    for copy in copies:
        copy.start()
    for copy in copies:
        copy.wait()
    total = all_ref.shape[0]
    own, width = pool_ref.shape
    factor = score_scale / width
    block = min(total, 512)
    flip, first = place_ref[0], place_ref[1]
    mine = own_ref[:, :width]
    mine_id = lax.broadcasted_iota(jnp.int32, (own, total), 0) + first
    other_id = segment_of(lax.broadcasted_iota(jnp.int32, (1, total), 1), own, *layout) ^ flip
    logits = dot_nt(mine, all_ref[:, :width]) * factor
    logits = jnp.where(mine_id == other_id, masked_value, logits)
    top = jnp.max(logits, axis=1, keepdims=True)
    log_own = top + jnp.log(jnp.sum(jnp.exp(logits - top), axis=1, keepdims=True))
    is_positive = other_id == pos_ref[...]
    picked = jnp.sum(jnp.where(is_positive, logits, 0.0), axis=1, keepdims=True)
    loss_ref[...] = log_own - picked
    d_logits = pair_weight * (jnp.exp(logits - log_own) - is_positive.astype(f32))
    d_emb = dot(d_logits.astype(bf16), all_ref[:, :width])
    lane = lax.broadcasted_iota(jnp.int32, (SEGS, TAIL), 1)
    digits = jnp.where(lane == 0, float(BASE), jnp.where(lane == 1, 1.0, 0.0)).astype(bf16)
    for at in range(0, total, block):
        rows = slice(at, at + block)
        table = dot_nt(all_ref[:, :width], all_ref[rows, :width]) * factor
        left = lax.broadcasted_iota(jnp.int32, (total, block), 0)
        right = lax.broadcasted_iota(jnp.int32, (total, block), 1) + at
        table = jnp.where(left == right, masked_value, table)
        top = jnp.max(table, axis=0, keepdims=True)
        log_all = top + jnp.log(jnp.sum(jnp.exp(table - top), axis=0, keepdims=True))
        partner = dot_nt(digits, all_ref[rows, width:])[0:1].astype(jnp.int32)
        chosen = partner == mine_id[:, rows]
        back = pair_weight * (jnp.exp(logits[:, rows] - log_all) - chosen.astype(f32))
        d_emb += dot(back.astype(bf16), all_ref[rows, :width])
    d_emb = d_emb * factor
    scale, counts = stat_ref[:, 0:1], stat_ref[:, 1:2]
    pooled = pool_ref[...]
    along = jnp.mean(d_emb * pooled, axis=-1, keepdims=True)
    grad_ref[...] = (d_emb * scale - pooled * (scale * scale * scale * along)) / counts


def contrast(place, layout, everyone, payload, positive, pooled, stats, after=()):
    own, width = pooled.shape
    total = sum(v.shape[0] for v in everyone)
    return call(
        functools.partial(contrast_kernel, layout),
        (1,),
        [whole(v.shape) for v in (payload, positive, pooled, stats)] + [ANY] * len(everyone),
        [whole((own, 1)), whole((own, width))],
        [shaped((own, 1), f32), shaped((own, width), f32)],
        [
            pltpu.VMEM((total, width + TAIL), bf16),
            pltpu.SemaphoreType.DMA((len(everyone),)),
        ],
        total * total * width * 2,
        total * width * 2,
        total * total,
        after=after,
        near=(1, 2, 3, 4, -1, -2),
    )(place, payload, positive, pooled, stats, *everyone)


def norm_back(d_out, normed, root, gain):
    scaled = d_out * gain
    mean = jnp.mean(scaled, axis=-1, keepdims=True)
    along = jnp.mean(scaled * normed, axis=-1, keepdims=True)
    return root * (scaled - mean - normed * along)


def column_sum(values):
    return jnp.sum(values, axis=0, keepdims=True)


def norm2_kernel(turns, index_ref, og_ref, norm_ref, root_ref, seg_ref, vec_in_ref, dp_ref, *rest):
    act_ref, dsum_ref, ddown_ref, vec_ref, keep_ref, send_ref, dt_ref = rest
    step = pl.program_id(0)
    chunk, width = og_ref.shape
    own = dp_ref.shape[0]

    @pl.when(step == 0)
    def _():
        vec_ref[...] = jnp.zeros_like(vec_ref)

    @pl.when(step < turns)
    def _():
        row = step // (turns * SEGS // own)
        pool = dp_ref[pl.ds(pl.multiple_of(row * SEGS, SEGS), SEGS)]
        high = pool.astype(bf16)
        left = pool - high.astype(f32)
        mid = left.astype(bf16)
        low = (left - mid.astype(f32)).astype(bf16)
        pad = jnp.zeros((TILE - 3 * SEGS, width), bf16)
        table = jnp.concatenate([high, mid, low, pad], axis=0)
        lane = lax.broadcasted_iota(jnp.int32, (chunk, TILE), 1) % SEGS
        keys = jnp.broadcast_to(seg_ref[0].astype(f32), (TILE, chunk)).T
        member = (lane.astype(f32) == keys).astype(f32).astype(bf16)

        def begin(here):
            return dot(member[here], table)

        def finish(here, shared):
            d_res = og_ref[here].astype(f32) + shared
            normed = norm_ref[here]
            d_sum = norm_back(d_res, normed, root_ref[here], vec_in_ref[4:5])
            d_down = d_sum.astype(bf16)
            dsum_ref[here] = d_sum
            ddown_ref[here] = d_down
            cols = pl.ds(pl.multiple_of(step * chunk + here.start, TILE), TILE)
            dt_ref[:, cols] = d_down.T
            vec_ref[0:1] += column_sum(d_down.astype(f32))
            vec_ref[1:2] += column_sum(d_res * normed)
            vec_ref[2:3] += column_sum(d_res)

        in_turn(chunk, begin, finish, TILE)

    @pl.when(step >= turns)
    def _():
        grad = dot(dt_ref[...], act_ref[...]).astype(bf16)
        half = grad.shape[1] // 2
        odd = index_ref[0] % 2 == 1
        keep_ref[0] = jnp.where(odd, grad[:, half:], grad[:, :half])
        send_ref[0] = jnp.where(odd, grad[:, :half], grad[:, half:])


def norm2(index, out_grad, normed, root, seg_rows, vectors, d_pool, activated, turns=4):
    count, width = out_grad.shape
    inner = activated.shape[1]
    tile = inner // 4
    own = d_pool.shape[0]
    first = lambda i: jnp.minimum(i, turns - 1)
    then = lambda i: jnp.maximum(i - turns, 0)
    split = turns // seg_rows.shape[0]
    block = pl.BlockSpec((count // turns, width), lambda i, s: (first(i), 0))
    column = pl.BlockSpec((count // turns, 1), lambda i, s: (first(i), 0))
    grads = pl.BlockSpec((1, width, tile // 2), lambda i, s: (then(i), 0, 0))
    return call(
        functools.partial(norm2_kernel, turns),
        (turns + 4,),
        [
            block,
            block,
            column,
            pl.BlockSpec((1, 1, count // turns), lambda i, s: (first(i) // split, 0, first(i) % split)),
            whole(vectors.shape),
            whole((own, width)),
            pl.BlockSpec((count, tile), lambda i, s: (0, (s[0] // 2) ^ then(i))),
        ],
        [block, block, whole((SEGS, width)), grads, grads],
        [
            shaped((count, width), f32),
            shaped((count, width), bf16),
            shaped((SEGS, width), f32),
            shaped((4, width, tile // 2), bf16),
            shaped((4, width, tile // 2), bf16),
        ],
        [pltpu.VMEM((width, count), bf16)],
        count * width * inner * 2,
        count * (width * 12 + inner * 2) + width * inner * 2,
        near=(5, 6, -1, -2, -3, -4, -5),
    )(index, out_grad, normed, root, seg_rows, vectors, d_pool, activated)


def put_turned(source_ref, target_ref, turn_ref, index):
    turn_ref[...] = source_ref[...].T
    rows = turn_ref.shape[0] // BLOCKS
    for place in range(BLOCKS):
        block = index ^ ((place % 4) * 2 + place // 4)
        start = pl.multiple_of(block * rows, 16)
        target_ref[place * rows : (place + 1) * rows] = turn_ref[pl.ds(start, rows)]


def weights_kernel(down_meta, up_meta, index_ref, *refs):
    pieces, (wd_ref, wu_ref, sems, up_sems) = refs[:-4], refs[-4:]
    low, high = pieces[: len(down_meta)], pieces[len(down_meta) :]
    width, inner = wu_ref.shape
    here = slice(width, width + inner)
    copies = copies_of(down_meta, inner // BLOCKS, low, wd_ref, sems, index_ref[0])
    copies += copies_of(up_meta, width // BLOCKS, high, wu_ref, up_sems, index_ref[0], here)
    start_all(copies)
    wait_all(copies)


def hold_weights(index, down_pieces, up_pieces, width, inner, after=()):
    down_meta, up_meta = meta_of(down_pieces), meta_of(up_pieces)
    return call(
        functools.partial(weights_kernel, down_meta, up_meta),
        (1,),
        [ANY] * (len(down_meta) + len(up_meta)),
        [HELD, HELD],
        [shaped((inner, width), bf16), shaped((width, inner), bf16)],
        [
            pltpu.SemaphoreType.DMA((len(down_meta),)),
            pltpu.SemaphoreType.DMA((len(up_meta),)),
        ],
        0,
        width * inner * 8,
        0,
        after,
        near=(-1, -2),
    )(index, *arrays_of(down_pieces), *arrays_of(up_pieces))


def turned_kernel(index_ref, one_ref, two_ref, out_one_ref, out_two_ref, turn_ref):
    put_turned(one_ref, out_one_ref, turn_ref, index_ref[0])
    put_turned(two_ref, out_two_ref, turn_ref, index_ref[0])


def hold_turned(index, one, two, after=()):
    count, width = one.shape
    return call(
        turned_kernel,
        (1,),
        [whole((count, width))] * 2,
        [HELD, HELD],
        [shaped((width, count), bf16)] * 2,
        [pltpu.VMEM((width, count), bf16)],
        0,
        count * width * 8,
        0,
        after,
        near=(-1, -2),
    )(index, one, two)


def up_back_kernel(first, before, index_ref, ddown_ref, slope_ref, ht_ref, wd_ref, wu_ref, *rest):
    earlier, rest = rest[:before], rest[before:]
    dhid_ref, bias_ref, keep_ref, send_ref = rest
    step = pl.program_id(0)
    tile = slope_ref.shape[1]
    width = ht_ref.shape[0]
    here = columns((index_ref[0] // 2) ^ (step + first), tile)
    wide = 256
    parts = []

    def begin(cols):
        rows = pl.ds(pl.multiple_of(here.start + cols.start, wide), wide)
        return dot_nt(ddown_ref[...], wd_ref[rows])

    def finish(cols, d_act):
        d_up = (d_act * slope_ref[:, cols].astype(f32)).astype(bf16)
        bias_ref[:, cols] = column_sum(d_up.astype(f32))
        parts.append(d_up)

    in_turn(tile, begin, finish, wide)
    d_up = jnp.concatenate(parts, axis=1)
    grad = dot(ht_ref[...], d_up).astype(bf16)
    half = width // 2
    keep_ref[...] = grad[:half].reshape(keep_ref.shape)
    send_ref[...] = grad[half:].reshape(send_ref.shape)
    share = dot_nt(d_up, wu_ref[:, here])

    @pl.when(step == 0)
    def _():
        dhid_ref[...] = earlier[0][...] + share if earlier else share

    @pl.when(step > 0)
    def _():
        dhid_ref[...] += share


def up_back(index, d_down, slope, turned, w_down, w_up, first, steps, before=(), after=()):
    count, width = d_down.shape
    inner = slope.shape[1]
    tile = inner // 4
    part = width // BLOCKS
    place = lambda i, s: (s[0] // 2) ^ (i + first)
    grads = pl.BlockSpec((4, part, tile), lambda i, s: (0, 0, place(i, s)))
    return call(
        functools.partial(up_back_kernel, first, len(before)),
        (steps,),
        [HELD, pl.BlockSpec((count, tile), lambda i, s: (0, place(i, s))), HELD, HELD, HELD]
        + ([HELD] + [ANY] * 3 if before else []),
        [HELD, pl.BlockSpec((1, tile), lambda i, s: (0, place(i, s))), grads, grads],
        [
            shaped((count, width), f32),
            shaped((1, inner), f32),
            shaped((4, part, inner), bf16),
            shaped((4, part, inner), bf16),
        ],
        [],
        count * width * tile * 6 * steps,
        count * (width * 8 + inner) + width * inner * 6,
        0,
        after,
        {6 + i: i for i in range(len(before))},
        (1, 3, 4, 5, 6, 7, 8, 9, -1, -2, -3, -4),
    )(index, d_down, slope, turned, w_down, w_up, *before)


def cut_vector(vector, size, index):
    width = vector.shape[1]
    owner = lax.broadcasted_iota(jnp.int32, (BLOCKS, width), 1) // size
    wanted = lax.broadcasted_iota(jnp.int32, (BLOCKS, width), 0) ^ index
    rows = jnp.where(owner == wanted, vector, 0.0).astype(bf16)
    source = lax.broadcasted_iota(jnp.int32, (width, 1), 0)
    place = source - source // size * size == lax.broadcasted_iota(jnp.int32, (width, TILE), 1)
    return dot(rows, place.astype(f32).astype(bf16))


def norm1_kernel(meta, parts, index_ref, *rest):
    dhids, rest = rest[:parts], rest[parts:]
    dsum_ref, norm_ref, root_ref, gain_ref, ctx_ref, other_ref, up_ref, *rest = rest
    pieces, rest = rest[: len(meta)], rest[len(meta) :]
    dattn_ref, dctx_ref, keep_ref, send_ref, w_ref, acc_ref, vec_ref, sems = rest
    step = pl.program_id(0)
    width = w_ref.shape[0]
    rows = width // BLOCKS

    @pl.when(step == 0)
    def _():
        here = slice(0, width)
        copies = copies_of(meta, rows, pieces, w_ref, sems, index_ref[0], here, here)
        start_all(copies)
        vec_ref[...] = jnp.zeros_like(vec_ref)
        acc_ref[...] = jnp.zeros_like(acc_ref)
        wait_all(copies)

    parts = []

    def begin(here):
        d_hid = dsum_ref[here]
        for dhid_ref in dhids:
            d_hid = d_hid + dhid_ref[here]
        normed = norm_ref[here]
        d_sum = norm_back(d_hid, normed, root_ref[here], gain_ref[1:2])
        d_attn = d_sum.astype(bf16)
        dattn_ref[here] = d_sum
        vec_ref[0:1] += column_sum(d_attn.astype(f32))
        vec_ref[1:2] += column_sum(d_hid * normed)
        vec_ref[2:3] += column_sum(d_hid)
        parts.append(d_attn)
        return d_attn

    def finish(here, d_attn):
        dctx_ref[here] = dot_nt(d_attn, w_ref[...]).astype(bf16)

    in_turn(dsum_ref.shape[0], begin, finish)
    acc_ref[...] += dot(ctx_ref[...].T, jnp.concatenate(parts, axis=0))

    @pl.when(step == pl.num_programs(0) - 1)
    def _():
        index = index_ref[0]
        vectors = [vec_ref[i : i + 1] for i in range(3)] + [other_ref[i : i + 1] for i in range(3)]
        top = [cut_vector(vector, rows, index) for vector in vectors]
        top = jnp.concatenate(top, axis=1)
        size = up_ref.shape[1] // BLOCKS
        line = lax.broadcasted_iota(jnp.int32, (16, width), 0)
        pad = jnp.zeros((1, width - size), f32)
        for place in range(4):
            for target, core in ((keep_ref, 0), (send_ref, 1)):
                number = 2 * place + core
                block = index ^ number
                start = pl.multiple_of(block * rows, 16)
                target[place, :rows] = acc_ref[pl.ds(start, rows)].astype(bf16)
                low = up_ref[:, pl.ds(pl.multiple_of(block * size, size), size)]
                low = jnp.concatenate([low, pad], axis=1)
                extra = jnp.where(line == 0, top[number : number + 1], 0.0)
                extra = jnp.where(line == 1, low, extra)
                target[place, rows:] = extra.astype(bf16)


def norm1(
    index, d_hiddens, d_summed, normed, root, gain, context, sums, sums_up, pieces, after=(), step=512
):
    count, width = d_summed.shape
    meta = meta_of(pieces)
    part = width // BLOCKS + 16
    block = pl.BlockSpec((step, width), lambda i, s: (i, 0))
    return call(
        functools.partial(norm1_kernel, meta, len(d_hiddens)),
        (count // step,),
        [block] * len(d_hiddens)
        + [
            block,
            block,
            pl.BlockSpec((step, 1), lambda i, s: (i, 0)),
            whole(gain.shape),
            block,
            whole(sums.shape),
            whole(sums_up.shape),
        ]
        + [ANY] * len(meta),
        [block, block, whole((4, part, width)), whole((4, part, width))],
        [
            shaped((count, width), f32),
            shaped((count, width), bf16),
            shaped((4, part, width), bf16),
            shaped((4, part, width), bf16),
        ],
        [
            pltpu.VMEM((width, width), bf16),
            pltpu.VMEM((width, width), f32),
            pltpu.VMEM((SEGS, width), f32),
            pltpu.SemaphoreType.DMA((len(meta),)),
        ],
        count * width * width * 4,
        count * width * 20 + width * width * 4,
        0,
        after,
        near=tuple(range(1, 2 + len(d_hiddens))) + (6, 7, 8, -1, -2, -3, -4),
    )(
        index, *d_hiddens, d_summed, normed, root, gain, context, sums, sums_up, *arrays_of(pieces)
    )


def attend_back_kernel(
    first, index_ref, q_ref, k_ref, v_ref, dctx_ref, lse_ref, seg_ref, tt_ref, *rest
):
    dq_ref, dk_ref, dv_ref, keep_ref, send_ref = rest[:5]
    mask_ref, kt_ref, two_ref, pt_ref, both_ref = rest[5:]
    rows, _, length = seg_ref.shape
    lanes = 2 * tt_ref.shape[0] // HEADS
    half = lanes // 2
    group = q_ref.shape[1] // lanes
    inv_root = 1.0 / math.sqrt(half)

    @pl.when(pl.program_id(0) == 0)
    def _():
        for row in range(rows):
            fill_mask(seg_ref[row].astype(f32), mask_ref.at[row])

    tiles = [
        (pair, row, band) for pair in range(group) for row in range(rows) for band in bands(length)
    ]
    for pair in range(group):
        for row in range(rows):
            here = slice(row * length, (row + 1) * length)
            kt_ref[pair, row] = k_ref[here, pair * lanes : (pair + 1) * lanes].T

    def begin(tile):
        pair, row, (lo, hi, at) = tile
        cols = slice(pair * lanes, (pair + 1) * lanes)
        base = row * length
        queries = two_heads(q_ref[base + at : base + at + TILE, cols])
        d_context = two_heads(dctx_ref[base + at : base + at + TILE, cols])
        two_ref[0, pair, row, 2 * at : 2 * at + 2 * TILE] = queries
        two_ref[1, pair, row, 2 * at : 2 * at + 2 * TILE] = d_context
        scores = dot_nt(k_ref[base + lo : base + hi, cols], queries)
        return scores, dot_nt(v_ref[base + lo : base + hi, cols], d_context)

    def middle_part(tile, scores, d_probs):
        pair, row, (lo, hi, at) = tile
        lse = jnp.concatenate(
            [lse_ref[row, pair, head : head + 1, at : at + TILE] for head in range(2)], axis=1
        )
        probs = jnp.exp(scores + twice(mask_ref[row, lo:hi, at : at + TILE]) - lse)
        inner = jnp.sum(d_probs * probs, axis=0, keepdims=True)
        d_scores = (probs * (d_probs - inner)).astype(bf16)
        pt_ref[0, pair, row, lo:hi, 2 * at : 2 * at + 2 * TILE] = d_scores
        pt_ref[1, pair, row, lo:hi, 2 * at : 2 * at + 2 * TILE] = probs.astype(bf16)
        return d_scores

    def put(tile, kind, value):
        pair, row, (_, _, at) = tile
        here = slice(row * length + at, row * length + at + TILE)
        cols = slice((3 * pair + kind) * lanes, (3 * pair + kind + 1) * lanes)
        both_ref[here, cols] = value.astype(bf16)

    def end(tile, d_scores):
        pair, row, (lo, hi, at) = tile
        dq = dot(kt_ref[pair, row, :, lo:hi], d_scores) * inv_root
        dq = jnp.concatenate([dq[:half, :TILE], dq[half:, TILE:]], axis=0)
        put(tile, 0, dq.T)

    def end_keys(tile):
        pair, row, (lo, hi, at) = tile
        cols = slice(2 * lo, 2 * hi)
        for kind in range(2):
            value = dot(
                pt_ref[kind, pair, row, at : at + TILE, cols], two_ref[kind, pair, row, cols]
            )
            put(tile, 1 + kind, value)

    ready = {}
    done = {}
    for step in range(len(tiles) + 3):
        if step < len(tiles):
            ready[step] = begin(tiles[step])
        if 0 <= step - 1 < len(tiles):
            done[step - 1] = middle_part(tiles[step - 1], *ready.pop(step - 1))
        if 0 <= step - 2 < len(tiles):
            end(tiles[step - 2], done.pop(step - 2))
        if 0 <= step - 3 < len(tiles):
            end_keys(tiles[step - 3])
    both = both_ref[...]
    for pair in range(group):
        for kind, target in enumerate((dq_ref, dk_ref, dv_ref)):
            cols = slice((3 * pair + kind) * lanes, (3 * pair + kind + 1) * lanes)
            target[:, pair * lanes : (pair + 1) * lanes] = both[:, cols]
    grad = dot(tt_ref[...], both).astype(bf16)
    width = grad.shape[0]
    part = width // BLOCKS
    span = both.shape[1]
    col = lax.broadcasted_iota(jnp.int32, (1, span), 1)
    kind = col // lanes % 3
    place = (pl.program_id(0) * group + first + col // (3 * lanes)) * lanes + col % lanes
    owner = jnp.where(kind == 1, -1, (place + jnp.where(kind == 2, width, 0)) // (2 * part))
    sums = column_sum(both.astype(f32))
    line = lax.broadcasted_iota(jnp.int32, (16, span), 0)
    for block in range(BLOCKS):
        target, core = (keep_ref, 0) if block < 4 else (send_ref, 1)
        target[block % 4, :part] = grad[block * part : (block + 1) * part]
        here = owner == (index_ref[0] ^ (2 * (block % 4) + core))
        extra = jnp.where(line == 0, jnp.where(here, sums, 0.0), 0.0)
        target[block % 4, part:] = extra.astype(bf16)


def attend_back(
    index, qkv, d_context, lse, seg_rows, turned, first, pairs, after=(), group=2
):
    width, count = turned.shape
    rows, _, length = seg_rows.shape
    every = HEADS // 2
    lanes = width // every
    part = width // BLOCKS + 16
    wide = group * lanes
    column = lambda place: pl.BlockSpec((count, wide), lambda i, s: (0, place // group + i))
    out = pl.BlockSpec((count, wide), lambda i, s: (0, i))
    grads = pl.BlockSpec((4, part, 3 * wide), lambda i, s: (0, 0, i))
    return call(
        functools.partial(attend_back_kernel, first),
        (pairs // group,),
        [
            column(first),
            column(every + first),
            column(2 * every + first),
            column(first),
            pl.BlockSpec((rows, group, 2, length), lambda i, s: (0, first // group + i, 0, 0)),
            whole((rows, 1, length)),
            HELD,
        ],
        [out, out, out, grads, grads],
        [
            shaped((count, pairs * lanes), bf16),
            shaped((count, pairs * lanes), bf16),
            shaped((count, pairs * lanes), bf16),
            shaped((4, part, pairs * 3 * lanes), bf16),
            shaped((4, part, pairs * 3 * lanes), bf16),
        ],
        [
            pltpu.VMEM((rows, length, length), f32),
            pltpu.VMEM((group, rows, lanes, length), bf16),
            pltpu.VMEM((2, group, rows, 2 * length, lanes), bf16),
            pltpu.VMEM((2, group, rows, length, 2 * length), bf16),
            pltpu.VMEM((count, 3 * wide), bf16),
        ],
        count * pairs * lanes * (width * 6 + length * 6),
        count * pairs * lanes * 14 + count * width * 2,
        count * length * pairs * 5 // 4,
        after,
        near=(4, 5, 7, -1, -2, -3, -4, -5),
    )(index, qkv, qkv, qkv, d_context, lse, seg_rows, turned)


def input_kernel(meta, parts, index_ref, dattn_ref, *rest):
    grads, rest = rest[: 3 * parts], rest[3 * parts :]
    pieces, rest = rest[: len(meta)], rest[len(meta) :]
    out_ref, w_ref, sems = rest
    width = out_ref.shape[1]
    step = width // parts
    first = pl.program_id(0) == 0

    def weights(kind):
        cols = columns(kind, width)
        rows = width // BLOCKS
        return copies_of(meta, rows, pieces, w_ref, sems.at[kind], index_ref[0], cols, cols)

    @pl.when(first)
    def _():
        for kind in range(3):
            start_all(weights(kind))

    total = dattn_ref[...]
    for kind in range(3):

        @pl.when(first)
        def _():
            wait_all(weights(kind))

        for part in range(parts):
            at = kind * width + part * step
            total += dot_nt(grads[kind * parts + part][...], w_ref[:, at : at + step])
    out_ref[...] = total


def input_grad(index, d_attn, grads, pieces, after=(), step=512):
    count, width = d_attn.shape
    meta = meta_of(pieces)
    parts = len(grads) // 3
    block = pl.BlockSpec((step, width), lambda i, s: (i, 0))
    return call(
        functools.partial(input_kernel, meta, parts),
        (count // step,),
        [block]
        + [pl.BlockSpec((step, g.shape[1]), lambda i, s: (i, 0)) for g in grads]
        + [ANY] * len(meta),
        [block],
        [shaped((count, width), f32)],
        [pltpu.VMEM((width, 3 * width), bf16), pltpu.SemaphoreType.DMA((3, len(meta)))],
        count * width * width * 6,
        count * width * 14 + width * width * 6,
        0,
        after,
        near=tuple(range(1, 2 + len(grads))),
    )(index, d_attn, *grads, *arrays_of(pieces))


def rounded(value):
    return lax.optimization_barrier(value.astype(bf16))


def add(*values):
    total = values[0].astype(f32)
    for value in values[1:]:
        total = total + value.astype(f32)
    return total


def along_z(value, pairs):
    return lax.ppermute(value, "batch", pairs)


def core_kernel(parts, index_ref, *refs):
    keeps, others = refs[:parts], refs[parts : 2 * parts]
    mine_ref, x_ref, y_ref, top_ref, low_ref = refs[2 * parts :]
    half = top_ref.shape[0]
    at = 0
    for keep, other in zip(keeps, others):
        cols = slice(at, at + keep.shape[2])
        at = cols.stop
        for place, target in enumerate((mine_ref, x_ref, y_ref)):
            target[:, cols] = add(keep[place], other[place]).astype(bf16)
        far = add(keep[3], other[3]).astype(bf16)
        top_ref[:, cols] = far[:half]
        low_ref[:, cols] = far[half:]


def add_cores(index, keeps, others):
    rows = keeps[0].shape[1]
    width = sum(keep.shape[2] for keep in keeps)
    half = rows // 32 * 16
    heights = (rows, rows, rows, half, rows - half)
    count = 2 * len(keeps)
    return call(
        functools.partial(core_kernel, len(keeps)),
        (1,),
        [HELD] * count,
        [HELD] * 5,
        [shaped((height, width), bf16) for height in heights],
        [],
        rows * width * 4,
        rows * width * 24,
        near=tuple(range(1, 1 + count)) + (-1, -2, -3, -4, -5),
    )(index, *keeps, *others)


class Sum:
    def __init__(self, index, planes, keeps, sends, line):
        self.index, self.planes, self.keeps, self.line = index, planes, keeps, line
        self.arrived = [fsdp_swap(send, 1) for send in sends]
        self.stages = [self.over_core, self.over_far, self.over_chips, self.over_z, self.over_middle]

    def next(self, clock):
        *self.arrived, _ = lax.optimization_barrier((*self.arrived, clock))
        return list(self.stages.pop(0)(*self.arrived))

    def over_core(self, *others):
        *self.blocks, _ = add_cores(self.index, self.keeps, others)
        self.half = self.blocks[3].shape[0]
        self.arrived = [fsdp_swap(self.blocks[3], 2), fsdp_swap(self.blocks[4], 4)]
        return self.blocks[3:]

    def over_far(self, top, low):
        _, over_x, over_y, _, _ = self.blocks
        half = self.half
        over_x = over_x.at[half:].set(add(over_x[half:], low).astype(bf16))
        over_y = over_y.at[:half].set(add(over_y[:half], top).astype(bf16))
        self.arrived = [fsdp_swap(over_x, 2), fsdp_swap(over_y, 4)]
        return [over_x, over_y]

    def over_chips(self, from_x, from_y):
        self.total = rounded(add(self.blocks[0], from_x, from_y))
        pairs = [(0, 1), (3, 2)] if self.line else [(0, 1), (1, 0), (2, 3), (3, 2)]
        self.arrived = [along_z(self.total, pairs)]
        return [self.total]

    def over_z(self, other):
        self.total = rounded(add(self.total, other))
        pairs = [(1, 2), (2, 1)] if self.line else [(0, 2), (2, 0), (1, 3), (3, 1)]
        self.arrived = [along_z(self.total, pairs)]
        return [self.total]

    def over_middle(self, other):
        if self.line:
            self.total = rounded(add(self.total, other))
            self.arrived = [along_z(self.total, [(1, 0), (2, 3)])]
        return [self.total]

    def result(self):
        other = self.arrived[0]
        if not self.line:
            return add(self.total, other)
        plane = lax.axis_index("batch")
        inside = (plane == 1) | (plane == 2)
        return jnp.where(inside, self.total, other).astype(f32)


def layer(
    planes,
    ring,
    tokens,
    seg_ids,
    positive,
    out_grad,
    w_qkv,
    b_qv,
    w_out,
    b_out,
    norm1_gain,
    norm1_shift,
    w_up,
    b_up,
    w_down,
    b_down,
    norm2_gain,
    norm2_shift,
):
    paired = ring == BLOCKS and planes == 4
    row_count, row_length, width = tokens.shape
    count = row_count * row_length
    own = row_count * SEGS
    token_rows = tokens.reshape(count, width)
    seg_rows = seg_ids.reshape(row_count, 1, row_length)
    pos_col = positive.reshape(own, 1)
    fsdp = lax.axis_index("fsdp")
    me = lax.axis_index("batch") * ring + fsdp
    index = (fsdp if paired else jnp.zeros_like(fsdp)).reshape(1).astype(jnp.int32)
    tie = lax.optimization_barrier

    small = (b_out, norm1_gain, norm1_shift, b_down, norm2_gain, norm2_shift, b_up)
    sizes = [value.shape[0] * ring // BLOCKS for value in small]
    inner = sizes[-1] * BLOCKS
    if paired:
        first = pack_first(w_qkv, b_qv)
        first_xy = first_stage(first)
        *first_xy, second = tie((*first_xy, pack_second(w_out, w_up, *small)))
        first_far = second_stage(first, *first_xy)
        second, *first_far = tie((second, *first_far))
        second_xy = first_stage(second)
        qkv_pieces = both_cores(own_pieces(first, *first_xy))
        qkv_pieces += both_cores(far_pieces(first, *first_far))
    else:
        blocks = [gather_whole(value) for value in (w_qkv, b_qv, w_down, w_out, w_up, *small)]
        blocks = list(enumerate(zip(*blocks)))
        qkv_pieces = [(pack_first(*b[:2]), i, 0) for i, b in blocks]
        down_pieces = [(b[2], i, 0) for i, b in blocks]
        mid_pieces = [(pack_second(*b[3:]), i, 0) for i, b in blocks]

    qkv, clock = project_qkv(index, token_rows, qkv_pieces, 2 * width // BLOCKS)
    attended = ()
    for row in range(row_count):
        late = ()
        if paired and row == row_count - 1:
            *second_xy, third, clock = tie((*second_xy, w_down, clock))
            second_far = second_stage(second, *second_xy)
            third_xy = first_stage(third)
            late = (*second_xy, clock)
        *attended, clock = attend(index, qkv, seg_rows, row, attended, late)
    context, lse = attended
    if paired:
        mid_pieces = both_cores(own_pieces(second, *second_xy))
        *second_far, clock = tie((*second_far, clock))
        mid_pieces += both_cores(far_pieces(second, *second_far))
    normed1, root1, hidden, rows, bias_up, clock = project(
        index, context, token_rows, mid_pieces, sizes, (clock,)
    )
    late = ()
    if paired:
        *third_xy, clock = tie((*third_xy, clock))
        third_far = second_stage(w_down, *third_xy)
        late = (*third_xy, clock)
    activated, slope, clock = up(index, hidden, bias_up, mid_pieces, late)
    if paired:
        down_pieces = both_cores(own_pieces(w_down, *third_xy))
        *third_far, clock = tie((*third_far, clock))
        down_pieces += both_cores(far_pieces(w_down, *third_far))
    result, normed2, root2, payload, pooled, stats, _ = down(
        index, activated, normed1, rows, seg_rows, pos_col, down_pieces, (clock,)
    )

    hidden_turned, tokens_turned, clock = hold_turned(index, hidden, token_rows, (payload,))
    if paired:
        line = [payload] + [swap(payload, "batch", planes, bit) for bit in (1, 2, 3)]
        *line, clock = tie((*line, clock))
        line = jnp.concatenate(line, axis=0)
        plane = [line] + [fsdp_swap(line, bit) for bit in (2, 4, 6)]
        wd_full, wu_full, clock = hold_weights(
            index, down_pieces, mid_pieces, width, inner, (line, clock)
        )
        *plane, clock = tie((*plane, clock))
        plane = jnp.concatenate(plane, axis=0)
        everyone = [plane, fsdp_swap(plane, 1)]
        layout = (2, ring // 2, planes)
        flip = me * own
    else:
        wd_full, wu_full, clock = hold_weights(index, down_pieces, mid_pieces, width, inner)
        everyone = [lax.all_gather(payload, ("batch", "fsdp"), axis=0, tiled=True)]
        layout = (1, planes * ring, 1)
        flip = jnp.zeros_like(me)
    place = jnp.stack([flip, me * own]).astype(jnp.int32)
    pair_loss, d_pool, _ = contrast(
        place, layout, everyone, payload, pos_col, pooled, stats, (clock,)
    )

    def start(keeps, sends, line):
        return Sum(index, planes, keeps, sends, line) if paired else None

    def go(results, *sums):
        sent, clock = [], results[0]
        for one in sums:
            if one is not None:
                stage = one.next(clock)
                clock = stage[0]
                sent += stage
        if sent:
            results = tie((*results, *sent))[: len(results)]
        return results, tuple(sent)

    d_summed, d_down, sums2, keep_down, send_down, _ = norm2(
        index,
        out_grad.reshape(count, width),
        normed2,
        root2,
        seg_rows,
        rows,
        d_pool,
        activated,
    )
    sum_down = start([keep_down], [send_down], True)
    half, sent = (), ()
    for first in (0, 2):
        half = up_back(
            index, d_down, slope, hidden_turned, wd_full, wu_full, first, 2, tuple(half), sent
        )[:4]
        half, sent = go(half, sum_down)
    d_hidden, sums_up, keep_up, send_up = half
    sum_up = start([keep_up], [send_up], True)
    *first_norm, _ = norm1(
        index,
        [d_hidden],
        d_summed,
        normed1,
        root1,
        rows,
        context,
        sums2,
        sums_up,
        mid_pieces,
        sent,
    )
    (d_attn, d_context, keep_out, send_out), sent = go(first_norm, sum_up)
    pairs = HEADS // 2
    cuts = 3
    backs = []
    for cut in range(cuts):
        *back, _ = attend_back(
            index,
            qkv,
            d_context,
            lse,
            seg_rows,
            tokens_turned,
            cut * pairs // cuts,
            pairs // cuts,
            sent,
        )
        if cut == 0:
            back, sent = go(back, sum_down, sum_up)
            sum_left = start([keep_out, back[3]], [send_out, back[4]], True)
        if cut == 1:
            back, sent = go(back, sum_left)
        if cut == 2:
            sum_right = start([backs[1][3], back[3]], [backs[1][4], back[4]], False)
            back, sent = go(back, sum_down, sum_up, sum_left, sum_right)
        backs.append(back)
    grads = [backs[cut][kind] for kind in range(3) for cut in range(cuts)]
    grad_tokens, _ = input_grad(index, d_attn, grads, qkv_pieces, sent)

    lanes = width // pairs

    part = width // BLOCKS
    if paired:
        (grad_tokens,), sent = go((grad_tokens,), sum_right, sum_down, sum_up)
        _, sent = go(sent, sum_left)
        _, sent = go(sent, sum_right)
        _, sent = go(sent, sum_up, sum_left)
        _, sent = go(sent, sum_right, sum_left)
        go(sent, sum_right)
        grad_down, grad_up = sum_down.result().T, sum_up.result()
        left, right = sum_left.result(), sum_right.result()
        grad_out = left[:part, :width]
        grad_qkv = jnp.concatenate([left[:part, width:], right[:part]], axis=1)
        vector = jnp.concatenate([left[part, width:], right[part]])
        own_vectors = [left[part, i * TILE : i * TILE + part] for i in range(6)]
        own_vectors.append(left[part + 1, : sizes[-1]])
    else:

        def scatter(keep, send):
            full = lax.psum(jnp.stack([keep, send], axis=1).astype(f32), "batch")
            return full.reshape((BLOCKS,) + full.shape[2:])

        def own_rows(full):
            full = full.reshape((-1,) + full.shape[2:])
            return lax.psum_scatter(full, "fsdp", scatter_dimension=0, tiled=True)

        def own_values(full):
            return lax.psum_scatter(full.reshape(-1), "fsdp", scatter_dimension=0, tiled=True)

        grad_down = own_rows(scatter(keep_down, send_down).transpose(0, 2, 1))
        grad_up = own_rows(scatter(keep_up, send_up))
        left = scatter(keep_out, send_out)
        grad_out = own_rows(left[:, :part])
        own_vectors = [own_values(left[:, part, i * TILE : i * TILE + part]) for i in range(6)]
        own_vectors.append(own_values(left[:, part + 1, : sizes[-1]]))
        wide = jnp.concatenate([scatter(back[3], back[4]) for back in backs], axis=2)
        grad_qkv = own_rows(wide[:, :part])
        vector = lax.psum(jnp.sum(wide[:, part], axis=0), "fsdp")

    depth = grad_qkv.shape[0]
    grad_qkv = grad_qkv.reshape(depth, pairs, 3, lanes).transpose(0, 2, 1, 3)
    grad_qkv = grad_qkv.reshape(depth, 3 * width)
    vector = vector.reshape(pairs, 3, lanes)
    vector = jnp.concatenate([vector[:, 0].reshape(-1), vector[:, 2].reshape(-1)])
    shard = vector.shape[0] // ring
    grad_bqv = lax.dynamic_slice(vector, (fsdp * shard,), (shard,))
    grad_bout, grad_g1, grad_s1, grad_bdown, grad_g2, grad_s2, grad_bup = own_vectors
    return (
        result.reshape(tokens.shape),
        pair_loss.reshape(own),
        grad_tokens.reshape(tokens.shape),
        grad_qkv,
        grad_bqv,
        grad_out,
        grad_bout,
        grad_g1,
        grad_s1,
        grad_up,
        grad_bup,
        grad_down,
        grad_bdown,
        grad_g2,
        grad_s2,
    )


def solution(mesh):
    rows = P(("batch", "fsdp"), None, None)
    matrix = P("fsdp", None)
    vector = P("fsdp")
    placed = (
        rows,
        P(("batch", "fsdp"), None),
        P(("batch", "fsdp")),
        rows,
        matrix,
        vector,
        matrix,
        vector,
        vector,
        vector,
        matrix,
        vector,
        matrix,
        vector,
        vector,
        vector,
    )
    given = (
        rows,
        P(("batch", "fsdp")),
        rows,
        matrix,
        vector,
        matrix,
        vector,
        vector,
        vector,
        matrix,
        vector,
        matrix,
        vector,
        vector,
        vector,
    )
    return jax.shard_map(
        functools.partial(layer, mesh.shape["batch"], mesh.shape["fsdp"]),
        mesh=mesh,
        in_specs=placed,
        out_specs=given,
        check_vma=False,
    )
```

```python
import functools
import math

import jax
import jax.numpy as jnp
from jax import lax
from jax.experimental import pallas as pl
from jax.experimental.pallas import tpu as pltpu
from jax.sharding import PartitionSpec as P

HEADS = 12
SEGS = 8

norm_eps = 1e-06
pool_eps = 1e-06
score_scale = 50.0
pair_weight = 256.0
masked_value = -1000000000.0

BLOCKS = 8
TILE = 128
TAIL = 128
BASE = 64

bf16 = jnp.bfloat16
f32 = jnp.float32
ANY = pl.BlockSpec(memory_space=pl.ANY)
HELD = pl.BlockSpec(memory_space=pltpu.VMEM)
VMEM_BYTES = 24 * 1024 * 1024


def dot(left, right):
    return jnp.dot(left, right, preferred_element_type=f32)


def dot_nt(left, right):
    return lax.dot_general(left, right, (((1,), (1,)), ((), ())), preferred_element_type=f32)


def whole(shape):
    return pl.BlockSpec(shape, lambda *_: (0,) * len(shape))


def call(
    kernel,
    grid,
    in_specs,
    out_specs,
    out_shape,
    scratch,
    flops,
    moved,
    special=0,
    after=(),
    alias=None,
    near=(),
    room=VMEM_BYTES,
):
    given, extra = len(in_specs) + 1, len(after)
    last = given + extra + len(out_shape)

    def body(*refs):
        refs[last][...] = jnp.zeros_like(refs[last])
        kernel(*refs[:given], *refs[given + extra : last], *refs[last + 1 :])

    shapes = [
        shape if -1 - number in near else pltpu.HBM(shape.shape, shape.dtype)
        for number, shape in enumerate(out_shape)
    ]
    shapes.append(shaped((8, TILE), f32))
    run = pl.pallas_call(
        body,
        out_shape=shapes,
        grid_spec=pltpu.PrefetchScalarGridSpec(
            num_scalar_prefetch=1,
            grid=grid,
            in_specs=in_specs + [ANY] * extra,
            out_specs=out_specs + [whole((8, TILE))],
            scratch_shapes=scratch,
        ),
        input_output_aliases=alias or {},
        compiler_params=pltpu.CompilerParams(vmem_limit_bytes=room),
        cost_estimate=pl.CostEstimate(
            flops=int(flops), bytes_accessed=int(moved), transcendentals=int(special)
        ),
    )

    def apply(index, *operands):
        placed = [
            value if 1 + number in near else pltpu.with_memory_space_constraint(value, pltpu.HBM)
            for number, value in enumerate(operands)
        ]
        return run(index, *placed, *after)

    return apply


def shaped(shape, dtype):
    return jax.ShapeDtypeStruct(shape, dtype)


def swap(value, axis, size, bit):
    return lax.ppermute(value, axis, [(i, i ^ bit) for i in range(size)])


def fsdp_swap(value, bit):
    return swap(value, "fsdp", BLOCKS, bit)


def middle(shard):
    return shard.shape[0] // 32 * 16


def first_stage(shard):
    return fsdp_swap(shard, 2), fsdp_swap(shard, 4)


def second_stage(shard, over_x, over_y):
    half = middle(shard)
    return fsdp_swap(over_y[:half], 2), fsdp_swap(over_x[half:], 4)


def own_pieces(shard, over_x, over_y):
    return [(shard, 0, 0), (over_x, 2, 0), (over_y, 4, 0)]


def far_pieces(shard, far_top, far_low):
    return [(far_top, 6, 0), (far_low, 6, middle(shard))]


def both_cores(pieces):
    return pieces + [(fsdp_swap(value, 1), place ^ 1, off) for value, place, off in pieces]


def gather_whole(shard):
    full = lax.all_gather(shard, "fsdp", axis=0, tiled=True)
    rows = full.shape[0] // BLOCKS
    return [full[i * rows : (i + 1) * rows] for i in range(BLOCKS)]


def meta_of(pieces):
    return tuple((place, off, value.shape[0]) for value, place, off in pieces)


def arrays_of(pieces):
    return [value for value, _, _ in pieces]


def copies_of(
    meta, rows, refs, target, sems, index, source=None, place=None, first=0
):
    copies = []
    for number, ((block, off, count), ref) in enumerate(zip(meta, refs)):
        low, high = max(off, first), min(off + count, first + rows)
        if low >= high:
            continue
        here = pl.ds(pl.multiple_of((index ^ block) * rows + low - first, 16), high - low)
        part = ref.at[low - off : high - off]
        copies.append(
            pltpu.make_async_copy(
                part if source is None else part.at[:, source],
                target.at[here] if place is None else target.at[here, place],
                sems.at[number],
            )
        )
    return copies


def pair_copies(meta, size, refs, target, sems, index, chip):
    copies = []
    for number, ((block, off, count), ref) in enumerate(zip(meta, refs)):
        if block // 2 == chip:
            start = pl.multiple_of((index ^ block) * size + off, 16)
            copies.append(
                pltpu.make_async_copy(ref, target.at[pl.ds(start, count)], sems.at[number])
            )
    return copies


def start_all(copies):
    for copy in copies:
        copy.start()


def wait_all(copies):
    for copy in copies:
        copy.wait()


def columns(number, size, base=0):
    return pl.ds(pl.multiple_of(base + number * size, TILE), size)


def fill_mask(seg_row, mask_ref):
    length = seg_row.shape[1]
    keys = jnp.broadcast_to(seg_row, (TILE, length)).T
    for lo, hi, at in bands(length):
        same = keys[lo:hi] == seg_row[:, at : at + TILE]
        mask_ref[lo:hi, at : at + TILE] = jnp.where(same, 0.0, masked_value)


def bands(length):
    out = []
    for at in range(0, length, TILE):
        out.append((max(at - TILE, 0), min(at + 2 * TILE, length), at))
    return out


def two_heads(pair):
    lane = lax.broadcasted_iota(jnp.int32, (1, pair.shape[1]), 1)
    first = (lane < pair.shape[1] // 2).astype(f32).astype(bf16)
    return jnp.concatenate([pair * first, pair * (1.0 - first)], axis=0)


def twice(value):
    return jnp.concatenate([value, value], axis=1)


def pack_line(vectors, width):
    line = jnp.concatenate([jnp.pad(v, (0, -v.shape[0] % TILE)) for v in vectors])
    return jnp.pad(line[None], ((0, 15), (0, width - line.shape[0])))


def pack_first(w_qkv, b_qv):
    return jnp.concatenate([w_qkv, pack_line([b_qv], w_qkv.shape[1])], axis=0)


def pack_second(w_out, w_up, *vectors):
    both = jnp.concatenate([w_out, w_up], axis=1)
    return jnp.concatenate([both, pack_line(vectors, both.shape[1])], axis=0)


def table_of(lines):
    line = lax.broadcasted_iota(jnp.int32, (BLOCKS, 16 * BLOCKS), 0) * 16
    pick = line == lax.broadcasted_iota(jnp.int32, (BLOCKS, 16 * BLOCKS), 1)
    return dot(pick.astype(f32).astype(bf16), lines)


def spread(table, at, size):
    count = table.shape[0]
    padded = size + -size % TILE
    block = table[:, at : at + padded].astype(bf16)
    col = lax.broadcasted_iota(jnp.int32, (1, count * size), 1)
    owner = col // size
    place = lax.broadcasted_iota(jnp.int32, (padded, count * size), 0) == col - owner * size
    value = dot(block, place.astype(f32).astype(bf16))
    keep = lax.broadcasted_iota(jnp.int32, value.shape, 0) == owner
    return jnp.sum(jnp.where(keep, value, 0.0), axis=0, keepdims=True), at + padded


def qkv_kernel(meta, size, index_ref, tok_ref, *rest):
    pieces, rest = rest[: len(meta)], rest[len(meta) :]
    qkv_ref, w_ref, small_ref, bias_ref, sems, small_sems = rest
    width = tok_ref.shape[1]
    rows = width // BLOCKS
    part = pl.program_id(0)
    index = index_ref[0]

    def weights(number):
        cols = columns(number, width)
        return copies_of(meta, rows, pieces, w_ref, sems.at[number], index, cols, cols)

    @pl.when(part == 0)
    def _():
        here = slice(0, small_ref.shape[1])
        small = copies_of(meta, 16, pieces, small_ref, small_sems, index, here, None, rows)
        start_all(small)
        for number in range(3):
            start_all(weights(number))
        wait_all(small)
        bias, _ = spread(table_of(small_ref[...]), 0, size)
        bias_ref[0] = bias[:, :width]
        bias_ref[1] = jnp.zeros((1, width), f32)
        bias_ref[2] = bias[:, width:]

    wait_all(weights(part))
    scale = jnp.where(part == 0, 1.0 / math.sqrt(width // HEADS), 1.0)
    value = dot(tok_ref[...], w_ref[:, columns(part, width)]) + bias_ref[part]
    qkv_ref[...] = (value * scale).astype(bf16)


def project_qkv(index, tokens, pieces, size):
    count, width = tokens.shape
    meta = meta_of(pieces)
    out = pl.BlockSpec((count, width), lambda i, s: (0, i))
    return call(
        functools.partial(qkv_kernel, meta, size),
        (3,),
        [whole((count, width))] + [ANY] * len(meta),
        [out],
        [shaped((count, 3 * width), bf16)],
        [
            pltpu.VMEM((width, 3 * width), bf16),
            pltpu.VMEM((16 * BLOCKS, size + -size % TILE), bf16),
            pltpu.VMEM((3, 1, width), f32),
            pltpu.SemaphoreType.DMA((3, len(meta))),
            pltpu.SemaphoreType.DMA((len(meta),)),
        ],
        count * width * width * 6,
        count * width * 8 + width * width * 6,
        near=(-1,),
    )(index, tokens, *arrays_of(pieces))


def attend_kernel(index_ref, qkv_ref, seg_ref, *rest):
    ctx_ref, lse_ref, vt_ref, ct_ref, mask_ref = rest[-5:]
    length, width = ctx_ref.shape
    pairs = HEADS // 2
    lanes = width // pairs
    half = lanes // 2
    fill_mask(seg_ref[0].astype(f32), mask_ref)
    vt_ref[...] = qkv_ref[:, 2 * width :].T

    tiles = [(pair, band) for pair in range(pairs) for band in bands(length)]

    def scores_of(tile):
        pair, (lo, hi, at) = tile
        queries = two_heads(qkv_ref[at : at + TILE, pair * lanes : (pair + 1) * lanes])
        keys = qkv_ref[lo:hi, width + pair * lanes : width + (pair + 1) * lanes]
        return dot_nt(keys, queries)

    def probs_of(tile, scores):
        pair, (lo, hi, at) = tile
        scores = scores + twice(mask_ref[lo:hi, at : at + TILE])
        top = jnp.max(scores, axis=0, keepdims=True)
        terms = jnp.exp(scores - top)
        total = jnp.sum(terms, axis=0, keepdims=True)
        lse = top + jnp.log(total)
        for head in range(2):
            lse_ref[0, pair, head : head + 1, at : at + TILE] = lse[:, head * TILE : (head + 1) * TILE]
        return (terms * (1.0 / total)).astype(bf16)

    def put_context(tile, probs):
        pair, (lo, hi, at) = tile
        context = dot(vt_ref[pair * lanes : (pair + 1) * lanes, lo:hi], probs)
        for head in range(2):
            rows = slice(pair * lanes + head * half, pair * lanes + (head + 1) * half)
            part = context[head * half : (head + 1) * half, head * TILE : (head + 1) * TILE]
            ct_ref[rows, at : at + TILE] = part.astype(bf16)

    ready = {}
    probs = {}
    for step in range(len(tiles) + 2):
        if step < len(tiles):
            ready[step] = scores_of(tiles[step])
        if 0 <= step - 1 < len(tiles):
            probs[step - 1] = probs_of(tiles[step - 1], ready.pop(step - 1))
        if 0 <= step - 2:
            put_context(tiles[step - 2], probs.pop(step - 2))
    ctx_ref[...] = ct_ref[...].T


def attend(index, qkv, seg_rows, row, before=(), after=()):
    count, width = qkv.shape[0], qkv.shape[1] // 3
    rows, _, length = seg_rows.shape
    pairs = HEADS // 2
    return call(
        attend_kernel,
        (1,),
        [
            pl.BlockSpec((length, 3 * width), lambda i, s: (row, 0)),
            pl.BlockSpec((1, 1, length), lambda i, s: (row, 0, 0)),
        ]
        + [ANY] * len(before),
        [
            pl.BlockSpec((length, width), lambda i, s: (row, 0)),
            pl.BlockSpec((1, pairs, 2, length), lambda i, s: (row, 0, 0, 0)),
        ],
        [
            shaped((count, width), bf16),
            shaped((rows, pairs, 2, length), f32),
        ],
        [
            pltpu.VMEM((width, length), bf16),
            pltpu.VMEM((width, length), bf16),
            pltpu.VMEM((length, length), f32),
        ],
        length * length * width * 4,
        length * width * 8,
        length * length * HEADS * 5 // 8,
        after,
        {3 + i: i for i in range(len(before))},
        (1, -1, -2) + ((3, 4) if before else ()),
    )(index, qkv, seg_rows, *before)


def row_stats(values):
    mean = jnp.mean(values, axis=-1, keepdims=True)
    centred = values - mean
    spread = jnp.mean(centred * centred, axis=-1, keepdims=True)
    return centred, lax.rsqrt(spread + norm_eps)


def project_kernel(meta, sizes, index_ref, ctx_ref, tok_ref, *rest):
    pieces, rest = rest[: len(meta)], rest[len(meta) :]
    norm_ref, root_ref, hid_ref, vec_ref, up_ref, w_ref, small_ref, sems, small_sems = rest
    width = w_ref.shape[0]

    @pl.when(pl.program_id(0) == 0)
    def _():
        rows = width // BLOCKS
        here = slice(0, width)
        copies = copies_of(meta, rows, pieces, w_ref, sems, index_ref[0], here, here)
        line = slice(0, small_ref.shape[1])
        small = copies_of(meta, 16, pieces, small_ref, small_sems, index_ref[0], line, None, rows)
        start_all(small)
        start_all(copies)
        vec_ref[...] = jnp.zeros_like(vec_ref)
        wait_all(small)
        table = table_of(small_ref[...])
        line, at = 0, 0
        for size in sizes:
            value, at = spread(table, at, size)
            if value.shape[1] == width:
                vec_ref[line : line + 1] = value
                line += 1
            else:
                up_ref[...] = value
        wait_all(copies)

    def finish(here, product):
        summed = tok_ref[here].astype(f32) + (product + vec_ref[0:1])
        centred, root = row_stats(summed)
        normed = centred * root
        norm_ref[here] = normed
        root_ref[here] = root
        hid_ref[here] = (normed * vec_ref[1:2] + vec_ref[2:3]).astype(bf16)

    in_turn(ctx_ref.shape[0], lambda here: dot(ctx_ref[here], w_ref[...]), finish)


def in_turn(count, begin, finish, size=2 * TILE):
    last = None
    for at in range(0, count, size):
        here = slice(at, at + size)
        value = begin(here)
        if last is not None:
            finish(*last)
        last = (here, value)
    finish(*last)


def project(index, context, tokens, pieces, sizes, after=(), step=512):
    count, width = tokens.shape
    inner = 4 * width
    used = sum(size + -size % TILE for size in sizes)
    meta = meta_of(pieces)
    rows = pl.BlockSpec((step, width), lambda i, s: (i, 0))
    return call(
        functools.partial(project_kernel, meta, sizes),
        (count // step,),
        [rows, rows] + [ANY] * len(meta),
        [
            rows,
            pl.BlockSpec((step, 1), lambda i, s: (i, 0)),
            rows,
            whole((SEGS, width)),
            whole((1, inner)),
        ],
        [
            shaped((count, width), f32),
            shaped((count, 1), f32),
            shaped((count, width), bf16),
            shaped((SEGS, width), f32),
            shaped((1, inner), f32),
        ],
        [
            pltpu.VMEM((width, width), bf16),
            pltpu.VMEM((16 * BLOCKS, used), bf16),
            pltpu.SemaphoreType.DMA((len(meta),)),
            pltpu.SemaphoreType.DMA((len(meta),)),
        ],
        count * width * width * 2,
        count * width * 10 + width * width * 2,
        0,
        after,
        near=(1, -3, -4, -5),
    )(index, context, tokens, *arrays_of(pieces))


def gelu_parts(value):
    share = 0.5 * lax.erf(value * math.sqrt(0.5)) + 0.5
    bell = jnp.exp2(value * value * (-0.5 / math.log(2.0)))
    return value * share, share + value * bell * (1.0 / math.sqrt(2.0 * math.pi))


def up_kernel(meta, index_ref, hid_ref, bias_ref, *rest):
    pieces, rest = rest[: len(meta)], rest[len(meta) :]
    act_ref, slope_ref, w_ref, sems = rest
    tile = act_ref.shape[1]
    width = w_ref.shape[0]
    step = pl.program_id(0)

    def weights(number):
        source, place = columns(number, tile, width), columns(number, tile)
        rows = width // BLOCKS
        return copies_of(meta, rows, pieces, w_ref, sems.at[number], index_ref[0], source, place)

    @pl.when(step == 0)
    def _():
        for number in range(sems.shape[0]):
            start_all(weights(number))

    wait_all(weights(step))
    wide = 256

    def begin(cols):
        here = pl.ds(pl.multiple_of(step * tile + cols.start, wide), wide)
        return dot(hid_ref[...], w_ref[:, here]) + bias_ref[:, cols]

    def finish(cols, value):
        act, slope = gelu_parts(value)
        act_ref[:, cols] = act.astype(bf16)
        slope_ref[:, cols] = slope.astype(bf16)

    in_turn(tile, begin, finish, wide)


def up(index, hidden, bias, pieces, after=(), tile=768):
    count, width = hidden.shape
    inner = bias.shape[1]
    meta = meta_of(pieces)
    out = pl.BlockSpec((count, tile), lambda i, s: (0, i))
    return call(
        functools.partial(up_kernel, meta),
        (inner // tile,),
        [HELD, pl.BlockSpec((1, tile), lambda i, s: (0, i))] + [ANY] * len(meta),
        [out, out],
        [shaped((count, inner), bf16)] * 2,
        [
            pltpu.VMEM((width, inner), bf16),
            pltpu.SemaphoreType.DMA((inner // tile, len(meta))),
        ],
        count * width * inner * 2,
        count * (width * 2 + inner * 4) + width * inner * 2,
        count * inner * 4,
        after,
        near=(1, 2),
    )(index, hidden, bias, *arrays_of(pieces))


def down_kernel(meta, index_ref, act_ref, norm_ref, vec_ref, seg_ref, pos_ref, *rest):
    pieces, rest = rest[: len(meta)], rest[len(meta) :]
    res_ref, norm2_ref, root_ref, pay_ref, pool_ref, stat_ref, *rest = rest
    w_ref, held_ref, sum_ref, num_ref, sems, act_sems = rest
    step, steps = pl.program_id(0), pl.num_programs(0)
    length, width = res_ref.shape
    tile = w_ref.shape[0] // 4
    index = index_ref[0]

    def weights(chip):
        return pair_copies(meta, tile // 2, pieces, w_ref, sems, index, chip)

    def inputs(row, chip):
        rows = pl.ds(pl.multiple_of(row * length, length), length)
        source = act_ref.at[rows, columns((index // 2) ^ chip, tile)]
        return pltpu.make_async_copy(source, held_ref.at[row, chip], act_sems.at[row, chip])

    @pl.when(step == 0)
    def _():
        inputs(0, 0).start()
        start_all(weights(0))

    wanted = lax.broadcasted_iota(jnp.int32, (SEGS, length), 0)
    member = (wanted == seg_ref[0]).astype(f32)
    product = None
    for chip in range(4):
        inputs(step, chip).wait()

        @pl.when(step == 0)
        def _():
            wait_all(weights(chip))
            if chip < 3:
                inputs(0, chip + 1).start()
                start_all(weights(chip + 1))
            else:
                for other in range(4):
                    inputs(1, other).start()

        value = dot(held_ref[step, chip], w_ref[columns((index // 2) ^ chip, tile)])
        product = value if product is None else product + value
    hidden = norm_ref[...] * vec_ref[1:2] + vec_ref[2:3]
    summed = hidden + (product + vec_ref[3:4])
    centred, root = row_stats(summed)
    normed = centred * root
    result = normed * vec_ref[4:5] + vec_ref[5:6]
    norm2_ref[...] = normed
    root_ref[...] = root
    high = result.astype(bf16)
    res_ref[...] = high
    low = (result - high.astype(f32)).astype(bf16)
    own = pl.ds(pl.multiple_of(step * SEGS, SEGS), SEGS)
    member_b = member.astype(bf16)
    sum_ref[own] = dot(member_b, high) + dot(member_b, low)
    num_ref[own] = jnp.broadcast_to(jnp.sum(member, axis=1, keepdims=True), (SEGS, TAIL))

    @pl.when(step == steps - 1)
    def _():
        counts = num_ref[:, 0:1]
        pooled = sum_ref[...] / counts
        scale = lax.rsqrt(jnp.mean(pooled * pooled, axis=-1, keepdims=True) + pool_eps)
        pool_ref[...] = pooled
        lane = lax.broadcasted_iota(jnp.int32, (pooled.shape[0], TAIL), 1)
        stat_ref[...] = jnp.where(lane == 0, scale, counts)
        pay_ref[:, :width] = (pooled * scale).astype(bf16)
        partner = pos_ref[...]
        digit = jnp.where(lane == 0, partner // BASE, partner % BASE)
        pay_ref[:, width:] = jnp.where(lane < 2, digit, 0).astype(f32).astype(bf16)


def down(index, activated, normed, vectors, seg_rows, positive, pieces, after=()):
    count, width = normed.shape
    inner = activated.shape[1]
    rows, _, step = seg_rows.shape
    own = rows * SEGS
    meta = meta_of(pieces)
    block = pl.BlockSpec((step, width), lambda i, s: (i, 0))
    return call(
        functools.partial(down_kernel, meta),
        (count // step,),
        [
            ANY,
            block,
            whole(vectors.shape),
            pl.BlockSpec((1, 1, step), lambda i, s: (i, 0, 0)),
            whole((own, 1)),
        ]
        + [ANY] * len(meta),
        [
            block,
            block,
            pl.BlockSpec((step, 1), lambda i, s: (i, 0)),
            whole((own, width + TAIL)),
            whole((own, width)),
            whole((own, TAIL)),
        ],
        [
            shaped((count, width), bf16),
            shaped((count, width), f32),
            shaped((count, 1), f32),
            shaped((own, width + TAIL), bf16),
            shaped((own, width), f32),
            shaped((own, TAIL), f32),
        ],
        [
            pltpu.VMEM((inner, width), bf16),
            pltpu.VMEM((rows, 4, step, inner // 4), bf16),
            pltpu.VMEM((own, width), f32),
            pltpu.VMEM((own, TAIL), f32),
            pltpu.SemaphoreType.DMA((len(meta),)),
            pltpu.SemaphoreType.DMA((rows, 4)),
        ],
        count * width * inner * 2,
        count * (width * 10 + inner * 2) + width * inner * 2,
        after=after,
        near=(3, 5, -4, -5, -6),
    )(index, activated, normed, vectors, seg_rows, positive, *arrays_of(pieces))


def segment_of(row, own, cores, chips, planes):
    block = row // own
    plane, chip, core = block % planes, block // planes % chips, block // (planes * chips)
    return ((plane * chips + chip) * cores + core) * own + row % own


def contrast_kernel(layout, place_ref, own_ref, pos_ref, pool_ref, stat_ref, *rest):
    pieces, (loss_ref, grad_ref, all_ref, sems) = rest[:-4], rest[-4:]
    copies, at = [], 0
    for number, piece in enumerate(pieces):
        here = all_ref.at[at : at + piece.shape[0]]
        copies.append(pltpu.make_async_copy(piece, here, sems.at[number]))
        at += piece.shape[0]
    for copy in copies:
        copy.start()
    for copy in copies:
        copy.wait()
    total = all_ref.shape[0]
    own, width = pool_ref.shape
    factor = score_scale / width
    block = min(total, 512)
    flip, first = place_ref[0], place_ref[1]
    mine = own_ref[:, :width]
    mine_id = lax.broadcasted_iota(jnp.int32, (own, total), 0) + first
    other_id = segment_of(lax.broadcasted_iota(jnp.int32, (1, total), 1), own, *layout) ^ flip
    logits = dot_nt(mine, all_ref[:, :width]) * factor
    logits = jnp.where(mine_id == other_id, masked_value, logits)
    top = jnp.max(logits, axis=1, keepdims=True)
    log_own = top + jnp.log(jnp.sum(jnp.exp(logits - top), axis=1, keepdims=True))
    is_positive = other_id == pos_ref[...]
    picked = jnp.sum(jnp.where(is_positive, logits, 0.0), axis=1, keepdims=True)
    loss_ref[...] = log_own - picked
    d_logits = pair_weight * (jnp.exp(logits - log_own) - is_positive.astype(f32))
    d_emb = dot(d_logits.astype(bf16), all_ref[:, :width])
    lane = lax.broadcasted_iota(jnp.int32, (SEGS, TAIL), 1)
    digits = jnp.where(lane == 0, float(BASE), jnp.where(lane == 1, 1.0, 0.0)).astype(bf16)
    for at in range(0, total, block):
        rows = slice(at, at + block)
        table = dot_nt(all_ref[:, :width], all_ref[rows, :width]) * factor
        left = lax.broadcasted_iota(jnp.int32, (total, block), 0)
        right = lax.broadcasted_iota(jnp.int32, (total, block), 1) + at
        table = jnp.where(left == right, masked_value, table)
        top = jnp.max(table, axis=0, keepdims=True)
        log_all = top + jnp.log(jnp.sum(jnp.exp(table - top), axis=0, keepdims=True))
        partner = dot_nt(digits, all_ref[rows, width:])[0:1].astype(jnp.int32)
        chosen = partner == mine_id[:, rows]
        back = pair_weight * (jnp.exp(logits[:, rows] - log_all) - chosen.astype(f32))
        d_emb += dot(back.astype(bf16), all_ref[rows, :width])
    d_emb = d_emb * factor
    scale, counts = stat_ref[:, 0:1], stat_ref[:, 1:2]
    pooled = pool_ref[...]
    along = jnp.mean(d_emb * pooled, axis=-1, keepdims=True)
    grad_ref[...] = (d_emb * scale - pooled * (scale * scale * scale * along)) / counts


def contrast(place, layout, everyone, payload, positive, pooled, stats, after=()):
    own, width = pooled.shape
    total = sum(v.shape[0] for v in everyone)
    return call(
        functools.partial(contrast_kernel, layout),
        (1,),
        [whole(v.shape) for v in (payload, positive, pooled, stats)] + [ANY] * len(everyone),
        [whole((own, 1)), whole((own, width))],
        [shaped((own, 1), f32), shaped((own, width), f32)],
        [
            pltpu.VMEM((total, width + TAIL), bf16),
            pltpu.SemaphoreType.DMA((len(everyone),)),
        ],
        total * total * width * 2,
        total * width * 2,
        total * total,
        after=after,
        near=(1, 2, 3, 4, -1, -2),
    )(place, payload, positive, pooled, stats, *everyone)


def norm_back(d_out, normed, root, gain):
    scaled = d_out * gain
    mean = jnp.mean(scaled, axis=-1, keepdims=True)
    along = jnp.mean(scaled * normed, axis=-1, keepdims=True)
    return root * (scaled - mean - normed * along)


def column_sum(values):
    return jnp.sum(values, axis=0, keepdims=True)


def norm2_kernel(turns, index_ref, og_ref, norm_ref, root_ref, seg_ref, vec_in_ref, dp_ref, *rest):
    act_ref, dsum_ref, ddown_ref, vec_ref, keep_ref, send_ref, dt_ref = rest
    step = pl.program_id(0)
    chunk, width = og_ref.shape
    own = dp_ref.shape[0]

    @pl.when(step == 0)
    def _():
        vec_ref[...] = jnp.zeros_like(vec_ref)

    @pl.when(step < turns)
    def _():
        row = step // (turns * SEGS // own)
        pool = dp_ref[pl.ds(pl.multiple_of(row * SEGS, SEGS), SEGS)]
        high = pool.astype(bf16)
        left = pool - high.astype(f32)
        mid = left.astype(bf16)
        low = (left - mid.astype(f32)).astype(bf16)
        pad = jnp.zeros((TILE - 3 * SEGS, width), bf16)
        table = jnp.concatenate([high, mid, low, pad], axis=0)
        lane = lax.broadcasted_iota(jnp.int32, (chunk, TILE), 1) % SEGS
        keys = jnp.broadcast_to(seg_ref[0].astype(f32), (TILE, chunk)).T
        member = (lane.astype(f32) == keys).astype(f32).astype(bf16)

        def begin(here):
            return dot(member[here], table)

        def finish(here, shared):
            d_res = og_ref[here].astype(f32) + shared
            normed = norm_ref[here]
            d_sum = norm_back(d_res, normed, root_ref[here], vec_in_ref[4:5])
            d_down = d_sum.astype(bf16)
            dsum_ref[here] = d_sum
            ddown_ref[here] = d_down
            cols = pl.ds(pl.multiple_of(step * chunk + here.start, TILE), TILE)
            dt_ref[:, cols] = d_down.T
            vec_ref[0:1] += column_sum(d_down.astype(f32))
            vec_ref[1:2] += column_sum(d_res * normed)
            vec_ref[2:3] += column_sum(d_res)

        in_turn(chunk, begin, finish, TILE)

    @pl.when(step >= turns)
    def _():
        grad = dot(dt_ref[...], act_ref[...]).astype(bf16)
        half = grad.shape[1] // 2
        odd = index_ref[0] % 2 == 1
        keep_ref[0] = jnp.where(odd, grad[:, half:], grad[:, :half])
        send_ref[0] = jnp.where(odd, grad[:, :half], grad[:, half:])


def norm2(index, out_grad, normed, root, seg_rows, vectors, d_pool, activated, turns=4):
    count, width = out_grad.shape
    inner = activated.shape[1]
    tile = inner // 4
    own = d_pool.shape[0]
    first = lambda i: jnp.minimum(i, turns - 1)
    then = lambda i: jnp.maximum(i - turns, 0)
    split = turns // seg_rows.shape[0]
    block = pl.BlockSpec((count // turns, width), lambda i, s: (first(i), 0))
    column = pl.BlockSpec((count // turns, 1), lambda i, s: (first(i), 0))
    grads = pl.BlockSpec((1, width, tile // 2), lambda i, s: (then(i), 0, 0))
    return call(
        functools.partial(norm2_kernel, turns),
        (turns + 4,),
        [
            block,
            block,
            column,
            pl.BlockSpec((1, 1, count // turns), lambda i, s: (first(i) // split, 0, first(i) % split)),
            whole(vectors.shape),
            whole((own, width)),
            pl.BlockSpec((count, tile), lambda i, s: (0, (s[0] // 2) ^ then(i))),
        ],
        [block, block, whole((SEGS, width)), grads, grads],
        [
            shaped((count, width), f32),
            shaped((count, width), bf16),
            shaped((SEGS, width), f32),
            shaped((4, width, tile // 2), bf16),
            shaped((4, width, tile // 2), bf16),
        ],
        [pltpu.VMEM((width, count), bf16)],
        count * width * inner * 2,
        count * (width * 12 + inner * 2) + width * inner * 2,
        near=(5, 6, -1, -2, -3, -4, -5),
    )(index, out_grad, normed, root, seg_rows, vectors, d_pool, activated)


def put_turned(source_ref, target_ref, turn_ref, index):
    turn_ref[...] = source_ref[...].T
    rows = turn_ref.shape[0] // BLOCKS
    for place in range(BLOCKS):
        block = index ^ ((place % 4) * 2 + place // 4)
        start = pl.multiple_of(block * rows, 16)
        target_ref[place * rows : (place + 1) * rows] = turn_ref[pl.ds(start, rows)]


def weights_kernel(down_meta, up_meta, index_ref, *refs):
    pieces, (wd_ref, wu_ref, sems, up_sems) = refs[:-4], refs[-4:]
    low, high = pieces[: len(down_meta)], pieces[len(down_meta) :]
    width, inner = wu_ref.shape
    here = slice(width, width + inner)
    copies = copies_of(down_meta, inner // BLOCKS, low, wd_ref, sems, index_ref[0])
    copies += copies_of(up_meta, width // BLOCKS, high, wu_ref, up_sems, index_ref[0], here)
    start_all(copies)
    wait_all(copies)


def hold_weights(index, down_pieces, up_pieces, width, inner, after=()):
    down_meta, up_meta = meta_of(down_pieces), meta_of(up_pieces)
    return call(
        functools.partial(weights_kernel, down_meta, up_meta),
        (1,),
        [ANY] * (len(down_meta) + len(up_meta)),
        [HELD, HELD],
        [shaped((inner, width), bf16), shaped((width, inner), bf16)],
        [
            pltpu.SemaphoreType.DMA((len(down_meta),)),
            pltpu.SemaphoreType.DMA((len(up_meta),)),
        ],
        0,
        width * inner * 8,
        0,
        after,
        near=(-1, -2),
    )(index, *arrays_of(down_pieces), *arrays_of(up_pieces))


def turned_kernel(index_ref, one_ref, two_ref, out_one_ref, out_two_ref, turn_ref):
    put_turned(one_ref, out_one_ref, turn_ref, index_ref[0])
    put_turned(two_ref, out_two_ref, turn_ref, index_ref[0])


def hold_turned(index, one, two, after=()):
    count, width = one.shape
    return call(
        turned_kernel,
        (1,),
        [whole((count, width))] * 2,
        [HELD, HELD],
        [shaped((width, count), bf16)] * 2,
        [pltpu.VMEM((width, count), bf16)],
        0,
        count * width * 8,
        0,
        after,
        near=(-1, -2),
    )(index, one, two)


def up_back_kernel(first, before, index_ref, ddown_ref, slope_ref, ht_ref, wd_ref, wu_ref, *rest):
    earlier, rest = rest[:before], rest[before:]
    dhid_ref, bias_ref, keep_ref, send_ref = rest
    step = pl.program_id(0)
    tile = slope_ref.shape[1]
    width = ht_ref.shape[0]
    here = columns((index_ref[0] // 2) ^ (step + first), tile)
    wide = 256
    parts = []

    def begin(cols):
        rows = pl.ds(pl.multiple_of(here.start + cols.start, wide), wide)
        return dot_nt(ddown_ref[...], wd_ref[rows])

    def finish(cols, d_act):
        d_up = (d_act * slope_ref[:, cols].astype(f32)).astype(bf16)
        bias_ref[:, cols] = column_sum(d_up.astype(f32))
        parts.append(d_up)

    in_turn(tile, begin, finish, wide)
    d_up = jnp.concatenate(parts, axis=1)
    grad = dot(ht_ref[...], d_up).astype(bf16)
    half = width // 2
    keep_ref[...] = grad[:half].reshape(keep_ref.shape)
    send_ref[...] = grad[half:].reshape(send_ref.shape)
    share = dot_nt(d_up, wu_ref[:, here])

    @pl.when(step == 0)
    def _():
        dhid_ref[...] = earlier[0][...] + share if earlier else share

    @pl.when(step > 0)
    def _():
        dhid_ref[...] += share


def up_back(index, d_down, slope, turned, w_down, w_up, first, steps, before=(), after=()):
    count, width = d_down.shape
    inner = slope.shape[1]
    tile = inner // 4
    part = width // BLOCKS
    place = lambda i, s: (s[0] // 2) ^ (i + first)
    grads = pl.BlockSpec((4, part, tile), lambda i, s: (0, 0, place(i, s)))
    return call(
        functools.partial(up_back_kernel, first, len(before)),
        (steps,),
        [HELD, pl.BlockSpec((count, tile), lambda i, s: (0, place(i, s))), HELD, HELD, HELD]
        + ([HELD] + [ANY] * 3 if before else []),
        [HELD, pl.BlockSpec((1, tile), lambda i, s: (0, place(i, s))), grads, grads],
        [
            shaped((count, width), f32),
            shaped((1, inner), f32),
            shaped((4, part, inner), bf16),
            shaped((4, part, inner), bf16),
        ],
        [],
        count * width * tile * 6 * steps,
        count * (width * 8 + inner) + width * inner * 6,
        0,
        after,
        {6 + i: i for i in range(len(before))},
        (1, 3, 4, 5, 6, 7, 8, 9, -1, -2, -3, -4),
    )(index, d_down, slope, turned, w_down, w_up, *before)


def cut_vector(vector, size, index):
    width = vector.shape[1]
    owner = lax.broadcasted_iota(jnp.int32, (BLOCKS, width), 1) // size
    wanted = lax.broadcasted_iota(jnp.int32, (BLOCKS, width), 0) ^ index
    rows = jnp.where(owner == wanted, vector, 0.0).astype(bf16)
    source = lax.broadcasted_iota(jnp.int32, (width, 1), 0)
    place = source - source // size * size == lax.broadcasted_iota(jnp.int32, (width, TILE), 1)
    return dot(rows, place.astype(f32).astype(bf16))


def norm1_kernel(meta, parts, index_ref, *rest):
    dhids, rest = rest[:parts], rest[parts:]
    dsum_ref, norm_ref, root_ref, gain_ref, ctx_ref, other_ref, up_ref, *rest = rest
    pieces, rest = rest[: len(meta)], rest[len(meta) :]
    dattn_ref, dctx_ref, keep_ref, send_ref, w_ref, acc_ref, vec_ref, sems = rest
    step = pl.program_id(0)
    width = w_ref.shape[0]
    rows = width // BLOCKS

    @pl.when(step == 0)
    def _():
        here = slice(0, width)
        copies = copies_of(meta, rows, pieces, w_ref, sems, index_ref[0], here, here)
        start_all(copies)
        vec_ref[...] = jnp.zeros_like(vec_ref)
        acc_ref[...] = jnp.zeros_like(acc_ref)
        wait_all(copies)

    parts = []

    def begin(here):
        d_hid = dsum_ref[here]
        for dhid_ref in dhids:
            d_hid = d_hid + dhid_ref[here]
        normed = norm_ref[here]
        d_sum = norm_back(d_hid, normed, root_ref[here], gain_ref[1:2])
        d_attn = d_sum.astype(bf16)
        dattn_ref[here] = d_sum
        vec_ref[0:1] += column_sum(d_attn.astype(f32))
        vec_ref[1:2] += column_sum(d_hid * normed)
        vec_ref[2:3] += column_sum(d_hid)
        parts.append(d_attn)
        return d_attn

    def finish(here, d_attn):
        dctx_ref[here] = dot_nt(d_attn, w_ref[...]).astype(bf16)

    in_turn(dsum_ref.shape[0], begin, finish)
    acc_ref[...] += dot(ctx_ref[...].T, jnp.concatenate(parts, axis=0))

    @pl.when(step == pl.num_programs(0) - 1)
    def _():
        index = index_ref[0]
        vectors = [vec_ref[i : i + 1] for i in range(3)] + [other_ref[i : i + 1] for i in range(3)]
        top = [cut_vector(vector, rows, index) for vector in vectors]
        top = jnp.concatenate(top, axis=1)
        size = up_ref.shape[1] // BLOCKS
        line = lax.broadcasted_iota(jnp.int32, (16, width), 0)
        pad = jnp.zeros((1, width - size), f32)
        for place in range(4):
            for target, core in ((keep_ref, 0), (send_ref, 1)):
                number = 2 * place + core
                block = index ^ number
                start = pl.multiple_of(block * rows, 16)
                target[place, :rows] = acc_ref[pl.ds(start, rows)].astype(bf16)
                low = up_ref[:, pl.ds(pl.multiple_of(block * size, size), size)]
                low = jnp.concatenate([low, pad], axis=1)
                extra = jnp.where(line == 0, top[number : number + 1], 0.0)
                extra = jnp.where(line == 1, low, extra)
                target[place, rows:] = extra.astype(bf16)


def norm1(
    index, d_hiddens, d_summed, normed, root, gain, context, sums, sums_up, pieces, after=(), step=512
):
    count, width = d_summed.shape
    meta = meta_of(pieces)
    part = width // BLOCKS + 16
    block = pl.BlockSpec((step, width), lambda i, s: (i, 0))
    return call(
        functools.partial(norm1_kernel, meta, len(d_hiddens)),
        (count // step,),
        [block] * len(d_hiddens)
        + [
            block,
            block,
            pl.BlockSpec((step, 1), lambda i, s: (i, 0)),
            whole(gain.shape),
            block,
            whole(sums.shape),
            whole(sums_up.shape),
        ]
        + [ANY] * len(meta),
        [block, block, whole((4, part, width)), whole((4, part, width))],
        [
            shaped((count, width), f32),
            shaped((count, width), bf16),
            shaped((4, part, width), bf16),
            shaped((4, part, width), bf16),
        ],
        [
            pltpu.VMEM((width, width), bf16),
            pltpu.VMEM((width, width), f32),
            pltpu.VMEM((SEGS, width), f32),
            pltpu.SemaphoreType.DMA((len(meta),)),
        ],
        count * width * width * 4,
        count * width * 20 + width * width * 4,
        0,
        after,
        near=tuple(range(1, 2 + len(d_hiddens))) + (6, 7, 8, -1, -2, -3, -4),
    )(
        index, *d_hiddens, d_summed, normed, root, gain, context, sums, sums_up, *arrays_of(pieces)
    )


def attend_back_kernel(
    first, index_ref, q_ref, k_ref, v_ref, dctx_ref, lse_ref, seg_ref, tt_ref, *rest
):
    dq_ref, dk_ref, dv_ref, keep_ref, send_ref = rest[:5]
    mask_ref, kt_ref, two_ref, pt_ref, both_ref = rest[5:]
    rows, _, length = seg_ref.shape
    lanes = 2 * tt_ref.shape[0] // HEADS
    half = lanes // 2
    group = q_ref.shape[1] // lanes
    inv_root = 1.0 / math.sqrt(half)

    @pl.when(pl.program_id(0) == 0)
    def _():
        for row in range(rows):
            fill_mask(seg_ref[row].astype(f32), mask_ref.at[row])

    tiles = [
        (pair, row, band) for pair in range(group) for row in range(rows) for band in bands(length)
    ]
    for pair in range(group):
        for row in range(rows):
            here = slice(row * length, (row + 1) * length)
            kt_ref[pair, row] = k_ref[here, pair * lanes : (pair + 1) * lanes].T

    def begin(tile):
        pair, row, (lo, hi, at) = tile
        cols = slice(pair * lanes, (pair + 1) * lanes)
        base = row * length
        queries = two_heads(q_ref[base + at : base + at + TILE, cols])
        d_context = two_heads(dctx_ref[base + at : base + at + TILE, cols])
        two_ref[0, pair, row, 2 * at : 2 * at + 2 * TILE] = queries
        two_ref[1, pair, row, 2 * at : 2 * at + 2 * TILE] = d_context
        scores = dot_nt(k_ref[base + lo : base + hi, cols], queries)
        return scores, dot_nt(v_ref[base + lo : base + hi, cols], d_context)

    def middle_part(tile, scores, d_probs):
        pair, row, (lo, hi, at) = tile
        lse = jnp.concatenate(
            [lse_ref[row, pair, head : head + 1, at : at + TILE] for head in range(2)], axis=1
        )
        probs = jnp.exp(scores + twice(mask_ref[row, lo:hi, at : at + TILE]) - lse)
        inner = jnp.sum(d_probs * probs, axis=0, keepdims=True)
        d_scores = (probs * (d_probs - inner)).astype(bf16)
        pt_ref[0, pair, row, lo:hi, 2 * at : 2 * at + 2 * TILE] = d_scores
        pt_ref[1, pair, row, lo:hi, 2 * at : 2 * at + 2 * TILE] = probs.astype(bf16)
        return d_scores

    def put(tile, kind, value):
        pair, row, (_, _, at) = tile
        here = slice(row * length + at, row * length + at + TILE)
        cols = slice((kind * group + pair) * lanes, (kind * group + pair + 1) * lanes)
        both_ref[here, cols] = value.astype(bf16)

    def end(tile, d_scores):
        pair, row, (lo, hi, at) = tile
        dq = dot(kt_ref[pair, row, :, lo:hi], d_scores) * inv_root
        dq = jnp.concatenate([dq[:half, :TILE], dq[half:, TILE:]], axis=0)
        put(tile, 0, dq.T)

    def end_keys(tile):
        pair, row, (lo, hi, at) = tile
        cols = slice(2 * lo, 2 * hi)
        for kind in range(2):
            value = dot(
                pt_ref[kind, pair, row, at : at + TILE, cols], two_ref[kind, pair, row, cols]
            )
            put(tile, 1 + kind, value)

    ready = {}
    done = {}
    for step in range(len(tiles) + 3):
        if step < len(tiles):
            ready[step] = begin(tiles[step])
        if 0 <= step - 1 < len(tiles):
            done[step - 1] = middle_part(tiles[step - 1], *ready.pop(step - 1))
        if 0 <= step - 2 < len(tiles):
            end(tiles[step - 2], done.pop(step - 2))
        if 0 <= step - 3 < len(tiles):
            end_keys(tiles[step - 3])
    both = both_ref[...]
    wide = group * lanes
    for kind, target in enumerate((dq_ref, dk_ref, dv_ref)):
        target[...] = both[:, kind * wide : (kind + 1) * wide]
    grad = dot(tt_ref[...], both).astype(bf16)
    width = grad.shape[0]
    part = width // BLOCKS
    span = both.shape[1]
    col = lax.broadcasted_iota(jnp.int32, (1, span), 1)
    kind = col // wide
    place = (pl.program_id(0) * group + first) * lanes + col - kind * wide
    owner = jnp.where(kind == 1, -1, (place + jnp.where(kind == 2, width, 0)) // (2 * part))
    sums = column_sum(both.astype(f32))
    line = lax.broadcasted_iota(jnp.int32, (16, span), 0)
    for block in range(BLOCKS):
        target, core = (keep_ref, 0) if block < 4 else (send_ref, 1)
        target[block % 4, :part] = grad[block * part : (block + 1) * part]
        here = owner == (index_ref[0] ^ (2 * (block % 4) + core))
        extra = jnp.where(line == 0, jnp.where(here, sums, 0.0), 0.0)
        target[block % 4, part:] = extra.astype(bf16)


def attend_back(
    index, qkv, d_context, lse, seg_rows, turned, first, pairs, after=(), group=2
):
    width, count = turned.shape
    rows, _, length = seg_rows.shape
    every = HEADS // 2
    lanes = width // every
    part = width // BLOCKS + 16
    wide = group * lanes
    column = lambda place: pl.BlockSpec((count, wide), lambda i, s: (0, place // group + i))
    out = pl.BlockSpec((count, wide), lambda i, s: (0, i))
    grads = pl.BlockSpec((4, part, 3 * wide), lambda i, s: (0, 0, i))
    return call(
        functools.partial(attend_back_kernel, first),
        (pairs // group,),
        [
            column(first),
            column(every + first),
            column(2 * every + first),
            column(first),
            pl.BlockSpec((rows, group, 2, length), lambda i, s: (0, first // group + i, 0, 0)),
            whole((rows, 1, length)),
            HELD,
        ],
        [out, out, out, grads, grads],
        [
            shaped((count, pairs * lanes), bf16),
            shaped((count, pairs * lanes), bf16),
            shaped((count, pairs * lanes), bf16),
            shaped((4, part, pairs * 3 * lanes), bf16),
            shaped((4, part, pairs * 3 * lanes), bf16),
        ],
        [
            pltpu.VMEM((rows, length, length), f32),
            pltpu.VMEM((group, rows, lanes, length), bf16),
            pltpu.VMEM((2, group, rows, 2 * length, lanes), bf16),
            pltpu.VMEM((2, group, rows, length, 2 * length), bf16),
            pltpu.VMEM((count, 3 * wide), bf16),
        ],
        count * pairs * lanes * (width * 6 + length * 6),
        count * pairs * lanes * 14 + count * width * 2,
        count * length * pairs * 5 // 4,
        after,
        near=(4, 5, 7, -1, -2, -3, -4, -5),
    )(index, qkv, qkv, qkv, d_context, lse, seg_rows, turned)


def input_kernel(meta, parts, index_ref, dattn_ref, *rest):
    grads, rest = rest[: 3 * parts], rest[3 * parts :]
    pieces, rest = rest[: len(meta)], rest[len(meta) :]
    out_ref, w_ref, sems = rest
    width = out_ref.shape[1]
    step = width // parts
    first = pl.program_id(0) == 0

    def weights(kind):
        cols = columns(kind, width)
        rows = width // BLOCKS
        return copies_of(meta, rows, pieces, w_ref, sems.at[kind], index_ref[0], cols, cols)

    @pl.when(first)
    def _():
        for kind in range(3):
            start_all(weights(kind))

    total = dattn_ref[...]
    for kind in range(3):

        @pl.when(first)
        def _():
            wait_all(weights(kind))

        for part in range(parts):
            at = kind * width + part * step
            total += dot_nt(grads[kind * parts + part][...], w_ref[:, at : at + step])
    out_ref[...] = total


def input_grad(index, d_attn, grads, pieces, after=(), step=512):
    count, width = d_attn.shape
    meta = meta_of(pieces)
    parts = len(grads) // 3
    block = pl.BlockSpec((step, width), lambda i, s: (i, 0))
    return call(
        functools.partial(input_kernel, meta, parts),
        (count // step,),
        [block]
        + [pl.BlockSpec((step, g.shape[1]), lambda i, s: (i, 0)) for g in grads]
        + [ANY] * len(meta),
        [block],
        [shaped((count, width), f32)],
        [pltpu.VMEM((width, 3 * width), bf16), pltpu.SemaphoreType.DMA((3, len(meta)))],
        count * width * width * 6,
        count * width * 14 + width * width * 6,
        0,
        after,
        near=tuple(range(1, 2 + len(grads))),
    )(index, d_attn, *grads, *arrays_of(pieces))


def rounded(value):
    return lax.optimization_barrier(value.astype(bf16))


def add(*values):
    total = values[0].astype(f32)
    for value in values[1:]:
        total = total + value.astype(f32)
    return total


def along_z(value, pairs):
    return lax.ppermute(value, "batch", pairs)


def core_kernel(parts, index_ref, *refs):
    keeps, others = refs[:parts], refs[parts : 2 * parts]
    mine_ref, x_ref, y_ref, top_ref, low_ref = refs[2 * parts :]
    half = top_ref.shape[0]
    at = 0
    for keep, other in zip(keeps, others):
        cols = slice(at, at + keep.shape[2])
        at = cols.stop
        for place, target in enumerate((mine_ref, x_ref, y_ref)):
            target[:, cols] = add(keep[place], other[place]).astype(bf16)
        far = add(keep[3], other[3]).astype(bf16)
        top_ref[:, cols] = far[:half]
        low_ref[:, cols] = far[half:]


def add_cores(index, keeps, others):
    rows = keeps[0].shape[1]
    width = sum(keep.shape[2] for keep in keeps)
    half = rows // 32 * 16
    heights = (rows, rows, rows, half, rows - half)
    count = 2 * len(keeps)
    return call(
        functools.partial(core_kernel, len(keeps)),
        (1,),
        [HELD] * count,
        [HELD] * 5,
        [shaped((height, width), bf16) for height in heights],
        [],
        rows * width * 4,
        rows * width * 24,
        near=tuple(range(1, 1 + count)) + (-1, -2, -3, -4, -5),
    )(index, *keeps, *others)


class Sum:
    def __init__(self, index, planes, keeps, sends, line):
        self.index, self.planes, self.keeps, self.line = index, planes, keeps, line
        self.arrived = [fsdp_swap(send, 1) for send in sends]
        self.stages = [self.over_core, self.over_far, self.over_chips, self.over_z, self.over_middle]

    def next(self, clock):
        *self.arrived, _ = lax.optimization_barrier((*self.arrived, clock))
        return list(self.stages.pop(0)(*self.arrived))

    def over_core(self, *others):
        *self.blocks, _ = add_cores(self.index, self.keeps, others)
        self.half = self.blocks[3].shape[0]
        self.arrived = [fsdp_swap(self.blocks[3], 2), fsdp_swap(self.blocks[4], 4)]
        return self.blocks[3:]

    def over_far(self, top, low):
        _, over_x, over_y, _, _ = self.blocks
        half = self.half
        over_x = over_x.at[half:].set(add(over_x[half:], low).astype(bf16))
        over_y = over_y.at[:half].set(add(over_y[:half], top).astype(bf16))
        self.arrived = [fsdp_swap(over_x, 2), fsdp_swap(over_y, 4)]
        return [over_x, over_y]

    def over_chips(self, from_x, from_y):
        self.total = rounded(add(self.blocks[0], from_x, from_y))
        sent = self.total
        if self.line:
            self.arrived = [along_z(sent, [(0, 1), (3, 2)])]
            return [sent]
        half = sent.shape[0] // 2
        self.odd = lax.axis_index("batch") % 2 == 1
        self.total = jnp.where(self.odd, sent[half:], sent[:half])
        sent = jnp.where(self.odd, sent[:half], sent[half:])
        self.arrived = [swap(sent, "batch", self.planes, 1)]
        return [sent]

    def over_z(self, other):
        self.total = rounded(add(self.total, other))
        pairs = [(1, 2), (2, 1)] if self.line else [(0, 2), (2, 0), (1, 3), (3, 1)]
        self.arrived = [along_z(self.total, pairs)]
        return [self.total]

    def over_middle(self, other):
        self.total = rounded(add(self.total, other))
        pairs = [(1, 0), (2, 3)] if self.line else [(0, 1), (1, 0), (2, 3), (3, 2)]
        self.arrived = [along_z(self.total, pairs)]
        return [self.total]

    def result(self):
        other = self.arrived[0]
        if self.line:
            plane = lax.axis_index("batch")
            inside = (plane == 1) | (plane == 2)
            return jnp.where(inside, self.total, other).astype(f32)
        upper = jnp.where(self.odd, other, self.total)
        lower = jnp.where(self.odd, self.total, other)
        return jnp.concatenate([upper, lower], axis=0).astype(f32)


def layer(
    planes,
    ring,
    tokens,
    seg_ids,
    positive,
    out_grad,
    w_qkv,
    b_qv,
    w_out,
    b_out,
    norm1_gain,
    norm1_shift,
    w_up,
    b_up,
    w_down,
    b_down,
    norm2_gain,
    norm2_shift,
):
    paired = ring == BLOCKS and planes == 4
    row_count, row_length, width = tokens.shape
    count = row_count * row_length
    own = row_count * SEGS
    token_rows = tokens.reshape(count, width)
    seg_rows = seg_ids.reshape(row_count, 1, row_length)
    pos_col = positive.reshape(own, 1)
    fsdp = lax.axis_index("fsdp")
    me = lax.axis_index("batch") * ring + fsdp
    index = (fsdp if paired else jnp.zeros_like(fsdp)).reshape(1).astype(jnp.int32)
    tie = lax.optimization_barrier

    small = (b_out, norm1_gain, norm1_shift, b_down, norm2_gain, norm2_shift, b_up)
    sizes = [value.shape[0] * ring // BLOCKS for value in small]
    inner = sizes[-1] * BLOCKS
    if paired:
        first = pack_first(w_qkv, b_qv)
        first_xy = first_stage(first)
        *first_xy, second = tie((*first_xy, pack_second(w_out, w_up, *small)))
        first_far = second_stage(first, *first_xy)
        second, *first_far = tie((second, *first_far))
        second_xy = first_stage(second)
        qkv_pieces = both_cores(own_pieces(first, *first_xy))
        qkv_pieces += both_cores(far_pieces(first, *first_far))
    else:
        blocks = [gather_whole(value) for value in (w_qkv, b_qv, w_down, w_out, w_up, *small)]
        blocks = list(enumerate(zip(*blocks)))
        qkv_pieces = [(pack_first(*b[:2]), i, 0) for i, b in blocks]
        down_pieces = [(b[2], i, 0) for i, b in blocks]
        mid_pieces = [(pack_second(*b[3:]), i, 0) for i, b in blocks]

    qkv, clock = project_qkv(index, token_rows, qkv_pieces, 2 * width // BLOCKS)
    attended = ()
    for row in range(row_count):
        late = ()
        if paired and row == row_count - 1:
            *second_xy, third, clock = tie((*second_xy, w_down, clock))
            second_far = second_stage(second, *second_xy)
            third_xy = first_stage(third)
            late = (*second_xy, clock)
        *attended, clock = attend(index, qkv, seg_rows, row, attended, late)
    context, lse = attended
    if paired:
        mid_pieces = both_cores(own_pieces(second, *second_xy))
        *second_far, clock = tie((*second_far, clock))
        mid_pieces += both_cores(far_pieces(second, *second_far))
    normed1, root1, hidden, rows, bias_up, clock = project(
        index, context, token_rows, mid_pieces, sizes, (clock,)
    )
    late = ()
    if paired:
        *third_xy, clock = tie((*third_xy, clock))
        third_far = fsdp_swap(third_xy[0], 4)
        late = (*third_xy, clock)
    activated, slope, clock = up(index, hidden, bias_up, mid_pieces, late)
    if paired:
        down_pieces = both_cores(own_pieces(w_down, *third_xy))
        third_far, clock = tie((third_far, clock))
        down_pieces += both_cores([(third_far, 6, 0)])
    result, normed2, root2, payload, pooled, stats, _ = down(
        index, activated, normed1, rows, seg_rows, pos_col, down_pieces, (clock,)
    )

    hidden_turned, tokens_turned, clock = hold_turned(index, hidden, token_rows, (payload,))
    if paired:
        line = [payload] + [swap(payload, "batch", planes, bit) for bit in (1, 2, 3)]
        *line, clock = tie((*line, clock))
        line = jnp.concatenate(line, axis=0)
        plane = [line] + [fsdp_swap(line, bit) for bit in (2, 4, 6)]
        wd_full, wu_full, clock = hold_weights(
            index, down_pieces, mid_pieces, width, inner, (line, clock)
        )
        *plane, clock = tie((*plane, clock))
        plane = jnp.concatenate(plane, axis=0)
        everyone = [plane, fsdp_swap(plane, 1)]
        layout = (2, ring // 2, planes)
        flip = me * own
    else:
        wd_full, wu_full, clock = hold_weights(index, down_pieces, mid_pieces, width, inner)
        everyone = [lax.all_gather(payload, ("batch", "fsdp"), axis=0, tiled=True)]
        layout = (1, planes * ring, 1)
        flip = jnp.zeros_like(me)
    place = jnp.stack([flip, me * own]).astype(jnp.int32)
    pair_loss, d_pool, _ = contrast(
        place, layout, everyone, payload, pos_col, pooled, stats, (clock,)
    )

    def start(keeps, sends, line):
        return Sum(index, planes, keeps, sends, line) if paired else None

    def go(results, *sums):
        sent, clock = [], results[0]
        for one in sums:
            if one is not None:
                stage = one.next(clock)
                clock = stage[0]
                sent += stage
        if sent:
            results = tie((*results, *sent))[: len(results)]
        return results, tuple(sent)

    d_summed, d_down, sums2, keep_down, send_down, _ = norm2(
        index,
        out_grad.reshape(count, width),
        normed2,
        root2,
        seg_rows,
        rows,
        d_pool,
        activated,
    )
    sum_down = start([keep_down], [send_down], True)
    half, sent = (), ()
    for first in (0, 2):
        half = up_back(
            index, d_down, slope, hidden_turned, wd_full, wu_full, first, 2, tuple(half), sent
        )[:4]
        half, sent = go(half, sum_down)
    d_hidden, sums_up, keep_up, send_up = half
    sum_up = start([keep_up], [send_up], False)
    *first_norm, _ = norm1(
        index,
        [d_hidden],
        d_summed,
        normed1,
        root1,
        rows,
        context,
        sums2,
        sums_up,
        mid_pieces,
        sent,
    )
    (d_attn, d_context, keep_out, send_out), sent = go(first_norm, sum_up)
    pairs = HEADS // 2
    cuts = 3
    backs = []
    for cut in range(cuts):
        *back, _ = attend_back(
            index,
            qkv,
            d_context,
            lse,
            seg_rows,
            tokens_turned,
            cut * pairs // cuts,
            pairs // cuts,
            sent,
        )
        if cut == 0:
            back, sent = go(back, sum_down, sum_up)
            sum_left = start([keep_out, back[3]], [send_out, back[4]], True)
        if cut == 1:
            back, sent = go(back, sum_left)
        if cut == 2:
            sum_right = start([backs[1][3], back[3]], [backs[1][4], back[4]], False)
            back, sent = go(back, sum_down, sum_up, sum_left, sum_right)
        backs.append(back)
    grads = [backs[cut][kind] for kind in range(3) for cut in range(cuts)]
    grad_tokens, _ = input_grad(index, d_attn, grads, qkv_pieces, sent)

    lanes = width // pairs

    part = width // BLOCKS
    if paired:
        (grad_tokens,), sent = go((grad_tokens,), sum_right, sum_down, sum_up)
        _, sent = go(sent, sum_left)
        _, sent = go(sent, sum_right)
        _, sent = go(sent, sum_up, sum_left)
        _, sent = go(sent, sum_right, sum_left)
        go(sent, sum_right)
        grad_down, grad_up = sum_down.result().T, sum_up.result()
        left, right = sum_left.result(), sum_right.result()
        grad_out = left[:part, :width]
        joined = [left[:, width:], right[:, :width], right[:, width:]]
        own_vectors = [left[part, i * TILE : i * TILE + part] for i in range(6)]
        own_vectors.append(left[part + 1, : sizes[-1]])
    else:

        def scatter(keep, send):
            full = lax.psum(jnp.stack([keep, send], axis=1).astype(f32), "batch")
            return full.reshape((BLOCKS,) + full.shape[2:])

        def own_rows(full):
            full = full.reshape((-1,) + full.shape[2:])
            return lax.psum_scatter(full, "fsdp", scatter_dimension=0, tiled=True)

        def own_values(full):
            return lax.psum_scatter(full.reshape(-1), "fsdp", scatter_dimension=0, tiled=True)

        grad_down = own_rows(scatter(keep_down, send_down).transpose(0, 2, 1))
        grad_up = own_rows(scatter(keep_up, send_up))
        left = scatter(keep_out, send_out)
        grad_out = own_rows(left[:, :part])
        own_vectors = [own_values(left[:, part, i * TILE : i * TILE + part]) for i in range(6)]
        own_vectors.append(own_values(left[:, part + 1, : sizes[-1]]))
        whole_grads = [scatter(back[3], back[4]) for back in backs]
        joined = []
        for grads in whole_grads:
            line = lax.psum(jnp.sum(grads[:, part], axis=0), "fsdp")
            joined.append(jnp.concatenate([own_rows(grads[:, :part]), line[None]], axis=0))

    span = width // cuts
    ordered = [
        group[:, kind * span : (kind + 1) * span] for kind in range(3) for group in joined
    ]
    depth = joined[0].shape[0] - 1 if not paired else part
    grad_qkv = jnp.concatenate([group[:depth] for group in ordered], axis=1)
    vector = jnp.concatenate([group[depth] for group in ordered[:cuts] + ordered[2 * cuts :]])
    shard = vector.shape[0] // ring
    grad_bqv = lax.dynamic_slice(vector, (fsdp * shard,), (shard,))
    grad_bout, grad_g1, grad_s1, grad_bdown, grad_g2, grad_s2, grad_bup = own_vectors
    return (
        result.reshape(tokens.shape),
        pair_loss.reshape(own),
        grad_tokens.reshape(tokens.shape),
        grad_qkv,
        grad_bqv,
        grad_out,
        grad_bout,
        grad_g1,
        grad_s1,
        grad_up,
        grad_bup,
        grad_down,
        grad_bdown,
        grad_g2,
        grad_s2,
    )


def solution(mesh):
    rows = P(("batch", "fsdp"), None, None)
    matrix = P("fsdp", None)
    vector = P("fsdp")
    placed = (
        rows,
        P(("batch", "fsdp"), None),
        P(("batch", "fsdp")),
        rows,
        matrix,
        vector,
        matrix,
        vector,
        vector,
        vector,
        matrix,
        vector,
        matrix,
        vector,
        vector,
        vector,
    )
    given = (
        rows,
        P(("batch", "fsdp")),
        rows,
        matrix,
        vector,
        matrix,
        vector,
        vector,
        vector,
        matrix,
        vector,
        matrix,
        vector,
        vector,
        vector,
    )
    return jax.shard_map(
        functools.partial(layer, mesh.shape["batch"], mesh.shape["fsdp"]),
        mesh=mesh,
        in_specs=placed,
        out_specs=given,
        check_vma=False,
    )
```

```python
import functools
import math

import jax
import jax.numpy as jnp
from jax import lax
from jax.experimental import pallas as pl
from jax.experimental.pallas import tpu as pltpu
from jax.sharding import PartitionSpec as P

HEADS = 12
SEGS = 8

norm_eps = 1e-06
pool_eps = 1e-06
score_scale = 50.0
pair_weight = 256.0
masked_value = -1000000000.0

BLOCKS = 8
TILE = 128
TAIL = 128
BASE = 64

bf16 = jnp.bfloat16
f32 = jnp.float32
ANY = pl.BlockSpec(memory_space=pl.ANY)
HELD = pl.BlockSpec(memory_space=pltpu.VMEM)
VMEM_BYTES = 16 * 1024 * 1024


def dot(left, right):
    return jnp.dot(left, right, preferred_element_type=f32)


def dot_nt(left, right):
    return lax.dot_general(left, right, (((1,), (1,)), ((), ())), preferred_element_type=f32)


def whole(shape):
    return pl.BlockSpec(shape, lambda *_: (0,) * len(shape))


def call(
    kernel,
    grid,
    in_specs,
    out_specs,
    out_shape,
    scratch,
    flops,
    moved,
    special=0,
    after=(),
    alias=None,
    near=(),
    room=VMEM_BYTES,
):
    given, extra = len(in_specs) + 1, len(after)
    last = given + extra + len(out_shape)

    def body(*refs):
        refs[last][...] = jnp.zeros_like(refs[last])
        kernel(*refs[:given], *refs[given + extra : last], *refs[last + 1 :])

    shapes = [
        shape if -1 - number in near else pltpu.HBM(shape.shape, shape.dtype)
        for number, shape in enumerate(out_shape)
    ]
    shapes.append(shaped((8, TILE), f32))
    run = pl.pallas_call(
        body,
        out_shape=shapes,
        grid_spec=pltpu.PrefetchScalarGridSpec(
            num_scalar_prefetch=1,
            grid=grid,
            in_specs=in_specs + [ANY] * extra,
            out_specs=out_specs + [whole((8, TILE))],
            scratch_shapes=scratch,
        ),
        input_output_aliases=alias or {},
        compiler_params=pltpu.CompilerParams(vmem_limit_bytes=room),
        cost_estimate=pl.CostEstimate(
            flops=int(flops), bytes_accessed=int(moved), transcendentals=int(special)
        ),
    )

    def apply(index, *operands):
        placed = [
            value if 1 + number in near else pltpu.with_memory_space_constraint(value, pltpu.HBM)
            for number, value in enumerate(operands)
        ]
        return run(index, *placed, *after)

    return apply


def shaped(shape, dtype):
    return jax.ShapeDtypeStruct(shape, dtype)


def swap(value, axis, size, bit):
    return lax.ppermute(value, axis, [(i, i ^ bit) for i in range(size)])


def fsdp_swap(value, bit):
    return swap(value, "fsdp", BLOCKS, bit)


def middle(shard):
    return shard.shape[0] // 32 * 16


def first_stage(shard):
    return fsdp_swap(shard, 2), fsdp_swap(shard, 4)


def second_stage(shard, over_x, over_y):
    half = middle(shard)
    return fsdp_swap(over_y[:half], 2), fsdp_swap(over_x[half:], 4)


def own_pieces(shard, over_x, over_y):
    return [(shard, 0, 0), (over_x, 2, 0), (over_y, 4, 0)]


def far_pieces(shard, far_top, far_low):
    return [(far_top, 6, 0), (far_low, 6, middle(shard))]


def both_cores(pieces):
    return pieces + [(fsdp_swap(value, 1), place ^ 1, off) for value, place, off in pieces]


def gather_whole(shard):
    full = lax.all_gather(shard, "fsdp", axis=0, tiled=True)
    rows = full.shape[0] // BLOCKS
    return [full[i * rows : (i + 1) * rows] for i in range(BLOCKS)]


def meta_of(pieces):
    return tuple((place, off, value.shape[0]) for value, place, off in pieces)


def arrays_of(pieces):
    return [value for value, _, _ in pieces]


def copies_of(
    meta, rows, refs, target, sems, index, source=None, place=None, first=0
):
    copies = []
    for number, ((block, off, count), ref) in enumerate(zip(meta, refs)):
        low, high = max(off, first), min(off + count, first + rows)
        if low >= high:
            continue
        here = pl.ds(pl.multiple_of((index ^ block) * rows + low - first, 16), high - low)
        part = ref.at[low - off : high - off]
        copies.append(
            pltpu.make_async_copy(
                part if source is None else part.at[:, source],
                target.at[here] if place is None else target.at[here, place],
                sems.at[number],
            )
        )
    return copies


def pair_copies(meta, size, refs, target, sems, index, chip):
    copies = []
    for number, ((block, off, count), ref) in enumerate(zip(meta, refs)):
        if block // 2 == chip:
            start = pl.multiple_of((index ^ block) * size + off, 16)
            copies.append(
                pltpu.make_async_copy(ref, target.at[pl.ds(start, count)], sems.at[number])
            )
    return copies


def start_all(copies):
    for copy in copies:
        copy.start()


def wait_all(copies):
    for copy in copies:
        copy.wait()


def columns(number, size, base=0):
    return pl.ds(pl.multiple_of(base + number * size, TILE), size)


def fill_mask(seg_row, mask_ref):
    length = seg_row.shape[1]
    keys = jnp.broadcast_to(seg_row, (TILE, length)).T
    for lo, hi, at in bands(length):
        same = keys[lo:hi] == seg_row[:, at : at + TILE]
        mask_ref[lo:hi, at : at + TILE] = jnp.where(same, 0.0, masked_value)


def bands(length):
    out = []
    for at in range(0, length, TILE):
        out.append((max(at - TILE, 0), min(at + 2 * TILE, length), at))
    return out


def two_heads(pair):
    lane = lax.broadcasted_iota(jnp.int32, (1, pair.shape[1]), 1)
    first = (lane < pair.shape[1] // 2).astype(f32).astype(bf16)
    return jnp.concatenate([pair * first, pair * (1.0 - first)], axis=0)


def twice(value):
    return jnp.concatenate([value, value], axis=1)


def pack_line(vectors, width):
    line = jnp.concatenate([jnp.pad(v, (0, -v.shape[0] % TILE)) for v in vectors])
    return jnp.pad(line[None], ((0, 15), (0, width - line.shape[0])))


def pack_first(w_qkv, b_qv):
    return jnp.concatenate([w_qkv, pack_line([b_qv], w_qkv.shape[1])], axis=0)


def pack_second(w_out, w_up, *vectors):
    both = jnp.concatenate([w_out, w_up], axis=1)
    return jnp.concatenate([both, pack_line(vectors, both.shape[1])], axis=0)


def table_of(lines):
    line = lax.broadcasted_iota(jnp.int32, (BLOCKS, 16 * BLOCKS), 0) * 16
    pick = line == lax.broadcasted_iota(jnp.int32, (BLOCKS, 16 * BLOCKS), 1)
    return dot(pick.astype(f32).astype(bf16), lines)


def spread(table, at, size):
    count = table.shape[0]
    padded = size + -size % TILE
    block = table[:, at : at + padded].astype(bf16)
    col = lax.broadcasted_iota(jnp.int32, (1, count * size), 1)
    owner = col // size
    place = lax.broadcasted_iota(jnp.int32, (padded, count * size), 0) == col - owner * size
    value = dot(block, place.astype(f32).astype(bf16))
    keep = lax.broadcasted_iota(jnp.int32, value.shape, 0) == owner
    return jnp.sum(jnp.where(keep, value, 0.0), axis=0, keepdims=True), at + padded


def qkv_kernel(meta, size, index_ref, tok_ref, *rest):
    pieces, rest = rest[: len(meta)], rest[len(meta) :]
    qkv_ref, w_ref, small_ref, bias_ref, sems, small_sems = rest
    width = tok_ref.shape[1]
    rows = width // BLOCKS
    part = pl.program_id(0)
    index = index_ref[0]

    def weights(number):
        cols = columns(number, width)
        return copies_of(meta, rows, pieces, w_ref, sems.at[number], index, cols, cols)

    @pl.when(part == 0)
    def _():
        here = slice(0, small_ref.shape[1])
        small = copies_of(meta, 16, pieces, small_ref, small_sems, index, here, None, rows)
        start_all(small)
        for number in range(3):
            start_all(weights(number))
        wait_all(small)
        bias, _ = spread(table_of(small_ref[...]), 0, size)
        bias_ref[0] = bias[:, :width]
        bias_ref[1] = jnp.zeros((1, width), f32)
        bias_ref[2] = bias[:, width:]

    wait_all(weights(part))
    scale = jnp.where(part == 0, 1.0 / math.sqrt(width // HEADS), 1.0)
    value = dot(tok_ref[...], w_ref[:, columns(part, width)]) + bias_ref[part]
    qkv_ref[...] = (value * scale).astype(bf16)


def project_qkv(index, tokens, pieces, size):
    count, width = tokens.shape
    meta = meta_of(pieces)
    out = pl.BlockSpec((count, width), lambda i, s: (0, i))
    return call(
        functools.partial(qkv_kernel, meta, size),
        (3,),
        [whole((count, width))] + [ANY] * len(meta),
        [out],
        [shaped((count, 3 * width), bf16)],
        [
            pltpu.VMEM((width, 3 * width), bf16),
            pltpu.VMEM((16 * BLOCKS, size + -size % TILE), bf16),
            pltpu.VMEM((3, 1, width), f32),
            pltpu.SemaphoreType.DMA((3, len(meta))),
            pltpu.SemaphoreType.DMA((len(meta),)),
        ],
        count * width * width * 6,
        count * width * 8 + width * width * 6,
        near=(-1,),
    )(index, tokens, *arrays_of(pieces))


def attend_kernel(index_ref, qkv_ref, seg_ref, *rest):
    ctx_ref, lse_ref, vt_ref, ct_ref, mask_ref = rest[-5:]
    length, width = ctx_ref.shape
    pairs = HEADS // 2
    lanes = width // pairs
    half = lanes // 2
    fill_mask(seg_ref[0].astype(f32), mask_ref)
    vt_ref[...] = qkv_ref[:, 2 * width :].T

    tiles = [(pair, band) for pair in range(pairs) for band in bands(length)]

    def scores_of(tile):
        pair, (lo, hi, at) = tile
        queries = two_heads(qkv_ref[at : at + TILE, pair * lanes : (pair + 1) * lanes])
        keys = qkv_ref[lo:hi, width + pair * lanes : width + (pair + 1) * lanes]
        return dot_nt(keys, queries)

    def probs_of(tile, scores):
        pair, (lo, hi, at) = tile
        scores = scores + twice(mask_ref[lo:hi, at : at + TILE])
        top = jnp.max(scores, axis=0, keepdims=True)
        terms = jnp.exp(scores - top)
        total = jnp.sum(terms, axis=0, keepdims=True)
        lse = top + jnp.log(total)
        for head in range(2):
            lse_ref[0, pair, head : head + 1, at : at + TILE] = lse[:, head * TILE : (head + 1) * TILE]
        return (terms * (1.0 / total)).astype(bf16)

    def put_context(tile, probs):
        pair, (lo, hi, at) = tile
        context = dot(vt_ref[pair * lanes : (pair + 1) * lanes, lo:hi], probs)
        for head in range(2):
            rows = slice(pair * lanes + head * half, pair * lanes + (head + 1) * half)
            part = context[head * half : (head + 1) * half, head * TILE : (head + 1) * TILE]
            ct_ref[rows, at : at + TILE] = part.astype(bf16)

    ready = {}
    probs = {}
    for step in range(len(tiles) + 2):
        if step < len(tiles):
            ready[step] = scores_of(tiles[step])
        if 0 <= step - 1 < len(tiles):
            probs[step - 1] = probs_of(tiles[step - 1], ready.pop(step - 1))
        if 0 <= step - 2:
            put_context(tiles[step - 2], probs.pop(step - 2))
    ctx_ref[...] = ct_ref[...].T


def attend(index, qkv, seg_rows, row, before=(), after=()):
    count, width = qkv.shape[0], qkv.shape[1] // 3
    rows, _, length = seg_rows.shape
    pairs = HEADS // 2
    return call(
        attend_kernel,
        (1,),
        [
            pl.BlockSpec((length, 3 * width), lambda i, s: (row, 0)),
            pl.BlockSpec((1, 1, length), lambda i, s: (row, 0, 0)),
        ]
        + [ANY] * len(before),
        [
            pl.BlockSpec((length, width), lambda i, s: (row, 0)),
            pl.BlockSpec((1, pairs, 2, length), lambda i, s: (row, 0, 0, 0)),
        ],
        [
            shaped((count, width), bf16),
            shaped((rows, pairs, 2, length), f32),
        ],
        [
            pltpu.VMEM((width, length), bf16),
            pltpu.VMEM((width, length), bf16),
            pltpu.VMEM((length, length), f32),
        ],
        length * length * width * 4,
        length * width * 8,
        length * length * HEADS * 5 // 8,
        after,
        {3 + i: i for i in range(len(before))},
        (1, -1, -2) + ((3, 4) if before else ()),
    )(index, qkv, seg_rows, *before)


def row_stats(values):
    mean = jnp.mean(values, axis=-1, keepdims=True)
    centred = values - mean
    spread = jnp.mean(centred * centred, axis=-1, keepdims=True)
    return centred, lax.rsqrt(spread + norm_eps)


def project_kernel(meta, sizes, index_ref, ctx_ref, tok_ref, *rest):
    pieces, rest = rest[: len(meta)], rest[len(meta) :]
    norm_ref, root_ref, hid_ref, vec_ref, up_ref, w_ref, small_ref, sems, small_sems = rest
    width = w_ref.shape[0]

    @pl.when(pl.program_id(0) == 0)
    def _():
        rows = width // BLOCKS
        here = slice(0, width)
        copies = copies_of(meta, rows, pieces, w_ref, sems, index_ref[0], here, here)
        line = slice(0, small_ref.shape[1])
        small = copies_of(meta, 16, pieces, small_ref, small_sems, index_ref[0], line, None, rows)
        start_all(small)
        start_all(copies)
        vec_ref[...] = jnp.zeros_like(vec_ref)
        wait_all(small)
        table = table_of(small_ref[...])
        line, at = 0, 0
        for size in sizes:
            value, at = spread(table, at, size)
            if value.shape[1] == width:
                vec_ref[line : line + 1] = value
                line += 1
            else:
                up_ref[...] = value
        wait_all(copies)

    def finish(here, product):
        summed = tok_ref[here].astype(f32) + (product + vec_ref[0:1])
        centred, root = row_stats(summed)
        normed = centred * root
        norm_ref[here] = normed
        root_ref[here] = root
        hid_ref[here] = (normed * vec_ref[1:2] + vec_ref[2:3]).astype(bf16)

    in_turn(ctx_ref.shape[0], lambda here: dot(ctx_ref[here], w_ref[...]), finish)


def in_turn(count, begin, finish, size=2 * TILE):
    last = None
    for at in range(0, count, size):
        here = slice(at, at + size)
        value = begin(here)
        if last is not None:
            finish(*last)
        last = (here, value)
    finish(*last)


def project(index, context, tokens, pieces, sizes, after=(), step=512):
    count, width = tokens.shape
    inner = 4 * width
    used = sum(size + -size % TILE for size in sizes)
    meta = meta_of(pieces)
    rows = pl.BlockSpec((step, width), lambda i, s: (i, 0))
    return call(
        functools.partial(project_kernel, meta, sizes),
        (count // step,),
        [rows, rows] + [ANY] * len(meta),
        [
            rows,
            pl.BlockSpec((step, 1), lambda i, s: (i, 0)),
            rows,
            whole((SEGS, width)),
            whole((1, inner)),
        ],
        [
            shaped((count, width), f32),
            shaped((count, 1), f32),
            shaped((count, width), bf16),
            shaped((SEGS, width), f32),
            shaped((1, inner), f32),
        ],
        [
            pltpu.VMEM((width, width), bf16),
            pltpu.VMEM((16 * BLOCKS, used), bf16),
            pltpu.SemaphoreType.DMA((len(meta),)),
            pltpu.SemaphoreType.DMA((len(meta),)),
        ],
        count * width * width * 2,
        count * width * 10 + width * width * 2,
        0,
        after,
        near=(1, -3, -4, -5),
    )(index, context, tokens, *arrays_of(pieces))


def gelu_parts(value):
    share = 0.5 * lax.erf(value * math.sqrt(0.5)) + 0.5
    bell = jnp.exp2(value * value * (-0.5 / math.log(2.0)))
    return value * share, share + value * bell * (1.0 / math.sqrt(2.0 * math.pi))


def up_kernel(meta, index_ref, hid_ref, bias_ref, *rest):
    pieces, rest = rest[: len(meta)], rest[len(meta) :]
    act_ref, slope_ref, w_ref, sems = rest
    tile = act_ref.shape[1]
    width = w_ref.shape[0]
    step = pl.program_id(0)

    def weights(number):
        source, place = columns(number, tile, width), columns(number, tile)
        rows = width // BLOCKS
        return copies_of(meta, rows, pieces, w_ref, sems.at[number], index_ref[0], source, place)

    @pl.when(step == 0)
    def _():
        for number in range(sems.shape[0]):
            start_all(weights(number))

    wait_all(weights(step))
    wide = 256

    def begin(cols):
        here = pl.ds(pl.multiple_of(step * tile + cols.start, wide), wide)
        return dot(hid_ref[...], w_ref[:, here]) + bias_ref[:, cols]

    def finish(cols, value):
        act, slope = gelu_parts(value)
        act_ref[:, cols] = act.astype(bf16)
        slope_ref[:, cols] = slope.astype(bf16)

    in_turn(tile, begin, finish, wide)


def up(index, hidden, bias, pieces, after=(), tile=768):
    count, width = hidden.shape
    inner = bias.shape[1]
    meta = meta_of(pieces)
    out = pl.BlockSpec((count, tile), lambda i, s: (0, i))
    return call(
        functools.partial(up_kernel, meta),
        (inner // tile,),
        [HELD, pl.BlockSpec((1, tile), lambda i, s: (0, i))] + [ANY] * len(meta),
        [out, out],
        [shaped((count, inner), bf16)] * 2,
        [
            pltpu.VMEM((width, inner), bf16),
            pltpu.SemaphoreType.DMA((inner // tile, len(meta))),
        ],
        count * width * inner * 2,
        count * (width * 2 + inner * 4) + width * inner * 2,
        count * inner * 4,
        after,
        near=(1, 2),
    )(index, hidden, bias, *arrays_of(pieces))


def down_kernel(meta, index_ref, act_ref, norm_ref, vec_ref, seg_ref, pos_ref, *rest):
    pieces, rest = rest[: len(meta)], rest[len(meta) :]
    res_ref, norm2_ref, root_ref, pay_ref, pool_ref, stat_ref, *rest = rest
    w_ref, held_ref, sum_ref, num_ref, sems, act_sems = rest
    step, steps = pl.program_id(0), pl.num_programs(0)
    length, width = res_ref.shape
    tile = w_ref.shape[0] // 4
    index = index_ref[0]

    def weights(chip):
        return pair_copies(meta, tile // 2, pieces, w_ref, sems, index, chip)

    def inputs(row, chip):
        rows = pl.ds(pl.multiple_of(row * length, length), length)
        source = act_ref.at[rows, columns((index // 2) ^ chip, tile)]
        return pltpu.make_async_copy(source, held_ref.at[row, chip], act_sems.at[row, chip])

    @pl.when(step == 0)
    def _():
        inputs(0, 0).start()
        start_all(weights(0))

    wanted = lax.broadcasted_iota(jnp.int32, (SEGS, length), 0)
    member = (wanted == seg_ref[0]).astype(f32)
    product = None
    for chip in range(4):
        inputs(step, chip).wait()

        @pl.when(step == 0)
        def _():
            wait_all(weights(chip))
            if chip < 3:
                inputs(0, chip + 1).start()
                start_all(weights(chip + 1))
            else:
                for other in range(4):
                    inputs(1, other).start()

        value = dot(held_ref[step, chip], w_ref[columns((index // 2) ^ chip, tile)])
        product = value if product is None else product + value
    hidden = norm_ref[...] * vec_ref[1:2] + vec_ref[2:3]
    summed = hidden + (product + vec_ref[3:4])
    centred, root = row_stats(summed)
    normed = centred * root
    result = normed * vec_ref[4:5] + vec_ref[5:6]
    norm2_ref[...] = normed
    root_ref[...] = root
    high = result.astype(bf16)
    res_ref[...] = high
    low = (result - high.astype(f32)).astype(bf16)
    own = pl.ds(pl.multiple_of(step * SEGS, SEGS), SEGS)
    member_b = member.astype(bf16)
    sum_ref[own] = dot(member_b, high) + dot(member_b, low)
    num_ref[own] = jnp.broadcast_to(jnp.sum(member, axis=1, keepdims=True), (SEGS, TAIL))

    @pl.when(step == steps - 1)
    def _():
        counts = num_ref[:, 0:1]
        pooled = sum_ref[...] / counts
        scale = lax.rsqrt(jnp.mean(pooled * pooled, axis=-1, keepdims=True) + pool_eps)
        pool_ref[...] = pooled
        lane = lax.broadcasted_iota(jnp.int32, (pooled.shape[0], TAIL), 1)
        stat_ref[...] = jnp.where(lane == 0, scale, counts)
        pay_ref[:, :width] = (pooled * scale).astype(bf16)
        partner = pos_ref[...]
        digit = jnp.where(lane == 0, partner // BASE, partner % BASE)
        pay_ref[:, width:] = jnp.where(lane < 2, digit, 0).astype(f32).astype(bf16)


def down(index, activated, normed, vectors, seg_rows, positive, pieces, after=()):
    count, width = normed.shape
    inner = activated.shape[1]
    rows, _, step = seg_rows.shape
    own = rows * SEGS
    meta = meta_of(pieces)
    block = pl.BlockSpec((step, width), lambda i, s: (i, 0))
    return call(
        functools.partial(down_kernel, meta),
        (count // step,),
        [
            ANY,
            block,
            whole(vectors.shape),
            pl.BlockSpec((1, 1, step), lambda i, s: (i, 0, 0)),
            whole((own, 1)),
        ]
        + [ANY] * len(meta),
        [
            block,
            block,
            pl.BlockSpec((step, 1), lambda i, s: (i, 0)),
            whole((own, width + TAIL)),
            whole((own, width)),
            whole((own, TAIL)),
        ],
        [
            shaped((count, width), bf16),
            shaped((count, width), f32),
            shaped((count, 1), f32),
            shaped((own, width + TAIL), bf16),
            shaped((own, width), f32),
            shaped((own, TAIL), f32),
        ],
        [
            pltpu.VMEM((inner, width), bf16),
            pltpu.VMEM((rows, 4, step, inner // 4), bf16),
            pltpu.VMEM((own, width), f32),
            pltpu.VMEM((own, TAIL), f32),
            pltpu.SemaphoreType.DMA((len(meta),)),
            pltpu.SemaphoreType.DMA((rows, 4)),
        ],
        count * width * inner * 2,
        count * (width * 10 + inner * 2) + width * inner * 2,
        after=after,
        near=(3, 5, -4, -5, -6),
        room=24 * 1024 * 1024,
    )(index, activated, normed, vectors, seg_rows, positive, *arrays_of(pieces))


def segment_of(row, own, cores, chips, planes):
    block = row // own
    plane, chip, core = block % planes, block // planes % chips, block // (planes * chips)
    return ((plane * chips + chip) * cores + core) * own + row % own


def contrast_kernel(layout, place_ref, own_ref, pos_ref, pool_ref, stat_ref, *rest):
    pieces, (loss_ref, grad_ref, all_ref, sems) = rest[:-4], rest[-4:]
    copies, at = [], 0
    for number, piece in enumerate(pieces):
        here = all_ref.at[at : at + piece.shape[0]]
        copies.append(pltpu.make_async_copy(piece, here, sems.at[number]))
        at += piece.shape[0]
    for copy in copies:
        copy.start()
    for copy in copies:
        copy.wait()
    total = all_ref.shape[0]
    own, width = pool_ref.shape
    factor = score_scale / width
    block = min(total, 512)
    flip, first = place_ref[0], place_ref[1]
    mine = own_ref[:, :width]
    mine_id = lax.broadcasted_iota(jnp.int32, (own, total), 0) + first
    other_id = segment_of(lax.broadcasted_iota(jnp.int32, (1, total), 1), own, *layout) ^ flip
    logits = dot_nt(mine, all_ref[:, :width]) * factor
    logits = jnp.where(mine_id == other_id, masked_value, logits)
    top = jnp.max(logits, axis=1, keepdims=True)
    log_own = top + jnp.log(jnp.sum(jnp.exp(logits - top), axis=1, keepdims=True))
    is_positive = other_id == pos_ref[...]
    picked = jnp.sum(jnp.where(is_positive, logits, 0.0), axis=1, keepdims=True)
    loss_ref[...] = log_own - picked
    d_logits = pair_weight * (jnp.exp(logits - log_own) - is_positive.astype(f32))
    d_emb = dot(d_logits.astype(bf16), all_ref[:, :width])
    lane = lax.broadcasted_iota(jnp.int32, (SEGS, TAIL), 1)
    digits = jnp.where(lane == 0, float(BASE), jnp.where(lane == 1, 1.0, 0.0)).astype(bf16)
    for at in range(0, total, block):
        rows = slice(at, at + block)
        table = dot_nt(all_ref[:, :width], all_ref[rows, :width]) * factor
        left = lax.broadcasted_iota(jnp.int32, (total, block), 0)
        right = lax.broadcasted_iota(jnp.int32, (total, block), 1) + at
        table = jnp.where(left == right, masked_value, table)
        top = jnp.max(table, axis=0, keepdims=True)
        log_all = top + jnp.log(jnp.sum(jnp.exp(table - top), axis=0, keepdims=True))
        partner = dot_nt(digits, all_ref[rows, width:])[0:1].astype(jnp.int32)
        chosen = partner == mine_id[:, rows]
        back = pair_weight * (jnp.exp(logits[:, rows] - log_all) - chosen.astype(f32))
        d_emb += dot(back.astype(bf16), all_ref[rows, :width])
    d_emb = d_emb * factor
    scale, counts = stat_ref[:, 0:1], stat_ref[:, 1:2]
    pooled = pool_ref[...]
    along = jnp.mean(d_emb * pooled, axis=-1, keepdims=True)
    grad_ref[...] = (d_emb * scale - pooled * (scale * scale * scale * along)) / counts


def contrast(place, layout, everyone, payload, positive, pooled, stats, after=()):
    own, width = pooled.shape
    total = sum(v.shape[0] for v in everyone)
    return call(
        functools.partial(contrast_kernel, layout),
        (1,),
        [whole(v.shape) for v in (payload, positive, pooled, stats)] + [ANY] * len(everyone),
        [whole((own, 1)), whole((own, width))],
        [shaped((own, 1), f32), shaped((own, width), f32)],
        [
            pltpu.VMEM((total, width + TAIL), bf16),
            pltpu.SemaphoreType.DMA((len(everyone),)),
        ],
        total * total * width * 2,
        total * width * 2,
        total * total,
        after=after,
        near=(1, 2, 3, 4, -1, -2),
    )(place, payload, positive, pooled, stats, *everyone)


def norm_back(d_out, normed, root, gain):
    scaled = d_out * gain
    mean = jnp.mean(scaled, axis=-1, keepdims=True)
    along = jnp.mean(scaled * normed, axis=-1, keepdims=True)
    return root * (scaled - mean - normed * along)


def column_sum(values):
    return jnp.sum(values, axis=0, keepdims=True)


def norm2_kernel(turns, index_ref, og_ref, norm_ref, root_ref, seg_ref, vec_in_ref, dp_ref, *rest):
    act_ref, dsum_ref, ddown_ref, vec_ref, keep_ref, send_ref, dt_ref = rest
    step = pl.program_id(0)
    chunk, width = og_ref.shape
    own = dp_ref.shape[0]

    @pl.when(step == 0)
    def _():
        vec_ref[...] = jnp.zeros_like(vec_ref)

    @pl.when(step < turns)
    def _():
        row = step // (turns * SEGS // own)
        pool = dp_ref[pl.ds(pl.multiple_of(row * SEGS, SEGS), SEGS)]
        high = pool.astype(bf16)
        left = pool - high.astype(f32)
        mid = left.astype(bf16)
        low = (left - mid.astype(f32)).astype(bf16)
        pad = jnp.zeros((TILE - 3 * SEGS, width), bf16)
        table = jnp.concatenate([high, mid, low, pad], axis=0)
        lane = lax.broadcasted_iota(jnp.int32, (chunk, TILE), 1) % SEGS
        keys = jnp.broadcast_to(seg_ref[0].astype(f32), (TILE, chunk)).T
        member = (lane.astype(f32) == keys).astype(f32).astype(bf16)

        def begin(here):
            return dot(member[here], table)

        def finish(here, shared):
            d_res = og_ref[here].astype(f32) + shared
            normed = norm_ref[here]
            d_sum = norm_back(d_res, normed, root_ref[here], vec_in_ref[4:5])
            d_down = d_sum.astype(bf16)
            dsum_ref[here] = d_sum
            ddown_ref[here] = d_down
            cols = pl.ds(pl.multiple_of(step * chunk + here.start, TILE), TILE)
            dt_ref[:, cols] = d_down.T
            vec_ref[0:1] += column_sum(d_down.astype(f32))
            vec_ref[1:2] += column_sum(d_res * normed)
            vec_ref[2:3] += column_sum(d_res)

        in_turn(chunk, begin, finish, TILE)

    @pl.when(step >= turns)
    def _():
        grad = dot(dt_ref[...], act_ref[...]).astype(bf16)
        half = grad.shape[1] // 2
        odd = index_ref[0] % 2 == 1
        keep_ref[0] = jnp.where(odd, grad[:, half:], grad[:, :half])
        send_ref[0] = jnp.where(odd, grad[:, :half], grad[:, half:])


def norm2(index, out_grad, normed, root, seg_rows, vectors, d_pool, activated, turns=4):
    count, width = out_grad.shape
    inner = activated.shape[1]
    tile = inner // 4
    own = d_pool.shape[0]
    first = lambda i: jnp.minimum(i, turns - 1)
    then = lambda i: jnp.maximum(i - turns, 0)
    split = turns // seg_rows.shape[0]
    block = pl.BlockSpec((count // turns, width), lambda i, s: (first(i), 0))
    column = pl.BlockSpec((count // turns, 1), lambda i, s: (first(i), 0))
    grads = pl.BlockSpec((1, width, tile // 2), lambda i, s: (then(i), 0, 0))
    return call(
        functools.partial(norm2_kernel, turns),
        (turns + 4,),
        [
            block,
            block,
            column,
            pl.BlockSpec((1, 1, count // turns), lambda i, s: (first(i) // split, 0, first(i) % split)),
            whole(vectors.shape),
            whole((own, width)),
            pl.BlockSpec((count, tile), lambda i, s: (0, (s[0] // 2) ^ then(i))),
        ],
        [block, block, whole((SEGS, width)), grads, grads],
        [
            shaped((count, width), f32),
            shaped((count, width), bf16),
            shaped((SEGS, width), f32),
            shaped((4, width, tile // 2), bf16),
            shaped((4, width, tile // 2), bf16),
        ],
        [pltpu.VMEM((width, count), bf16)],
        count * width * inner * 2,
        count * (width * 12 + inner * 2) + width * inner * 2,
        near=(5, 6, -1, -2, -3, -4, -5),
    )(index, out_grad, normed, root, seg_rows, vectors, d_pool, activated)


def put_turned(source_ref, target_ref, turn_ref, index):
    turn_ref[...] = source_ref[...].T
    rows = turn_ref.shape[0] // BLOCKS
    for place in range(BLOCKS):
        block = index ^ ((place % 4) * 2 + place // 4)
        start = pl.multiple_of(block * rows, 16)
        target_ref[place * rows : (place + 1) * rows] = turn_ref[pl.ds(start, rows)]


def weights_kernel(meta, base, index_ref, *refs):
    pieces, (out_ref, sems) = refs[:-2], refs[-2:]
    height, width = out_ref.shape
    here = slice(base, base + width)
    copies = copies_of(meta, height // BLOCKS, pieces, out_ref, sems, index_ref[0], here)
    start_all(copies)
    wait_all(copies)


def hold_weights(index, pieces, shape, base, after=()):
    meta = meta_of(pieces)
    return call(
        functools.partial(weights_kernel, meta, base),
        (1,),
        [ANY] * len(meta),
        [HELD],
        [shaped(shape, bf16)],
        [pltpu.SemaphoreType.DMA((len(meta),))],
        0,
        shape[0] * shape[1] * 4,
        0,
        after,
        near=(-1,),
    )(index, *arrays_of(pieces))


def turned_kernel(index_ref, one_ref, two_ref, out_one_ref, out_two_ref, turn_ref):
    put_turned(one_ref, out_one_ref, turn_ref, index_ref[0])
    put_turned(two_ref, out_two_ref, turn_ref, index_ref[0])


def hold_turned(index, one, two, after=()):
    count, width = one.shape
    return call(
        turned_kernel,
        (1,),
        [whole((count, width))] * 2,
        [HELD, HELD],
        [shaped((width, count), bf16)] * 2,
        [pltpu.VMEM((width, count), bf16)],
        0,
        count * width * 8,
        0,
        after,
        near=(-1, -2),
    )(index, one, two)


def up_back_kernel(first, before, index_ref, ddown_ref, slope_ref, ht_ref, wd_ref, wu_ref, *rest):
    earlier, rest = rest[:before], rest[before:]
    dhid_ref, bias_ref, keep_ref, send_ref = rest
    step = pl.program_id(0)
    tile = slope_ref.shape[1]
    width = ht_ref.shape[0]
    here = columns((index_ref[0] // 2) ^ (step + first), tile)
    wide = 256
    parts = []

    def begin(cols):
        rows = pl.ds(pl.multiple_of(here.start + cols.start, wide), wide)
        return dot_nt(ddown_ref[...], wd_ref[rows])

    def finish(cols, d_act):
        d_up = (d_act * slope_ref[:, cols].astype(f32)).astype(bf16)
        bias_ref[:, cols] = column_sum(d_up.astype(f32))
        parts.append(d_up)

    in_turn(tile, begin, finish, wide)
    d_up = jnp.concatenate(parts, axis=1)
    grad = dot(ht_ref[...], d_up).astype(bf16)
    half = width // 2
    keep_ref[...] = grad[:half].reshape(keep_ref.shape)
    send_ref[...] = grad[half:].reshape(send_ref.shape)
    share = dot_nt(d_up, wu_ref[:, here])

    @pl.when(step == 0)
    def _():
        dhid_ref[...] = earlier[0][...] + share if earlier else share

    @pl.when(step > 0)
    def _():
        dhid_ref[...] += share


def up_back(index, d_down, slope, turned, w_down, w_up, first, steps, before=(), after=()):
    count, width = d_down.shape
    inner = slope.shape[1]
    tile = inner // 4
    part = width // BLOCKS
    place = lambda i, s: (s[0] // 2) ^ (i + first)
    grads = pl.BlockSpec((4, part, tile), lambda i, s: (0, 0, place(i, s)))
    return call(
        functools.partial(up_back_kernel, first, len(before)),
        (steps,),
        [HELD, pl.BlockSpec((count, tile), lambda i, s: (0, place(i, s))), HELD, HELD, HELD]
        + ([HELD] + [ANY] * 3 if before else []),
        [HELD, pl.BlockSpec((1, tile), lambda i, s: (0, place(i, s))), grads, grads],
        [
            shaped((count, width), f32),
            shaped((1, inner), f32),
            shaped((4, part, inner), bf16),
            shaped((4, part, inner), bf16),
        ],
        [],
        count * width * tile * 6 * steps,
        count * (width * 8 + inner) + width * inner * 6,
        0,
        after,
        {6 + i: i for i in range(len(before))},
        (1, 3, 4, 5, 6, 7, 8, 9, -1, -2, -3, -4),
    )(index, d_down, slope, turned, w_down, w_up, *before)


def cut_vector(vector, size, index):
    width = vector.shape[1]
    owner = lax.broadcasted_iota(jnp.int32, (BLOCKS, width), 1) // size
    wanted = lax.broadcasted_iota(jnp.int32, (BLOCKS, width), 0) ^ index
    rows = jnp.where(owner == wanted, vector, 0.0).astype(bf16)
    source = lax.broadcasted_iota(jnp.int32, (width, 1), 0)
    place = source - source // size * size == lax.broadcasted_iota(jnp.int32, (width, TILE), 1)
    return dot(rows, place.astype(f32).astype(bf16))


def norm1_kernel(meta, parts, index_ref, *rest):
    dhids, rest = rest[:parts], rest[parts:]
    dsum_ref, norm_ref, root_ref, gain_ref, ctx_ref, other_ref, up_ref, *rest = rest
    pieces, rest = rest[: len(meta)], rest[len(meta) :]
    dattn_ref, dctx_ref, keep_ref, send_ref, w_ref, acc_ref, vec_ref, sems = rest
    step = pl.program_id(0)
    width = w_ref.shape[0]
    rows = width // BLOCKS

    @pl.when(step == 0)
    def _():
        here = slice(0, width)
        copies = copies_of(meta, rows, pieces, w_ref, sems, index_ref[0], here, here)
        start_all(copies)
        vec_ref[...] = jnp.zeros_like(vec_ref)
        acc_ref[...] = jnp.zeros_like(acc_ref)
        wait_all(copies)

    parts = []

    def begin(here):
        d_hid = dsum_ref[here]
        for dhid_ref in dhids:
            d_hid = d_hid + dhid_ref[here]
        normed = norm_ref[here]
        d_sum = norm_back(d_hid, normed, root_ref[here], gain_ref[1:2])
        d_attn = d_sum.astype(bf16)
        dattn_ref[here] = d_sum
        vec_ref[0:1] += column_sum(d_attn.astype(f32))
        vec_ref[1:2] += column_sum(d_hid * normed)
        vec_ref[2:3] += column_sum(d_hid)
        parts.append(d_attn)
        return d_attn

    def finish(here, d_attn):
        dctx_ref[here] = dot_nt(d_attn, w_ref[...]).astype(bf16)

    in_turn(dsum_ref.shape[0], begin, finish)
    acc_ref[...] += dot(ctx_ref[...].T, jnp.concatenate(parts, axis=0))

    @pl.when(step == pl.num_programs(0) - 1)
    def _():
        index = index_ref[0]
        vectors = [vec_ref[i : i + 1] for i in range(3)] + [other_ref[i : i + 1] for i in range(3)]
        top = [cut_vector(vector, rows, index) for vector in vectors]
        top = jnp.concatenate(top, axis=1)
        size = up_ref.shape[1] // BLOCKS
        line = lax.broadcasted_iota(jnp.int32, (16, width), 0)
        pad = jnp.zeros((1, width - size), f32)
        for place in range(4):
            for target, core in ((keep_ref, 0), (send_ref, 1)):
                number = 2 * place + core
                block = index ^ number
                start = pl.multiple_of(block * rows, 16)
                target[place, :rows] = acc_ref[pl.ds(start, rows)].astype(bf16)
                low = up_ref[:, pl.ds(pl.multiple_of(block * size, size), size)]
                low = jnp.concatenate([low, pad], axis=1)
                extra = jnp.where(line == 0, top[number : number + 1], 0.0)
                extra = jnp.where(line == 1, low, extra)
                target[place, rows:] = extra.astype(bf16)


def norm1(
    index, d_hiddens, d_summed, normed, root, gain, context, sums, sums_up, pieces, after=(), step=512
):
    count, width = d_summed.shape
    meta = meta_of(pieces)
    part = width // BLOCKS + 16
    block = pl.BlockSpec((step, width), lambda i, s: (i, 0))
    return call(
        functools.partial(norm1_kernel, meta, len(d_hiddens)),
        (count // step,),
        [block] * len(d_hiddens)
        + [
            block,
            block,
            pl.BlockSpec((step, 1), lambda i, s: (i, 0)),
            whole(gain.shape),
            block,
            whole(sums.shape),
            whole(sums_up.shape),
        ]
        + [ANY] * len(meta),
        [block, block, whole((4, part, width)), whole((4, part, width))],
        [
            shaped((count, width), f32),
            shaped((count, width), bf16),
            shaped((4, part, width), bf16),
            shaped((4, part, width), bf16),
        ],
        [
            pltpu.VMEM((width, width), bf16),
            pltpu.VMEM((width, width), f32),
            pltpu.VMEM((SEGS, width), f32),
            pltpu.SemaphoreType.DMA((len(meta),)),
        ],
        count * width * width * 4,
        count * width * 20 + width * width * 4,
        0,
        after,
        near=tuple(range(1, 2 + len(d_hiddens))) + (6, 7, 8, -1, -2, -3, -4),
    )(
        index, *d_hiddens, d_summed, normed, root, gain, context, sums, sums_up, *arrays_of(pieces)
    )


def attend_back_kernel(
    first, index_ref, q_ref, k_ref, v_ref, dctx_ref, lse_ref, seg_ref, tt_ref, *rest
):
    dq_ref, dk_ref, dv_ref, keep_ref, send_ref = rest[:5]
    mask_ref, kt_ref, two_ref, pt_ref, both_ref = rest[5:]
    rows, _, length = seg_ref.shape
    lanes = 2 * tt_ref.shape[0] // HEADS
    half = lanes // 2
    group = q_ref.shape[1] // lanes
    inv_root = 1.0 / math.sqrt(half)

    @pl.when(pl.program_id(0) == 0)
    def _():
        for row in range(rows):
            fill_mask(seg_ref[row].astype(f32), mask_ref.at[row])

    tiles = [
        (pair, row, band) for pair in range(group) for row in range(rows) for band in bands(length)
    ]
    for pair in range(group):
        for row in range(rows):
            here = slice(row * length, (row + 1) * length)
            kt_ref[pair, row] = k_ref[here, pair * lanes : (pair + 1) * lanes].T

    def begin(tile):
        pair, row, (lo, hi, at) = tile
        cols = slice(pair * lanes, (pair + 1) * lanes)
        base = row * length
        queries = two_heads(q_ref[base + at : base + at + TILE, cols])
        d_context = two_heads(dctx_ref[base + at : base + at + TILE, cols])
        two_ref[0, pair, row, 2 * at : 2 * at + 2 * TILE] = queries
        two_ref[1, pair, row, 2 * at : 2 * at + 2 * TILE] = d_context
        scores = dot_nt(k_ref[base + lo : base + hi, cols], queries)
        return scores, dot_nt(v_ref[base + lo : base + hi, cols], d_context)

    def middle_part(tile, scores, d_probs):
        pair, row, (lo, hi, at) = tile
        lse = jnp.concatenate(
            [lse_ref[row, pair, head : head + 1, at : at + TILE] for head in range(2)], axis=1
        )
        probs = jnp.exp(scores + twice(mask_ref[row, lo:hi, at : at + TILE]) - lse)
        inner = jnp.sum(d_probs * probs, axis=0, keepdims=True)
        d_scores = (probs * (d_probs - inner)).astype(bf16)
        pt_ref[0, pair, row, lo:hi, 2 * at : 2 * at + 2 * TILE] = d_scores
        pt_ref[1, pair, row, lo:hi, 2 * at : 2 * at + 2 * TILE] = probs.astype(bf16)
        return d_scores

    def put(tile, kind, value):
        pair, row, (_, _, at) = tile
        here = slice(row * length + at, row * length + at + TILE)
        cols = slice((kind * group + pair) * lanes, (kind * group + pair + 1) * lanes)
        both_ref[here, cols] = value.astype(bf16)

    def end(tile, d_scores):
        pair, row, (lo, hi, at) = tile
        dq = dot(kt_ref[pair, row, :, lo:hi], d_scores) * inv_root
        dq = jnp.concatenate([dq[:half, :TILE], dq[half:, TILE:]], axis=0)
        put(tile, 0, dq.T)

    def end_keys(tile):
        pair, row, (lo, hi, at) = tile
        cols = slice(2 * lo, 2 * hi)
        for kind in range(2):
            value = dot(
                pt_ref[kind, pair, row, at : at + TILE, cols], two_ref[kind, pair, row, cols]
            )
            put(tile, 1 + kind, value)

    ready = {}
    done = {}
    for step in range(len(tiles) + 3):
        if step < len(tiles):
            ready[step] = begin(tiles[step])
        if 0 <= step - 1 < len(tiles):
            done[step - 1] = middle_part(tiles[step - 1], *ready.pop(step - 1))
        if 0 <= step - 2 < len(tiles):
            end(tiles[step - 2], done.pop(step - 2))
        if 0 <= step - 3 < len(tiles):
            end_keys(tiles[step - 3])
    both = both_ref[...]
    wide = group * lanes
    for kind, target in enumerate((dq_ref, dk_ref, dv_ref)):
        target[...] = both[:, kind * wide : (kind + 1) * wide]
    grad = dot(tt_ref[...], both).astype(bf16)
    width = grad.shape[0]
    part = width // BLOCKS
    span = both.shape[1]
    col = lax.broadcasted_iota(jnp.int32, (1, span), 1)
    kind = col // wide
    place = (pl.program_id(0) * group + first) * lanes + col - kind * wide
    owner = jnp.where(kind == 1, -1, (place + jnp.where(kind == 2, width, 0)) // (2 * part))
    sums = column_sum(both.astype(f32))
    line = lax.broadcasted_iota(jnp.int32, (16, span), 0)
    for block in range(BLOCKS):
        target, core = (keep_ref, 0) if block < 4 else (send_ref, 1)
        target[block % 4, :part] = grad[block * part : (block + 1) * part]
        here = owner == (index_ref[0] ^ (2 * (block % 4) + core))
        extra = jnp.where(line == 0, jnp.where(here, sums, 0.0), 0.0)
        target[block % 4, part:] = extra.astype(bf16)


def attend_back(
    index, qkv, d_context, lse, seg_rows, turned, first, pairs, after=(), group=2
):
    width, count = turned.shape
    rows, _, length = seg_rows.shape
    every = HEADS // 2
    lanes = width // every
    part = width // BLOCKS + 16
    wide = group * lanes
    column = lambda place: pl.BlockSpec((count, wide), lambda i, s: (0, place // group + i))
    out = pl.BlockSpec((count, wide), lambda i, s: (0, i))
    grads = pl.BlockSpec((4, part, 3 * wide), lambda i, s: (0, 0, i))
    return call(
        functools.partial(attend_back_kernel, first),
        (pairs // group,),
        [
            column(first),
            column(every + first),
            column(2 * every + first),
            column(first),
            pl.BlockSpec((rows, group, 2, length), lambda i, s: (0, first // group + i, 0, 0)),
            whole((rows, 1, length)),
            HELD,
        ],
        [out, out, out, grads, grads],
        [
            shaped((count, pairs * lanes), bf16),
            shaped((count, pairs * lanes), bf16),
            shaped((count, pairs * lanes), bf16),
            shaped((4, part, pairs * 3 * lanes), bf16),
            shaped((4, part, pairs * 3 * lanes), bf16),
        ],
        [
            pltpu.VMEM((rows, length, length), f32),
            pltpu.VMEM((group, rows, lanes, length), bf16),
            pltpu.VMEM((2, group, rows, 2 * length, lanes), bf16),
            pltpu.VMEM((2, group, rows, length, 2 * length), bf16),
            pltpu.VMEM((count, 3 * wide), bf16),
        ],
        count * pairs * lanes * (width * 6 + length * 6),
        count * pairs * lanes * 14 + count * width * 2,
        count * length * pairs * 5 // 4,
        after,
        near=(4, 5, 7, -1, -2, -3, -4, -5),
    )(index, qkv, qkv, qkv, d_context, lse, seg_rows, turned)


def input_kernel(meta, parts, index_ref, dattn_ref, *rest):
    grads, rest = rest[: 3 * parts], rest[3 * parts :]
    pieces, rest = rest[: len(meta)], rest[len(meta) :]
    out_ref, w_ref, sems = rest
    width = out_ref.shape[1]
    step = width // parts
    first = pl.program_id(0) == 0

    def weights(kind):
        cols = columns(kind, width)
        rows = width // BLOCKS
        return copies_of(meta, rows, pieces, w_ref, sems.at[kind], index_ref[0], cols, cols)

    @pl.when(first)
    def _():
        for kind in range(3):
            start_all(weights(kind))

    total = dattn_ref[...]
    for kind in range(3):

        @pl.when(first)
        def _():
            wait_all(weights(kind))

        for part in range(parts):
            at = kind * width + part * step
            total += dot_nt(grads[kind * parts + part][...], w_ref[:, at : at + step])
    out_ref[...] = total


def input_grad(index, d_attn, grads, pieces, after=(), step=512):
    count, width = d_attn.shape
    meta = meta_of(pieces)
    parts = len(grads) // 3
    block = pl.BlockSpec((step, width), lambda i, s: (i, 0))
    return call(
        functools.partial(input_kernel, meta, parts),
        (count // step,),
        [block]
        + [pl.BlockSpec((step, g.shape[1]), lambda i, s: (i, 0)) for g in grads]
        + [ANY] * len(meta),
        [block],
        [shaped((count, width), f32)],
        [pltpu.VMEM((width, 3 * width), bf16), pltpu.SemaphoreType.DMA((3, len(meta)))],
        count * width * width * 6,
        count * width * 14 + width * width * 6,
        0,
        after,
        near=tuple(range(1, 2 + len(grads))),
    )(index, d_attn, *grads, *arrays_of(pieces))


def rounded(value):
    return lax.optimization_barrier(value.astype(bf16))


def add(*values):
    total = values[0].astype(f32)
    for value in values[1:]:
        total = total + value.astype(f32)
    return total


def along_z(value, pairs):
    return lax.ppermute(value, "batch", pairs)


def core_kernel(parts, index_ref, *refs):
    keeps, others = refs[:parts], refs[parts : 2 * parts]
    mine_ref, x_ref, y_ref, *far_refs = refs[2 * parts :]
    at = 0
    for keep, other in zip(keeps, others):
        cols = slice(at, at + keep.shape[2])
        at = cols.stop
        for place, target in enumerate((mine_ref, x_ref, y_ref)):
            target[:, cols] = add(keep[place], other[place]).astype(bf16)
        far = add(keep[3], other[3]).astype(bf16)
        row = 0
        for far_ref in far_refs:
            far_ref[:, cols] = far[row : row + far_ref.shape[0]]
            row += far_ref.shape[0]


def add_cores(index, keeps, others, whole_far):
    rows = keeps[0].shape[1]
    width = sum(keep.shape[2] for keep in keeps)
    half = rows // 32 * 16
    heights = (rows, rows, rows) + ((rows,) if whole_far else (half, rows - half))
    count = 2 * len(keeps)
    return call(
        functools.partial(core_kernel, len(keeps)),
        (1,),
        [HELD] * count,
        [HELD] * len(heights),
        [shaped((height, width), bf16) for height in heights],
        [],
        rows * width * 4,
        rows * width * 24,
        near=tuple(range(1, 1 + count)) + (-1, -2, -3, -4, -5)[: len(heights)],
    )(index, *keeps, *others)


class Sum:
    def __init__(self, index, planes, keeps, sends, line, axis=None):
        self.index, self.planes, self.keeps, self.line = index, planes, keeps, line
        self.axis = axis
        self.arrived = [fsdp_swap(send, 1) for send in sends]
        self.stages = [self.over_core, self.over_far, self.over_chips, self.over_z, self.over_middle]

    def next(self, clock):
        *self.arrived, _ = lax.optimization_barrier((*self.arrived, clock))
        return list(self.stages.pop(0)(*self.arrived))

    def over_core(self, *others):
        *self.blocks, _ = add_cores(self.index, self.keeps, others, self.axis is not None)
        far = self.blocks[3:]
        axes = (2, 4) if self.axis is None else (self.axis,)
        self.arrived = [fsdp_swap(block, axis) for block, axis in zip(far, axes)]
        return far

    def over_far(self, *arrived):
        over_x, over_y = self.blocks[1:3]
        if self.axis is None:
            top, low = arrived
            half = top.shape[0]
            over_x = over_x.at[half:].set(add(over_x[half:], low).astype(bf16))
            over_y = over_y.at[:half].set(add(over_y[:half], top).astype(bf16))
        elif self.axis == 2:
            over_y = rounded(add(over_y, arrived[0]))
        else:
            over_x = rounded(add(over_x, arrived[0]))
        self.arrived = [fsdp_swap(over_x, 2), fsdp_swap(over_y, 4)]
        return [over_x, over_y]

    def over_chips(self, from_x, from_y):
        self.total = rounded(add(self.blocks[0], from_x, from_y))
        sent = self.total
        if self.line:
            self.arrived = [along_z(sent, [(0, 1), (3, 2)])]
            return [sent]
        half = sent.shape[0] // 2
        self.odd = lax.axis_index("batch") % 2 == 1
        self.total = jnp.where(self.odd, sent[half:], sent[:half])
        sent = jnp.where(self.odd, sent[:half], sent[half:])
        self.arrived = [swap(sent, "batch", self.planes, 1)]
        return [sent]

    def over_z(self, other):
        self.total = rounded(add(self.total, other))
        pairs = [(1, 2), (2, 1)] if self.line else [(0, 2), (2, 0), (1, 3), (3, 1)]
        self.arrived = [along_z(self.total, pairs)]
        return [self.total]

    def over_middle(self, other):
        self.total = rounded(add(self.total, other))
        pairs = [(1, 0), (2, 3)] if self.line else [(0, 1), (1, 0), (2, 3), (3, 2)]
        self.arrived = [along_z(self.total, pairs)]
        return [self.total]

    def result(self):
        other = self.arrived[0]
        if self.line:
            plane = lax.axis_index("batch")
            inside = (plane == 1) | (plane == 2)
            return jnp.where(inside, self.total, other).astype(f32)
        upper = jnp.where(self.odd, other, self.total)
        lower = jnp.where(self.odd, self.total, other)
        return jnp.concatenate([upper, lower], axis=0).astype(f32)


def layer(
    planes,
    ring,
    tokens,
    seg_ids,
    positive,
    out_grad,
    w_qkv,
    b_qv,
    w_out,
    b_out,
    norm1_gain,
    norm1_shift,
    w_up,
    b_up,
    w_down,
    b_down,
    norm2_gain,
    norm2_shift,
):
    paired = ring == BLOCKS and planes == 4
    row_count, row_length, width = tokens.shape
    count = row_count * row_length
    own = row_count * SEGS
    token_rows = tokens.reshape(count, width)
    seg_rows = seg_ids.reshape(row_count, 1, row_length)
    pos_col = positive.reshape(own, 1)
    fsdp = lax.axis_index("fsdp")
    me = lax.axis_index("batch") * ring + fsdp
    index = (fsdp if paired else jnp.zeros_like(fsdp)).reshape(1).astype(jnp.int32)
    tie = lax.optimization_barrier

    small = (b_out, norm1_gain, norm1_shift, b_down, norm2_gain, norm2_shift, b_up)
    sizes = [value.shape[0] * ring // BLOCKS for value in small]
    inner = sizes[-1] * BLOCKS
    if paired:
        first = pack_first(w_qkv, b_qv)
        first_xy = first_stage(first)
        *first_xy, second = tie((*first_xy, pack_second(w_out, w_up, *small)))
        first_far = second_stage(first, *first_xy)
        second, *first_far = tie((second, *first_far))
        second_xy = first_stage(second)
        qkv_pieces = both_cores(own_pieces(first, *first_xy))
        qkv_pieces += both_cores(far_pieces(first, *first_far))
    else:
        blocks = [gather_whole(value) for value in (w_qkv, b_qv, w_down, w_out, w_up, *small)]
        blocks = list(enumerate(zip(*blocks)))
        qkv_pieces = [(pack_first(*b[:2]), i, 0) for i, b in blocks]
        down_pieces = [(b[2], i, 0) for i, b in blocks]
        mid_pieces = [(pack_second(*b[3:]), i, 0) for i, b in blocks]

    qkv, clock = project_qkv(index, token_rows, qkv_pieces, 2 * width // BLOCKS)
    attended = ()
    for row in range(row_count):
        late = ()
        if paired and row == row_count - 1:
            *second_xy, third, clock = tie((*second_xy, w_down, clock))
            second_far = second_stage(second, *second_xy)
            third_xy = first_stage(third)
            late = (*second_xy, clock)
        *attended, clock = attend(index, qkv, seg_rows, row, attended, late)
    context, lse = attended
    if paired:
        mid_pieces = both_cores(own_pieces(second, *second_xy))
        *second_far, clock = tie((*second_far, clock))
        mid_pieces += both_cores(far_pieces(second, *second_far))
    normed1, root1, hidden, rows, bias_up, clock = project(
        index, context, token_rows, mid_pieces, sizes, (clock,)
    )
    hidden_turned, tokens_turned, clock = hold_turned(index, hidden, token_rows, (clock,))
    late = (clock,)
    if paired:
        *third_xy, clock = tie((*third_xy, clock))
        third_far = fsdp_swap(third_xy[0], 4)
        late = (*third_xy, clock)
    activated, slope, clock = up(index, hidden, bias_up, mid_pieces, late)
    if paired:
        down_pieces = both_cores(own_pieces(w_down, *third_xy))
        third_far, clock = tie((third_far, clock))
        down_pieces += both_cores([(third_far, 6, 0)])
    result, normed2, root2, payload, pooled, stats, _ = down(
        index, activated, normed1, rows, seg_rows, pos_col, down_pieces, (clock,)
    )

    wd_full, clock = hold_weights(index, down_pieces, (inner, width), 0, (payload,))
    if paired:
        line = [payload] + [swap(payload, "batch", planes, bit) for bit in (1, 2, 3)]
        *line, clock = tie((*line, clock))
        line = jnp.concatenate(line, axis=0)
        plane = [line] + [fsdp_swap(line, bit) for bit in (2, 4, 6)]
        wu_full, clock = hold_weights(index, mid_pieces, (width, inner), width, (line, clock))
        *plane, clock = tie((*plane, clock))
        plane = jnp.concatenate(plane, axis=0)
        everyone = [plane, fsdp_swap(plane, 1)]
        layout = (2, ring // 2, planes)
        flip = me * own
    else:
        wu_full, clock = hold_weights(index, mid_pieces, (width, inner), width)
        everyone = [lax.all_gather(payload, ("batch", "fsdp"), axis=0, tiled=True)]
        layout = (1, planes * ring, 1)
        flip = jnp.zeros_like(me)
    place = jnp.stack([flip, me * own]).astype(jnp.int32)
    pair_loss, d_pool, _ = contrast(
        place, layout, everyone, payload, pos_col, pooled, stats, (clock,)
    )

    def start(keeps, sends, line, axis=None):
        return Sum(index, planes, keeps, sends, line, axis) if paired else None

    def go(results, *sums):
        sent, clock = [], results[0]
        for one in sums:
            if one is not None:
                stage = one.next(clock)
                clock = stage[0]
                sent += stage
        if sent:
            results = tie((*results, *sent))[: len(results)]
        return results, tuple(sent)

    d_summed, d_down, sums2, keep_down, send_down, _ = norm2(
        index,
        out_grad.reshape(count, width),
        normed2,
        root2,
        seg_rows,
        rows,
        d_pool,
        activated,
    )
    sum_down = start([keep_down], [send_down], True)
    half, sent = (), ()
    for first in (0, 2):
        half = up_back(
            index, d_down, slope, hidden_turned, wd_full, wu_full, first, 2, tuple(half), sent
        )[:4]
        half, sent = go(half, sum_down)
    d_hidden, sums_up, keep_up, send_up = half
    sum_up = start([keep_up], [send_up], False)
    *first_norm, _ = norm1(
        index,
        [d_hidden],
        d_summed,
        normed1,
        root1,
        rows,
        context,
        sums2,
        sums_up,
        mid_pieces,
        sent,
    )
    (d_attn, d_context, keep_out, send_out), sent = go(first_norm, sum_up)
    pairs = HEADS // 2
    cuts = 3
    backs = []
    for cut in range(cuts):
        *back, _ = attend_back(
            index,
            qkv,
            d_context,
            lse,
            seg_rows,
            tokens_turned,
            cut * pairs // cuts,
            pairs // cuts,
            sent,
        )
        if cut == 0:
            back, sent = go(back, sum_down, sum_up)
            sum_left = start([keep_out, back[3]], [send_out, back[4]], True, 2)
        if cut == 1:
            back, sent = go(back, sum_left)
        if cut == 2:
            sum_right = start([backs[1][3], back[3]], [backs[1][4], back[4]], False, 4)
            back, sent = go(back, sum_down, sum_up, sum_left, sum_right)
        backs.append(back)
    grads = [backs[cut][kind] for kind in range(3) for cut in range(cuts)]
    grad_tokens, _ = input_grad(index, d_attn, grads, qkv_pieces, sent)

    lanes = width // pairs

    part = width // BLOCKS
    if paired:
        (grad_tokens,), sent = go((grad_tokens,), sum_right, sum_down, sum_up)
        _, sent = go(sent, sum_left)
        _, sent = go(sent, sum_right)
        _, sent = go(sent, sum_up, sum_left)
        _, sent = go(sent, sum_right, sum_left)
        go(sent, sum_right)
        grad_down, grad_up = sum_down.result().T, sum_up.result()
        left, right = sum_left.result(), sum_right.result()
        grad_out = left[:part, :width]
        joined = [left[:, width:], right[:, :width], right[:, width:]]
        own_vectors = [left[part, i * TILE : i * TILE + part] for i in range(6)]
        own_vectors.append(left[part + 1, : sizes[-1]])
    else:

        def scatter(keep, send):
            full = lax.psum(jnp.stack([keep, send], axis=1).astype(f32), "batch")
            return full.reshape((BLOCKS,) + full.shape[2:])

        def own_rows(full):
            full = full.reshape((-1,) + full.shape[2:])
            return lax.psum_scatter(full, "fsdp", scatter_dimension=0, tiled=True)

        def own_values(full):
            return lax.psum_scatter(full.reshape(-1), "fsdp", scatter_dimension=0, tiled=True)

        grad_down = own_rows(scatter(keep_down, send_down).transpose(0, 2, 1))
        grad_up = own_rows(scatter(keep_up, send_up))
        left = scatter(keep_out, send_out)
        grad_out = own_rows(left[:, :part])
        own_vectors = [own_values(left[:, part, i * TILE : i * TILE + part]) for i in range(6)]
        own_vectors.append(own_values(left[:, part + 1, : sizes[-1]]))
        whole_grads = [scatter(back[3], back[4]) for back in backs]
        joined = []
        for grads in whole_grads:
            line = lax.psum(jnp.sum(grads[:, part], axis=0), "fsdp")
            joined.append(jnp.concatenate([own_rows(grads[:, :part]), line[None]], axis=0))

    span = width // cuts
    ordered = [
        group[:, kind * span : (kind + 1) * span] for kind in range(3) for group in joined
    ]
    depth = joined[0].shape[0] - 1 if not paired else part
    grad_qkv = jnp.concatenate([group[:depth] for group in ordered], axis=1)
    vector = jnp.concatenate([group[depth] for group in ordered[:cuts] + ordered[2 * cuts :]])
    shard = vector.shape[0] // ring
    grad_bqv = lax.dynamic_slice(vector, (fsdp * shard,), (shard,))
    grad_bout, grad_g1, grad_s1, grad_bdown, grad_g2, grad_s2, grad_bup = own_vectors
    return (
        result.reshape(tokens.shape),
        pair_loss.reshape(own),
        grad_tokens.reshape(tokens.shape),
        grad_qkv,
        grad_bqv,
        grad_out,
        grad_bout,
        grad_g1,
        grad_s1,
        grad_up,
        grad_bup,
        grad_down,
        grad_bdown,
        grad_g2,
        grad_s2,
    )


def solution(mesh):
    rows = P(("batch", "fsdp"), None, None)
    matrix = P("fsdp", None)
    vector = P("fsdp")
    placed = (
        rows,
        P(("batch", "fsdp"), None),
        P(("batch", "fsdp")),
        rows,
        matrix,
        vector,
        matrix,
        vector,
        vector,
        vector,
        matrix,
        vector,
        matrix,
        vector,
        vector,
        vector,
    )
    given = (
        rows,
        P(("batch", "fsdp")),
        rows,
        matrix,
        vector,
        matrix,
        vector,
        vector,
        vector,
        matrix,
        vector,
        matrix,
        vector,
        vector,
        vector,
    )
    return jax.shard_map(
        functools.partial(layer, mesh.shape["batch"], mesh.shape["fsdp"]),
        mesh=mesh,
        in_specs=placed,
        out_specs=given,
        check_vma=False,
    )
```

```python
import functools
import math

import jax
import jax.numpy as jnp
from jax import lax
from jax.experimental import pallas as pl
from jax.experimental.pallas import tpu as pltpu
from jax.sharding import PartitionSpec as P

HEADS = 12
SEGS = 8

norm_eps = 1e-06
pool_eps = 1e-06
score_scale = 50.0
pair_weight = 256.0
masked_value = -1000000000.0

BLOCKS = 8
TILE = 128
TAIL = 128
BASE = 64

bf16 = jnp.bfloat16
f32 = jnp.float32
ANY = pl.BlockSpec(memory_space=pl.ANY)
HELD = pl.BlockSpec(memory_space=pltpu.VMEM)
VMEM_BYTES = 16 * 1024 * 1024


def dot(left, right):
    return jnp.dot(left, right, preferred_element_type=f32)


def dot_nt(left, right):
    return lax.dot_general(left, right, (((1,), (1,)), ((), ())), preferred_element_type=f32)


def whole(shape):
    return pl.BlockSpec(shape, lambda *_: (0,) * len(shape))


def call(
    kernel,
    grid,
    in_specs,
    out_specs,
    out_shape,
    scratch,
    flops,
    moved,
    special=0,
    after=(),
    alias=None,
    near=(),
    room=VMEM_BYTES,
):
    given, extra = len(in_specs) + 1, len(after)
    last = given + extra + len(out_shape)

    def body(*refs):
        refs[last][...] = jnp.zeros_like(refs[last])
        kernel(*refs[:given], *refs[given + extra : last], *refs[last + 1 :])

    shapes = [
        shape if -1 - number in near else pltpu.HBM(shape.shape, shape.dtype)
        for number, shape in enumerate(out_shape)
    ]
    shapes.append(shaped((8, TILE), f32))
    run = pl.pallas_call(
        body,
        out_shape=shapes,
        grid_spec=pltpu.PrefetchScalarGridSpec(
            num_scalar_prefetch=1,
            grid=grid,
            in_specs=in_specs + [ANY] * extra,
            out_specs=out_specs + [whole((8, TILE))],
            scratch_shapes=scratch,
        ),
        input_output_aliases=alias or {},
        compiler_params=pltpu.CompilerParams(vmem_limit_bytes=room),
        cost_estimate=pl.CostEstimate(
            flops=int(flops), bytes_accessed=int(moved), transcendentals=int(special)
        ),
    )

    def apply(index, *operands):
        placed = [
            value if 1 + number in near else pltpu.with_memory_space_constraint(value, pltpu.HBM)
            for number, value in enumerate(operands)
        ]
        return run(index, *placed, *after)

    return apply


def shaped(shape, dtype):
    return jax.ShapeDtypeStruct(shape, dtype)


def swap(value, axis, size, bit):
    return lax.ppermute(value, axis, [(i, i ^ bit) for i in range(size)])


def fsdp_swap(value, bit):
    return swap(value, "fsdp", BLOCKS, bit)


def middle(shard):
    return shard.shape[0] // 32 * 16


def first_stage(shard):
    return fsdp_swap(shard, 2), fsdp_swap(shard, 4)


def second_stage(shard, over_x, over_y):
    half = middle(shard)
    return fsdp_swap(over_y[:half], 2), fsdp_swap(over_x[half:], 4)


def own_pieces(shard, over_x, over_y):
    return [(shard, 0, 0), (over_x, 2, 0), (over_y, 4, 0)]


def far_pieces(shard, far_top, far_low):
    return [(far_top, 6, 0), (far_low, 6, middle(shard))]


def both_cores(pieces):
    return pieces + [(fsdp_swap(value, 1), place ^ 1, off) for value, place, off in pieces]


def gather_whole(shard):
    full = lax.all_gather(shard, "fsdp", axis=0, tiled=True)
    rows = full.shape[0] // BLOCKS
    return [full[i * rows : (i + 1) * rows] for i in range(BLOCKS)]


def meta_of(pieces):
    return tuple((place, off, value.shape[0]) for value, place, off in pieces)


def arrays_of(pieces):
    return [value for value, _, _ in pieces]


def copies_of(
    meta, rows, refs, target, sems, index, source=None, place=None, first=0
):
    copies = []
    for number, ((block, off, count), ref) in enumerate(zip(meta, refs)):
        low, high = max(off, first), min(off + count, first + rows)
        if low >= high:
            continue
        here = pl.ds(pl.multiple_of((index ^ block) * rows + low - first, 16), high - low)
        part = ref.at[low - off : high - off]
        copies.append(
            pltpu.make_async_copy(
                part if source is None else part.at[:, source],
                target.at[here] if place is None else target.at[here, place],
                sems.at[number],
            )
        )
    return copies


def pair_copies(meta, size, refs, target, sems, index, chip):
    copies = []
    for number, ((block, off, count), ref) in enumerate(zip(meta, refs)):
        if block // 2 == chip:
            start = pl.multiple_of((index ^ block) * size + off, 16)
            copies.append(
                pltpu.make_async_copy(ref, target.at[pl.ds(start, count)], sems.at[number])
            )
    return copies


def start_all(copies):
    for copy in copies:
        copy.start()


def wait_all(copies):
    for copy in copies:
        copy.wait()


def columns(number, size, base=0):
    return pl.ds(pl.multiple_of(base + number * size, TILE), size)


def fill_mask(seg_row, mask_ref):
    length = seg_row.shape[1]
    keys = jnp.broadcast_to(seg_row, (TILE, length)).T
    for lo, hi, at in bands(length):
        same = keys[lo:hi] == seg_row[:, at : at + TILE]
        mask_ref[lo:hi, at : at + TILE] = jnp.where(same, 0.0, masked_value)


def bands(length):
    out = []
    for at in range(0, length, TILE):
        out.append((max(at - TILE, 0), min(at + 2 * TILE, length), at))
    return out


def two_heads(pair):
    lane = lax.broadcasted_iota(jnp.int32, (1, pair.shape[1]), 1)
    first = (lane < pair.shape[1] // 2).astype(f32).astype(bf16)
    return jnp.concatenate([pair * first, pair * (1.0 - first)], axis=0)


def twice(value):
    return jnp.concatenate([value, value], axis=1)


def pack_line(vectors, width):
    line = jnp.concatenate([jnp.pad(v, (0, -v.shape[0] % TILE)) for v in vectors])
    return jnp.pad(line[None], ((0, 15), (0, width - line.shape[0])))


def pack_first(w_qkv, b_qv):
    return jnp.concatenate([w_qkv, pack_line([b_qv], w_qkv.shape[1])], axis=0)


def pack_second(w_out, w_up, *vectors):
    both = jnp.concatenate([w_out, w_up], axis=1)
    return jnp.concatenate([both, pack_line(vectors, both.shape[1])], axis=0)


def table_of(lines):
    line = lax.broadcasted_iota(jnp.int32, (BLOCKS, 16 * BLOCKS), 0) * 16
    pick = line == lax.broadcasted_iota(jnp.int32, (BLOCKS, 16 * BLOCKS), 1)
    return dot(pick.astype(f32).astype(bf16), lines)


def spread(table, at, size):
    count = table.shape[0]
    padded = size + -size % TILE
    block = table[:, at : at + padded].astype(bf16)
    col = lax.broadcasted_iota(jnp.int32, (1, count * size), 1)
    owner = col // size
    place = lax.broadcasted_iota(jnp.int32, (padded, count * size), 0) == col - owner * size
    value = dot(block, place.astype(f32).astype(bf16))
    keep = lax.broadcasted_iota(jnp.int32, value.shape, 0) == owner
    return jnp.sum(jnp.where(keep, value, 0.0), axis=0, keepdims=True), at + padded


def qkv_kernel(meta, size, index_ref, tok_ref, *rest):
    pieces, rest = rest[: len(meta)], rest[len(meta) :]
    qkv_ref, w_ref, small_ref, bias_ref, sems, small_sems = rest
    width = tok_ref.shape[1]
    rows = width // BLOCKS
    part = pl.program_id(0)
    index = index_ref[0]

    def weights(number):
        cols = columns(number, width)
        return copies_of(meta, rows, pieces, w_ref, sems.at[number], index, cols, cols)

    @pl.when(part == 0)
    def _():
        here = slice(0, small_ref.shape[1])
        small = copies_of(meta, 16, pieces, small_ref, small_sems, index, here, None, rows)
        start_all(small)
        for number in range(3):
            start_all(weights(number))
        wait_all(small)
        bias, _ = spread(table_of(small_ref[...]), 0, size)
        bias_ref[0] = bias[:, :width]
        bias_ref[1] = jnp.zeros((1, width), f32)
        bias_ref[2] = bias[:, width:]

    wait_all(weights(part))
    scale = jnp.where(part == 0, 1.0 / math.sqrt(width // HEADS), 1.0)
    value = dot(tok_ref[...], w_ref[:, columns(part, width)]) + bias_ref[part]
    qkv_ref[...] = (value * scale).astype(bf16)


def project_qkv(index, tokens, pieces, size):
    count, width = tokens.shape
    meta = meta_of(pieces)
    out = pl.BlockSpec((count, width), lambda i, s: (0, i))
    return call(
        functools.partial(qkv_kernel, meta, size),
        (3,),
        [whole((count, width))] + [ANY] * len(meta),
        [out],
        [shaped((count, 3 * width), bf16)],
        [
            pltpu.VMEM((width, 3 * width), bf16),
            pltpu.VMEM((16 * BLOCKS, size + -size % TILE), bf16),
            pltpu.VMEM((3, 1, width), f32),
            pltpu.SemaphoreType.DMA((3, len(meta))),
            pltpu.SemaphoreType.DMA((len(meta),)),
        ],
        count * width * width * 6,
        count * width * 8 + width * width * 6,
        near=(-1,),
    )(index, tokens, *arrays_of(pieces))


def attend_kernel(index_ref, qkv_ref, seg_ref, *rest):
    ctx_ref, lse_ref, vt_ref, ct_ref, mask_ref = rest[-5:]
    length, width = ctx_ref.shape
    pairs = HEADS // 2
    lanes = width // pairs
    half = lanes // 2
    fill_mask(seg_ref[0].astype(f32), mask_ref)
    vt_ref[...] = qkv_ref[:, 2 * width :].T

    tiles = [(pair, band) for pair in range(pairs) for band in bands(length)]

    def scores_of(tile):
        pair, (lo, hi, at) = tile
        queries = two_heads(qkv_ref[at : at + TILE, pair * lanes : (pair + 1) * lanes])
        keys = qkv_ref[lo:hi, width + pair * lanes : width + (pair + 1) * lanes]
        return dot_nt(keys, queries)

    def probs_of(tile, scores):
        pair, (lo, hi, at) = tile
        scores = scores + twice(mask_ref[lo:hi, at : at + TILE])
        top = jnp.max(scores, axis=0, keepdims=True)
        terms = jnp.exp(scores - top)
        total = jnp.sum(terms, axis=0, keepdims=True)
        lse = top + jnp.log(total)
        for head in range(2):
            lse_ref[0, pair, head : head + 1, at : at + TILE] = lse[:, head * TILE : (head + 1) * TILE]
        return (terms * (1.0 / total)).astype(bf16)

    def put_context(tile, probs):
        pair, (lo, hi, at) = tile
        context = dot(vt_ref[pair * lanes : (pair + 1) * lanes, lo:hi], probs)
        for head in range(2):
            rows = slice(pair * lanes + head * half, pair * lanes + (head + 1) * half)
            part = context[head * half : (head + 1) * half, head * TILE : (head + 1) * TILE]
            ct_ref[rows, at : at + TILE] = part.astype(bf16)

    ready = {}
    probs = {}
    for step in range(len(tiles) + 2):
        if step < len(tiles):
            ready[step] = scores_of(tiles[step])
        if 0 <= step - 1 < len(tiles):
            probs[step - 1] = probs_of(tiles[step - 1], ready.pop(step - 1))
        if 0 <= step - 2:
            put_context(tiles[step - 2], probs.pop(step - 2))
    ctx_ref[...] = ct_ref[...].T


def attend(index, qkv, seg_rows, row, before=(), after=()):
    count, width = qkv.shape[0], qkv.shape[1] // 3
    rows, _, length = seg_rows.shape
    pairs = HEADS // 2
    return call(
        attend_kernel,
        (1,),
        [
            pl.BlockSpec((length, 3 * width), lambda i, s: (row, 0)),
            pl.BlockSpec((1, 1, length), lambda i, s: (row, 0, 0)),
        ]
        + [ANY] * len(before),
        [
            pl.BlockSpec((length, width), lambda i, s: (row, 0)),
            pl.BlockSpec((1, pairs, 2, length), lambda i, s: (row, 0, 0, 0)),
        ],
        [
            shaped((count, width), bf16),
            shaped((rows, pairs, 2, length), f32),
        ],
        [
            pltpu.VMEM((width, length), bf16),
            pltpu.VMEM((width, length), bf16),
            pltpu.VMEM((length, length), f32),
        ],
        length * length * width * 4,
        length * width * 8,
        length * length * HEADS * 5 // 8,
        after,
        {3 + i: i for i in range(len(before))},
        (1, -1, -2) + ((3, 4) if before else ()),
    )(index, qkv, seg_rows, *before)


def row_stats(values):
    mean = jnp.mean(values, axis=-1, keepdims=True)
    centred = values - mean
    spread = jnp.mean(centred * centred, axis=-1, keepdims=True)
    return centred, lax.rsqrt(spread + norm_eps)


def project_kernel(meta, sizes, index_ref, ctx_ref, tok_ref, *rest):
    pieces, rest = rest[: len(meta)], rest[len(meta) :]
    norm_ref, root_ref, hid_ref, vec_ref, up_ref, w_ref, small_ref, sems, small_sems = rest
    width = w_ref.shape[0]

    @pl.when(pl.program_id(0) == 0)
    def _():
        rows = width // BLOCKS
        here = slice(0, width)
        copies = copies_of(meta, rows, pieces, w_ref, sems, index_ref[0], here, here)
        line = slice(0, small_ref.shape[1])
        small = copies_of(meta, 16, pieces, small_ref, small_sems, index_ref[0], line, None, rows)
        start_all(small)
        start_all(copies)
        vec_ref[...] = jnp.zeros_like(vec_ref)
        wait_all(small)
        table = table_of(small_ref[...])
        line, at = 0, 0
        for size in sizes:
            value, at = spread(table, at, size)
            if value.shape[1] == width:
                vec_ref[line : line + 1] = value
                line += 1
            else:
                up_ref[...] = value
        wait_all(copies)

    def finish(here, product):
        summed = tok_ref[here].astype(f32) + (product + vec_ref[0:1])
        centred, root = row_stats(summed)
        normed = centred * root
        norm_ref[here] = normed
        root_ref[here] = root
        hid_ref[here] = (normed * vec_ref[1:2] + vec_ref[2:3]).astype(bf16)

    in_turn(ctx_ref.shape[0], lambda here: dot(ctx_ref[here], w_ref[...]), finish)


def in_turn(count, begin, finish, size=2 * TILE):
    last = None
    for at in range(0, count, size):
        here = slice(at, at + size)
        value = begin(here)
        if last is not None:
            finish(*last)
        last = (here, value)
    finish(*last)


def project(index, context, tokens, pieces, sizes, after=(), step=512):
    count, width = tokens.shape
    inner = 4 * width
    used = sum(size + -size % TILE for size in sizes)
    meta = meta_of(pieces)
    rows = pl.BlockSpec((step, width), lambda i, s: (i, 0))
    return call(
        functools.partial(project_kernel, meta, sizes),
        (count // step,),
        [rows, rows] + [ANY] * len(meta),
        [
            rows,
            pl.BlockSpec((step, 1), lambda i, s: (i, 0)),
            rows,
            whole((SEGS, width)),
            whole((1, inner)),
        ],
        [
            shaped((count, width), f32),
            shaped((count, 1), f32),
            shaped((count, width), bf16),
            shaped((SEGS, width), f32),
            shaped((1, inner), f32),
        ],
        [
            pltpu.VMEM((width, width), bf16),
            pltpu.VMEM((16 * BLOCKS, used), bf16),
            pltpu.SemaphoreType.DMA((len(meta),)),
            pltpu.SemaphoreType.DMA((len(meta),)),
        ],
        count * width * width * 2,
        count * width * 10 + width * width * 2,
        0,
        after,
        near=(1, -3, -4, -5),
    )(index, context, tokens, *arrays_of(pieces))


def gelu_parts(value):
    share = 0.5 * lax.erf(value * math.sqrt(0.5)) + 0.5
    bell = jnp.exp2(value * value * (-0.5 / math.log(2.0)))
    return value * share, share + value * bell * (1.0 / math.sqrt(2.0 * math.pi))


def up_kernel(meta, index_ref, hid_ref, bias_ref, *rest):
    pieces, rest = rest[: len(meta)], rest[len(meta) :]
    act_ref, slope_ref, w_ref, sems = rest
    tile = act_ref.shape[1]
    width = w_ref.shape[0]
    step = pl.program_id(0)

    def weights(number):
        source, place = columns(number, tile, width), columns(number, tile)
        rows = width // BLOCKS
        return copies_of(meta, rows, pieces, w_ref, sems.at[number], index_ref[0], source, place)

    @pl.when(step == 0)
    def _():
        for number in range(sems.shape[0]):
            start_all(weights(number))

    wait_all(weights(step))
    wide = 256

    def begin(cols):
        here = pl.ds(pl.multiple_of(step * tile + cols.start, wide), wide)
        return dot(hid_ref[...], w_ref[:, here]) + bias_ref[:, cols]

    def finish(cols, value):
        act, slope = gelu_parts(value)
        act_ref[:, cols] = act.astype(bf16)
        slope_ref[:, cols] = slope.astype(bf16)

    in_turn(tile, begin, finish, wide)


def up(index, hidden, bias, pieces, after=(), tile=768):
    count, width = hidden.shape
    inner = bias.shape[1]
    meta = meta_of(pieces)
    out = pl.BlockSpec((count, tile), lambda i, s: (0, i))
    return call(
        functools.partial(up_kernel, meta),
        (inner // tile,),
        [HELD, pl.BlockSpec((1, tile), lambda i, s: (0, i))] + [ANY] * len(meta),
        [out, out],
        [shaped((count, inner), bf16)] * 2,
        [
            pltpu.VMEM((width, inner), bf16),
            pltpu.SemaphoreType.DMA((inner // tile, len(meta))),
        ],
        count * width * inner * 2,
        count * (width * 2 + inner * 4) + width * inner * 2,
        count * inner * 4,
        after,
        near=(1, 2),
    )(index, hidden, bias, *arrays_of(pieces))


def down_kernel(meta, index_ref, act_ref, norm_ref, vec_ref, seg_ref, pos_ref, *rest):
    pieces, rest = rest[: len(meta)], rest[len(meta) :]
    res_ref, norm2_ref, root_ref, pay_ref, pool_ref, stat_ref, *rest = rest
    w_ref, held_ref, sum_ref, num_ref, sems, act_sems = rest
    step, steps = pl.program_id(0), pl.num_programs(0)
    length, width = res_ref.shape
    tile = w_ref.shape[0] // 4
    index = index_ref[0]

    def weights(chip):
        return pair_copies(meta, tile // 2, pieces, w_ref, sems, index, chip)

    def inputs(row, chip):
        rows = pl.ds(pl.multiple_of(row * length, length), length)
        source = act_ref.at[rows, columns((index // 2) ^ chip, tile)]
        return pltpu.make_async_copy(source, held_ref.at[row, chip], act_sems.at[row, chip])

    @pl.when(step == 0)
    def _():
        inputs(0, 0).start()
        start_all(weights(0))

    wanted = lax.broadcasted_iota(jnp.int32, (SEGS, length), 0)
    member = (wanted == seg_ref[0]).astype(f32)
    product = None
    for chip in range(4):
        inputs(step, chip).wait()

        @pl.when(step == 0)
        def _():
            wait_all(weights(chip))
            if chip < 3:
                inputs(0, chip + 1).start()
                start_all(weights(chip + 1))
            else:
                for other in range(4):
                    inputs(1, other).start()

        value = dot(held_ref[step, chip], w_ref[columns((index // 2) ^ chip, tile)])
        product = value if product is None else product + value
    hidden = norm_ref[...] * vec_ref[1:2] + vec_ref[2:3]
    summed = hidden + (product + vec_ref[3:4])
    centred, root = row_stats(summed)
    normed = centred * root
    result = normed * vec_ref[4:5] + vec_ref[5:6]
    norm2_ref[...] = normed
    root_ref[...] = root
    high = result.astype(bf16)
    res_ref[...] = high
    low = (result - high.astype(f32)).astype(bf16)
    own = pl.ds(pl.multiple_of(step * SEGS, SEGS), SEGS)
    member_b = member.astype(bf16)
    sum_ref[own] = dot(member_b, high) + dot(member_b, low)
    num_ref[own] = jnp.broadcast_to(jnp.sum(member, axis=1, keepdims=True), (SEGS, TAIL))

    @pl.when(step == steps - 1)
    def _():
        counts = num_ref[:, 0:1]
        pooled = sum_ref[...] / counts
        scale = lax.rsqrt(jnp.mean(pooled * pooled, axis=-1, keepdims=True) + pool_eps)
        pool_ref[...] = pooled
        lane = lax.broadcasted_iota(jnp.int32, (pooled.shape[0], TAIL), 1)
        stat_ref[...] = jnp.where(lane == 0, scale, counts)
        pay_ref[:, :width] = (pooled * scale).astype(bf16)
        partner = pos_ref[...]
        digit = jnp.where(lane == 0, partner // BASE, partner % BASE)
        pay_ref[:, width:] = jnp.where(lane < 2, digit, 0).astype(f32).astype(bf16)


def down(index, activated, normed, vectors, seg_rows, positive, pieces, after=()):
    count, width = normed.shape
    inner = activated.shape[1]
    rows, _, step = seg_rows.shape
    own = rows * SEGS
    meta = meta_of(pieces)
    block = pl.BlockSpec((step, width), lambda i, s: (i, 0))
    return call(
        functools.partial(down_kernel, meta),
        (count // step,),
        [
            ANY,
            block,
            whole(vectors.shape),
            pl.BlockSpec((1, 1, step), lambda i, s: (i, 0, 0)),
            whole((own, 1)),
        ]
        + [ANY] * len(meta),
        [
            block,
            block,
            pl.BlockSpec((step, 1), lambda i, s: (i, 0)),
            whole((own, width + TAIL)),
            whole((own, width)),
            whole((own, TAIL)),
        ],
        [
            shaped((count, width), bf16),
            shaped((count, width), f32),
            shaped((count, 1), f32),
            shaped((own, width + TAIL), bf16),
            shaped((own, width), f32),
            shaped((own, TAIL), f32),
        ],
        [
            pltpu.VMEM((inner, width), bf16),
            pltpu.VMEM((rows, 4, step, inner // 4), bf16),
            pltpu.VMEM((own, width), f32),
            pltpu.VMEM((own, TAIL), f32),
            pltpu.SemaphoreType.DMA((len(meta),)),
            pltpu.SemaphoreType.DMA((rows, 4)),
        ],
        count * width * inner * 2,
        count * (width * 10 + inner * 2) + width * inner * 2,
        after=after,
        near=(3, 5, -4, -5, -6),
        room=24 * 1024 * 1024,
    )(index, activated, normed, vectors, seg_rows, positive, *arrays_of(pieces))


def segment_of(row, own, cores, chips, planes):
    block = row // own
    plane, chip, core = block % planes, block // planes % chips, block // (planes * chips)
    return ((plane * chips + chip) * cores + core) * own + row % own


def contrast_kernel(layout, place_ref, own_ref, pos_ref, pool_ref, stat_ref, *rest):
    pieces, (loss_ref, grad_ref, all_ref, sems) = rest[:-4], rest[-4:]
    copies, at = [], 0
    for number, piece in enumerate(pieces):
        here = all_ref.at[at : at + piece.shape[0]]
        copies.append(pltpu.make_async_copy(piece, here, sems.at[number]))
        at += piece.shape[0]
    for copy in copies:
        copy.start()
    for copy in copies:
        copy.wait()
    total = all_ref.shape[0]
    own, width = pool_ref.shape
    factor = score_scale / width
    block = min(total, 512)
    flip, first = place_ref[0], place_ref[1]
    mine = own_ref[:, :width]
    mine_id = lax.broadcasted_iota(jnp.int32, (own, total), 0) + first
    other_id = segment_of(lax.broadcasted_iota(jnp.int32, (1, total), 1), own, *layout) ^ flip
    logits = dot_nt(mine, all_ref[:, :width]) * factor
    logits = jnp.where(mine_id == other_id, masked_value, logits)
    top = jnp.max(logits, axis=1, keepdims=True)
    log_own = top + jnp.log(jnp.sum(jnp.exp(logits - top), axis=1, keepdims=True))
    is_positive = other_id == pos_ref[...]
    picked = jnp.sum(jnp.where(is_positive, logits, 0.0), axis=1, keepdims=True)
    loss_ref[...] = log_own - picked
    d_logits = pair_weight * (jnp.exp(logits - log_own) - is_positive.astype(f32))
    d_emb = dot(d_logits.astype(bf16), all_ref[:, :width])
    lane = lax.broadcasted_iota(jnp.int32, (SEGS, TAIL), 1)
    digits = jnp.where(lane == 0, float(BASE), jnp.where(lane == 1, 1.0, 0.0)).astype(bf16)
    for at in range(0, total, block):
        rows = slice(at, at + block)
        table = dot_nt(all_ref[:, :width], all_ref[rows, :width]) * factor
        left = lax.broadcasted_iota(jnp.int32, (total, block), 0)
        right = lax.broadcasted_iota(jnp.int32, (total, block), 1) + at
        table = jnp.where(left == right, masked_value, table)
        top = jnp.max(table, axis=0, keepdims=True)
        log_all = top + jnp.log(jnp.sum(jnp.exp(table - top), axis=0, keepdims=True))
        partner = dot_nt(digits, all_ref[rows, width:])[0:1].astype(jnp.int32)
        chosen = partner == mine_id[:, rows]
        back = pair_weight * (jnp.exp(logits[:, rows] - log_all) - chosen.astype(f32))
        d_emb += dot(back.astype(bf16), all_ref[rows, :width])
    d_emb = d_emb * factor
    scale, counts = stat_ref[:, 0:1], stat_ref[:, 1:2]
    pooled = pool_ref[...]
    along = jnp.mean(d_emb * pooled, axis=-1, keepdims=True)
    grad_ref[...] = (d_emb * scale - pooled * (scale * scale * scale * along)) / counts


def contrast(place, layout, everyone, payload, positive, pooled, stats, after=()):
    own, width = pooled.shape
    total = sum(v.shape[0] for v in everyone)
    return call(
        functools.partial(contrast_kernel, layout),
        (1,),
        [whole(v.shape) for v in (payload, positive, pooled, stats)] + [ANY] * len(everyone),
        [whole((own, 1)), whole((own, width))],
        [shaped((own, 1), f32), shaped((own, width), f32)],
        [
            pltpu.VMEM((total, width + TAIL), bf16),
            pltpu.SemaphoreType.DMA((len(everyone),)),
        ],
        total * total * width * 2,
        total * width * 2,
        total * total,
        after=after,
        near=tuple(range(1, 5 + len(everyone))) + (-1, -2),
    )(place, payload, positive, pooled, stats, *everyone)


def norm_back(d_out, normed, root, gain):
    scaled = d_out * gain
    mean = jnp.mean(scaled, axis=-1, keepdims=True)
    along = jnp.mean(scaled * normed, axis=-1, keepdims=True)
    return root * (scaled - mean - normed * along)


def column_sum(values):
    return jnp.sum(values, axis=0, keepdims=True)


def norm2_kernel(turns, index_ref, og_ref, norm_ref, root_ref, seg_ref, vec_in_ref, dp_ref, *rest):
    act_ref, dsum_ref, ddown_ref, vec_ref, keep_ref, send_ref, dt_ref = rest
    step = pl.program_id(0)
    chunk, width = og_ref.shape
    own = dp_ref.shape[0]

    @pl.when(step == 0)
    def _():
        vec_ref[...] = jnp.zeros_like(vec_ref)

    @pl.when(step < turns)
    def _():
        row = step // (turns * SEGS // own)
        pool = dp_ref[pl.ds(pl.multiple_of(row * SEGS, SEGS), SEGS)]
        high = pool.astype(bf16)
        left = pool - high.astype(f32)
        mid = left.astype(bf16)
        low = (left - mid.astype(f32)).astype(bf16)
        pad = jnp.zeros((TILE - 3 * SEGS, width), bf16)
        table = jnp.concatenate([high, mid, low, pad], axis=0)
        lane = lax.broadcasted_iota(jnp.int32, (chunk, TILE), 1) % SEGS
        keys = jnp.broadcast_to(seg_ref[0].astype(f32), (TILE, chunk)).T
        member = (lane.astype(f32) == keys).astype(f32).astype(bf16)

        def begin(here):
            return dot(member[here], table)

        def finish(here, shared):
            d_res = og_ref[here].astype(f32) + shared
            normed = norm_ref[here]
            d_sum = norm_back(d_res, normed, root_ref[here], vec_in_ref[4:5])
            d_down = d_sum.astype(bf16)
            dsum_ref[here] = d_sum
            ddown_ref[here] = d_down
            cols = pl.ds(pl.multiple_of(step * chunk + here.start, TILE), TILE)
            dt_ref[:, cols] = d_down.T
            vec_ref[0:1] += column_sum(d_down.astype(f32))
            vec_ref[1:2] += column_sum(d_res * normed)
            vec_ref[2:3] += column_sum(d_res)

        in_turn(chunk, begin, finish, TILE)

    @pl.when(step >= turns)
    def _():
        grad = dot(dt_ref[...], act_ref[...]).astype(bf16)
        half = grad.shape[1] // 2
        odd = index_ref[0] % 2 == 1
        keep_ref[0] = jnp.where(odd, grad[:, half:], grad[:, :half])
        send_ref[0] = jnp.where(odd, grad[:, :half], grad[:, half:])


def norm2(index, out_grad, normed, root, seg_rows, vectors, d_pool, activated, turns=4):
    count, width = out_grad.shape
    inner = activated.shape[1]
    tile = inner // 4
    own = d_pool.shape[0]
    first = lambda i: jnp.minimum(i, turns - 1)
    then = lambda i: jnp.maximum(i - turns, 0)
    split = turns // seg_rows.shape[0]
    block = pl.BlockSpec((count // turns, width), lambda i, s: (first(i), 0))
    column = pl.BlockSpec((count // turns, 1), lambda i, s: (first(i), 0))
    grads = pl.BlockSpec((1, width, tile // 2), lambda i, s: (then(i), 0, 0))
    return call(
        functools.partial(norm2_kernel, turns),
        (turns + 4,),
        [
            block,
            block,
            column,
            pl.BlockSpec((1, 1, count // turns), lambda i, s: (first(i) // split, 0, first(i) % split)),
            whole(vectors.shape),
            whole((own, width)),
            pl.BlockSpec((count, tile), lambda i, s: (0, (s[0] // 2) ^ then(i))),
        ],
        [block, block, whole((SEGS, width)), grads, grads],
        [
            shaped((count, width), f32),
            shaped((count, width), bf16),
            shaped((SEGS, width), f32),
            shaped((4, width, tile // 2), bf16),
            shaped((4, width, tile // 2), bf16),
        ],
        [pltpu.VMEM((width, count), bf16)],
        count * width * inner * 2,
        count * (width * 12 + inner * 2) + width * inner * 2,
        near=(5, 6, -1, -2, -3, -4, -5),
    )(index, out_grad, normed, root, seg_rows, vectors, d_pool, activated)


def put_turned(source_ref, target_ref, turn_ref, index):
    turn_ref[...] = source_ref[...].T
    rows = turn_ref.shape[0] // BLOCKS
    for place in range(BLOCKS):
        block = index ^ ((place % 4) * 2 + place // 4)
        start = pl.multiple_of(block * rows, 16)
        target_ref[place * rows : (place + 1) * rows] = turn_ref[pl.ds(start, rows)]


def weights_kernel(meta, base, index_ref, *refs):
    pieces, (out_ref, sems) = refs[:-2], refs[-2:]
    height, width = out_ref.shape
    here = slice(base, base + width)
    copies = copies_of(meta, height // BLOCKS, pieces, out_ref, sems, index_ref[0], here)
    start_all(copies)
    wait_all(copies)


def hold_weights(index, pieces, shape, base, after=()):
    meta = meta_of(pieces)
    return call(
        functools.partial(weights_kernel, meta, base),
        (1,),
        [ANY] * len(meta),
        [HELD],
        [shaped(shape, bf16)],
        [pltpu.SemaphoreType.DMA((len(meta),))],
        0,
        shape[0] * shape[1] * 4,
        0,
        after,
        near=(-1,),
    )(index, *arrays_of(pieces))


def turned_kernel(index_ref, one_ref, two_ref, out_one_ref, out_two_ref, turn_ref):
    put_turned(one_ref, out_one_ref, turn_ref, index_ref[0])
    put_turned(two_ref, out_two_ref, turn_ref, index_ref[0])


def hold_turned(index, one, two, after=()):
    count, width = one.shape
    return call(
        turned_kernel,
        (1,),
        [whole((count, width))] * 2,
        [HELD, HELD],
        [shaped((width, count), bf16)] * 2,
        [pltpu.VMEM((width, count), bf16)],
        0,
        count * width * 8,
        0,
        after,
        near=(-1, -2),
    )(index, one, two)


def up_back_kernel(first, before, index_ref, ddown_ref, slope_ref, ht_ref, wd_ref, wu_ref, *rest):
    earlier, rest = rest[:before], rest[before:]
    dhid_ref, bias_ref, keep_ref, send_ref = rest
    step = pl.program_id(0)
    tile = slope_ref.shape[1]
    width = ht_ref.shape[0]
    here = columns((index_ref[0] // 2) ^ (step + first), tile)
    wide = 256
    parts = []

    def begin(cols):
        rows = pl.ds(pl.multiple_of(here.start + cols.start, wide), wide)
        return dot_nt(ddown_ref[...], wd_ref[rows])

    def finish(cols, d_act):
        d_up = (d_act * slope_ref[:, cols].astype(f32)).astype(bf16)
        bias_ref[:, cols] = column_sum(d_up.astype(f32))
        parts.append(d_up)

    in_turn(tile, begin, finish, wide)
    d_up = jnp.concatenate(parts, axis=1)
    grad = dot(ht_ref[...], d_up).astype(bf16)
    half = width // 2
    keep_ref[...] = grad[:half].reshape(keep_ref.shape)
    send_ref[...] = grad[half:].reshape(send_ref.shape)
    share = dot_nt(d_up, wu_ref[:, here])

    @pl.when(step == 0)
    def _():
        dhid_ref[...] = earlier[0][...] + share if earlier else share

    @pl.when(step > 0)
    def _():
        dhid_ref[...] += share


def up_back(index, d_down, slope, turned, w_down, w_up, first, steps, before=(), after=()):
    count, width = d_down.shape
    inner = slope.shape[1]
    tile = inner // 4
    part = width // BLOCKS
    place = lambda i, s: (s[0] // 2) ^ (i + first)
    grads = pl.BlockSpec((4, part, tile), lambda i, s: (0, 0, place(i, s)))
    return call(
        functools.partial(up_back_kernel, first, len(before)),
        (steps,),
        [HELD, pl.BlockSpec((count, tile), lambda i, s: (0, place(i, s))), HELD, HELD, HELD]
        + ([HELD] + [ANY] * 3 if before else []),
        [HELD, pl.BlockSpec((1, tile), lambda i, s: (0, place(i, s))), grads, grads],
        [
            shaped((count, width), f32),
            shaped((1, inner), f32),
            shaped((4, part, inner), bf16),
            shaped((4, part, inner), bf16),
        ],
        [],
        count * width * tile * 6 * steps,
        count * (width * 8 + inner) + width * inner * 6,
        0,
        after,
        {6 + i: i for i in range(len(before))},
        (1, 3, 4, 5, 6, 7, 8, 9, -1, -2, -3, -4),
    )(index, d_down, slope, turned, w_down, w_up, *before)


def cut_vector(vector, size, index):
    width = vector.shape[1]
    owner = lax.broadcasted_iota(jnp.int32, (BLOCKS, width), 1) // size
    wanted = lax.broadcasted_iota(jnp.int32, (BLOCKS, width), 0) ^ index
    rows = jnp.where(owner == wanted, vector, 0.0).astype(bf16)
    source = lax.broadcasted_iota(jnp.int32, (width, 1), 0)
    place = source - source // size * size == lax.broadcasted_iota(jnp.int32, (width, TILE), 1)
    return dot(rows, place.astype(f32).astype(bf16))


def norm1_kernel(meta, parts, index_ref, *rest):
    dhids, rest = rest[:parts], rest[parts:]
    dsum_ref, norm_ref, root_ref, gain_ref, ctx_ref, other_ref, up_ref, *rest = rest
    pieces, rest = rest[: len(meta)], rest[len(meta) :]
    dattn_ref, dctx_ref, keep_ref, send_ref, w_ref, acc_ref, vec_ref, sems = rest
    step = pl.program_id(0)
    width = w_ref.shape[0]
    rows = width // BLOCKS

    @pl.when(step == 0)
    def _():
        here = slice(0, width)
        copies = copies_of(meta, rows, pieces, w_ref, sems, index_ref[0], here, here)
        start_all(copies)
        vec_ref[...] = jnp.zeros_like(vec_ref)
        acc_ref[...] = jnp.zeros_like(acc_ref)
        wait_all(copies)

    parts = []

    def begin(here):
        d_hid = dsum_ref[here]
        for dhid_ref in dhids:
            d_hid = d_hid + dhid_ref[here]
        normed = norm_ref[here]
        d_sum = norm_back(d_hid, normed, root_ref[here], gain_ref[1:2])
        d_attn = d_sum.astype(bf16)
        dattn_ref[here] = d_sum
        vec_ref[0:1] += column_sum(d_attn.astype(f32))
        vec_ref[1:2] += column_sum(d_hid * normed)
        vec_ref[2:3] += column_sum(d_hid)
        parts.append(d_attn)
        return d_attn

    def finish(here, d_attn):
        dctx_ref[here] = dot_nt(d_attn, w_ref[...]).astype(bf16)

    in_turn(dsum_ref.shape[0], begin, finish)
    acc_ref[...] += dot(ctx_ref[...].T, jnp.concatenate(parts, axis=0))

    @pl.when(step == pl.num_programs(0) - 1)
    def _():
        index = index_ref[0]
        vectors = [vec_ref[i : i + 1] for i in range(3)] + [other_ref[i : i + 1] for i in range(3)]
        top = [cut_vector(vector, rows, index) for vector in vectors]
        top = jnp.concatenate(top, axis=1)
        size = up_ref.shape[1] // BLOCKS
        line = lax.broadcasted_iota(jnp.int32, (16, width), 0)
        pad = jnp.zeros((1, width - size), f32)
        for place in range(4):
            for target, core in ((keep_ref, 0), (send_ref, 1)):
                number = 2 * place + core
                block = index ^ number
                start = pl.multiple_of(block * rows, 16)
                target[place, :rows] = acc_ref[pl.ds(start, rows)].astype(bf16)
                low = up_ref[:, pl.ds(pl.multiple_of(block * size, size), size)]
                low = jnp.concatenate([low, pad], axis=1)
                extra = jnp.where(line == 0, top[number : number + 1], 0.0)
                extra = jnp.where(line == 1, low, extra)
                target[place, rows:] = extra.astype(bf16)


def norm1(
    index, d_hiddens, d_summed, normed, root, gain, context, sums, sums_up, pieces, after=(), step=512
):
    count, width = d_summed.shape
    meta = meta_of(pieces)
    part = width // BLOCKS + 16
    block = pl.BlockSpec((step, width), lambda i, s: (i, 0))
    return call(
        functools.partial(norm1_kernel, meta, len(d_hiddens)),
        (count // step,),
        [block] * len(d_hiddens)
        + [
            block,
            block,
            pl.BlockSpec((step, 1), lambda i, s: (i, 0)),
            whole(gain.shape),
            block,
            whole(sums.shape),
            whole(sums_up.shape),
        ]
        + [ANY] * len(meta),
        [block, block, whole((4, part, width)), whole((4, part, width))],
        [
            shaped((count, width), f32),
            shaped((count, width), bf16),
            shaped((4, part, width), bf16),
            shaped((4, part, width), bf16),
        ],
        [
            pltpu.VMEM((width, width), bf16),
            pltpu.VMEM((width, width), f32),
            pltpu.VMEM((SEGS, width), f32),
            pltpu.SemaphoreType.DMA((len(meta),)),
        ],
        count * width * width * 4,
        count * width * 20 + width * width * 4,
        0,
        after,
        near=tuple(range(1, 2 + len(d_hiddens))) + (6, 7, 8, -1, -2, -3, -4),
    )(
        index, *d_hiddens, d_summed, normed, root, gain, context, sums, sums_up, *arrays_of(pieces)
    )


def attend_back_kernel(
    first, index_ref, q_ref, k_ref, v_ref, dctx_ref, lse_ref, seg_ref, tt_ref, *rest
):
    dq_ref, dk_ref, dv_ref, keep_ref, send_ref = rest[:5]
    mask_ref, kt_ref, two_ref, pt_ref, both_ref = rest[5:]
    rows, _, length = seg_ref.shape
    lanes = 2 * tt_ref.shape[0] // HEADS
    half = lanes // 2
    group = q_ref.shape[1] // lanes
    inv_root = 1.0 / math.sqrt(half)

    @pl.when(pl.program_id(0) == 0)
    def _():
        for row in range(rows):
            fill_mask(seg_ref[row].astype(f32), mask_ref.at[row])

    tiles = [
        (pair, row, band) for pair in range(group) for row in range(rows) for band in bands(length)
    ]
    for pair in range(group):
        for row in range(rows):
            here = slice(row * length, (row + 1) * length)
            kt_ref[pair, row] = k_ref[here, pair * lanes : (pair + 1) * lanes].T

    def begin(tile):
        pair, row, (lo, hi, at) = tile
        cols = slice(pair * lanes, (pair + 1) * lanes)
        base = row * length
        queries = two_heads(q_ref[base + at : base + at + TILE, cols])
        d_context = two_heads(dctx_ref[base + at : base + at + TILE, cols])
        two_ref[0, pair, row, 2 * at : 2 * at + 2 * TILE] = queries
        two_ref[1, pair, row, 2 * at : 2 * at + 2 * TILE] = d_context
        scores = dot_nt(k_ref[base + lo : base + hi, cols], queries)
        return scores, dot_nt(v_ref[base + lo : base + hi, cols], d_context)

    def middle_part(tile, scores, d_probs):
        pair, row, (lo, hi, at) = tile
        lse = jnp.concatenate(
            [lse_ref[row, pair, head : head + 1, at : at + TILE] for head in range(2)], axis=1
        )
        probs = jnp.exp(scores + twice(mask_ref[row, lo:hi, at : at + TILE]) - lse)
        inner = jnp.sum(d_probs * probs, axis=0, keepdims=True)
        d_scores = (probs * (d_probs - inner)).astype(bf16)
        pt_ref[0, pair, row, lo:hi, 2 * at : 2 * at + 2 * TILE] = d_scores
        pt_ref[1, pair, row, lo:hi, 2 * at : 2 * at + 2 * TILE] = probs.astype(bf16)
        return d_scores

    def put(tile, kind, value):
        pair, row, (_, _, at) = tile
        here = slice(row * length + at, row * length + at + TILE)
        cols = slice((kind * group + pair) * lanes, (kind * group + pair + 1) * lanes)
        both_ref[here, cols] = value.astype(bf16)

    def end(tile, d_scores):
        pair, row, (lo, hi, at) = tile
        dq = dot(kt_ref[pair, row, :, lo:hi], d_scores) * inv_root
        dq = jnp.concatenate([dq[:half, :TILE], dq[half:, TILE:]], axis=0)
        put(tile, 0, dq.T)

    def end_keys(tile):
        pair, row, (lo, hi, at) = tile
        cols = slice(2 * lo, 2 * hi)
        for kind in range(2):
            value = dot(
                pt_ref[kind, pair, row, at : at + TILE, cols], two_ref[kind, pair, row, cols]
            )
            put(tile, 1 + kind, value)

    ready = {}
    done = {}
    for step in range(len(tiles) + 3):
        if step < len(tiles):
            ready[step] = begin(tiles[step])
        if 0 <= step - 1 < len(tiles):
            done[step - 1] = middle_part(tiles[step - 1], *ready.pop(step - 1))
        if 0 <= step - 2 < len(tiles):
            end(tiles[step - 2], done.pop(step - 2))
        if 0 <= step - 3 < len(tiles):
            end_keys(tiles[step - 3])
    both = both_ref[...]
    wide = group * lanes
    for kind, target in enumerate((dq_ref, dk_ref, dv_ref)):
        target[...] = both[:, kind * wide : (kind + 1) * wide]
    grad = dot(tt_ref[...], both).astype(bf16)
    width = grad.shape[0]
    part = width // BLOCKS
    span = both.shape[1]
    col = lax.broadcasted_iota(jnp.int32, (1, span), 1)
    kind = col // wide
    place = (pl.program_id(0) * group + first) * lanes + col - kind * wide
    owner = jnp.where(kind == 1, -1, (place + jnp.where(kind == 2, width, 0)) // (2 * part))
    sums = column_sum(both.astype(f32))
    line = lax.broadcasted_iota(jnp.int32, (16, span), 0)
    for block in range(BLOCKS):
        target, core = (keep_ref, 0) if block < 4 else (send_ref, 1)
        target[block % 4, :part] = grad[block * part : (block + 1) * part]
        here = owner == (index_ref[0] ^ (2 * (block % 4) + core))
        extra = jnp.where(line == 0, jnp.where(here, sums, 0.0), 0.0)
        target[block % 4, part:] = extra.astype(bf16)


def attend_back(
    index, qkv, d_context, lse, seg_rows, turned, first, pairs, after=(), group=2
):
    width, count = turned.shape
    rows, _, length = seg_rows.shape
    every = HEADS // 2
    lanes = width // every
    part = width // BLOCKS + 16
    wide = group * lanes
    column = lambda place: pl.BlockSpec((count, wide), lambda i, s: (0, place // group + i))
    out = pl.BlockSpec((count, wide), lambda i, s: (0, i))
    grads = pl.BlockSpec((4, part, 3 * wide), lambda i, s: (0, 0, i))
    return call(
        functools.partial(attend_back_kernel, first),
        (pairs // group,),
        [
            column(first),
            column(every + first),
            column(2 * every + first),
            column(first),
            pl.BlockSpec((rows, group, 2, length), lambda i, s: (0, first // group + i, 0, 0)),
            whole((rows, 1, length)),
            HELD,
        ],
        [out, out, out, grads, grads],
        [
            shaped((count, pairs * lanes), bf16),
            shaped((count, pairs * lanes), bf16),
            shaped((count, pairs * lanes), bf16),
            shaped((4, part, pairs * 3 * lanes), bf16),
            shaped((4, part, pairs * 3 * lanes), bf16),
        ],
        [
            pltpu.VMEM((rows, length, length), f32),
            pltpu.VMEM((group, rows, lanes, length), bf16),
            pltpu.VMEM((2, group, rows, 2 * length, lanes), bf16),
            pltpu.VMEM((2, group, rows, length, 2 * length), bf16),
            pltpu.VMEM((count, 3 * wide), bf16),
        ],
        count * pairs * lanes * (width * 6 + length * 6),
        count * pairs * lanes * 14 + count * width * 2,
        count * length * pairs * 5 // 4,
        after,
        near=(4, 5, 7, -1, -2, -3, -4, -5),
    )(index, qkv, qkv, qkv, d_context, lse, seg_rows, turned)


def input_kernel(meta, parts, index_ref, dattn_ref, *rest):
    grads, rest = rest[: 3 * parts], rest[3 * parts :]
    pieces, rest = rest[: len(meta)], rest[len(meta) :]
    out_ref, w_ref, sems = rest
    width = out_ref.shape[1]
    step = width // parts
    first = pl.program_id(0) == 0

    def weights(kind):
        cols = columns(kind, width)
        rows = width // BLOCKS
        return copies_of(meta, rows, pieces, w_ref, sems.at[kind], index_ref[0], cols, cols)

    @pl.when(first)
    def _():
        for kind in range(3):
            start_all(weights(kind))

    total = dattn_ref[...]
    for kind in range(3):

        @pl.when(first)
        def _():
            wait_all(weights(kind))

        for part in range(parts):
            at = kind * width + part * step
            total += dot_nt(grads[kind * parts + part][...], w_ref[:, at : at + step])
    out_ref[...] = total


def input_grad(index, d_attn, grads, pieces, after=(), step=512):
    count, width = d_attn.shape
    meta = meta_of(pieces)
    parts = len(grads) // 3
    block = pl.BlockSpec((step, width), lambda i, s: (i, 0))
    return call(
        functools.partial(input_kernel, meta, parts),
        (count // step,),
        [block]
        + [pl.BlockSpec((step, g.shape[1]), lambda i, s: (i, 0)) for g in grads]
        + [ANY] * len(meta),
        [block],
        [shaped((count, width), f32)],
        [pltpu.VMEM((width, 3 * width), bf16), pltpu.SemaphoreType.DMA((3, len(meta)))],
        count * width * width * 6,
        count * width * 14 + width * width * 6,
        0,
        after,
        near=tuple(range(1, 2 + len(grads))),
    )(index, d_attn, *grads, *arrays_of(pieces))


def rounded(value):
    return lax.optimization_barrier(value.astype(bf16))


def add(*values):
    total = values[0].astype(f32)
    for value in values[1:]:
        total = total + value.astype(f32)
    return total


def along_z(value, pairs):
    return lax.ppermute(value, "batch", pairs)


def core_kernel(parts, index_ref, *refs):
    keeps, others = refs[:parts], refs[parts : 2 * parts]
    mine_ref, x_ref, y_ref, *far_refs = refs[2 * parts :]
    at = 0
    for keep, other in zip(keeps, others):
        cols = slice(at, at + keep.shape[2])
        at = cols.stop
        for place, target in enumerate((mine_ref, x_ref, y_ref)):
            target[:, cols] = add(keep[place], other[place]).astype(bf16)
        far = add(keep[3], other[3]).astype(bf16)
        row = 0
        for far_ref in far_refs:
            far_ref[:, cols] = far[row : row + far_ref.shape[0]]
            row += far_ref.shape[0]


def add_cores(index, keeps, others, whole_far):
    rows = keeps[0].shape[1]
    width = sum(keep.shape[2] for keep in keeps)
    half = rows // 32 * 16
    heights = (rows, rows, rows) + ((rows,) if whole_far else (half, rows - half))
    count = 2 * len(keeps)
    return call(
        functools.partial(core_kernel, len(keeps)),
        (1,),
        [HELD] * count,
        [HELD] * len(heights),
        [shaped((height, width), bf16) for height in heights],
        [],
        rows * width * 4,
        rows * width * 24,
        near=tuple(range(1, 1 + count)) + (-1, -2, -3, -4, -5)[: len(heights)],
    )(index, *keeps, *others)


class Sum:
    def __init__(self, index, planes, keeps, sends, line, axis=None):
        self.index, self.planes, self.keeps, self.line = index, planes, keeps, line
        self.axis = axis
        self.arrived = [fsdp_swap(send, 1) for send in sends]
        self.stages = [self.over_core, self.over_far, self.over_chips, self.over_z, self.over_middle]

    def next(self, clock):
        *self.arrived, _ = lax.optimization_barrier((*self.arrived, clock))
        return list(self.stages.pop(0)(*self.arrived))

    def over_core(self, *others):
        *self.blocks, _ = add_cores(self.index, self.keeps, others, self.axis is not None)
        far = self.blocks[3:]
        axes = (2, 4) if self.axis is None else (self.axis,)
        self.arrived = [fsdp_swap(block, axis) for block, axis in zip(far, axes)]
        return far

    def over_far(self, *arrived):
        over_x, over_y = self.blocks[1:3]
        if self.axis is None:
            top, low = arrived
            half = top.shape[0]
            over_x = over_x.at[half:].set(add(over_x[half:], low).astype(bf16))
            over_y = over_y.at[:half].set(add(over_y[:half], top).astype(bf16))
        elif self.axis == 2:
            over_y = rounded(add(over_y, arrived[0]))
        else:
            over_x = rounded(add(over_x, arrived[0]))
        self.arrived = [fsdp_swap(over_x, 2), fsdp_swap(over_y, 4)]
        return [over_x, over_y]

    def over_chips(self, from_x, from_y):
        self.total = rounded(add(self.blocks[0], from_x, from_y))
        sent = self.total
        if self.line:
            self.arrived = [along_z(sent, [(0, 1), (3, 2)])]
            return [sent]
        half = sent.shape[0] // 2
        self.odd = lax.axis_index("batch") % 2 == 1
        self.total = jnp.where(self.odd, sent[half:], sent[:half])
        sent = jnp.where(self.odd, sent[:half], sent[half:])
        self.arrived = [swap(sent, "batch", self.planes, 1)]
        return [sent]

    def over_z(self, other):
        self.total = rounded(add(self.total, other))
        pairs = [(1, 2), (2, 1)] if self.line else [(0, 2), (2, 0), (1, 3), (3, 1)]
        self.arrived = [along_z(self.total, pairs)]
        return [self.total]

    def over_middle(self, other):
        self.total = rounded(add(self.total, other))
        pairs = [(1, 0), (2, 3)] if self.line else [(0, 1), (1, 0), (2, 3), (3, 2)]
        self.arrived = [along_z(self.total, pairs)]
        return [self.total]

    def result(self):
        other = self.arrived[0]
        if self.line:
            plane = lax.axis_index("batch")
            inside = (plane == 1) | (plane == 2)
            return jnp.where(inside, self.total, other).astype(f32)
        upper = jnp.where(self.odd, other, self.total)
        lower = jnp.where(self.odd, self.total, other)
        return jnp.concatenate([upper, lower], axis=0).astype(f32)


def layer(
    planes,
    ring,
    tokens,
    seg_ids,
    positive,
    out_grad,
    w_qkv,
    b_qv,
    w_out,
    b_out,
    norm1_gain,
    norm1_shift,
    w_up,
    b_up,
    w_down,
    b_down,
    norm2_gain,
    norm2_shift,
):
    paired = ring == BLOCKS and planes == 4
    row_count, row_length, width = tokens.shape
    count = row_count * row_length
    own = row_count * SEGS
    token_rows = tokens.reshape(count, width)
    seg_rows = seg_ids.reshape(row_count, 1, row_length)
    pos_col = positive.reshape(own, 1)
    fsdp = lax.axis_index("fsdp")
    me = lax.axis_index("batch") * ring + fsdp
    index = (fsdp if paired else jnp.zeros_like(fsdp)).reshape(1).astype(jnp.int32)
    tie = lax.optimization_barrier

    small = (b_out, norm1_gain, norm1_shift, b_down, norm2_gain, norm2_shift, b_up)
    sizes = [value.shape[0] * ring // BLOCKS for value in small]
    inner = sizes[-1] * BLOCKS
    if paired:
        first = pack_first(w_qkv, b_qv)
        first_xy = first_stage(first)
        *first_xy, second = tie((*first_xy, pack_second(w_out, w_up, *small)))
        first_far = second_stage(first, *first_xy)
        second, *first_far = tie((second, *first_far))
        second_xy = first_stage(second)
        qkv_pieces = both_cores(own_pieces(first, *first_xy))
        qkv_pieces += both_cores(far_pieces(first, *first_far))
    else:
        blocks = [gather_whole(value) for value in (w_qkv, b_qv, w_down, w_out, w_up, *small)]
        blocks = list(enumerate(zip(*blocks)))
        qkv_pieces = [(pack_first(*b[:2]), i, 0) for i, b in blocks]
        down_pieces = [(b[2], i, 0) for i, b in blocks]
        mid_pieces = [(pack_second(*b[3:]), i, 0) for i, b in blocks]

    qkv, clock = project_qkv(index, token_rows, qkv_pieces, 2 * width // BLOCKS)
    attended = ()
    for row in range(row_count):
        late = ()
        if paired and row == row_count - 1:
            *second_xy, third, clock = tie((*second_xy, w_down, clock))
            second_far = second_stage(second, *second_xy)
            third_xy = first_stage(third)
            late = (*second_xy, clock)
        *attended, clock = attend(index, qkv, seg_rows, row, attended, late)
    context, lse = attended
    if paired:
        mid_pieces = both_cores(own_pieces(second, *second_xy))
        *second_far, clock = tie((*second_far, clock))
        mid_pieces += both_cores(far_pieces(second, *second_far))
    normed1, root1, hidden, rows, bias_up, clock = project(
        index, context, token_rows, mid_pieces, sizes, (clock,)
    )
    hidden_turned, tokens_turned, clock = hold_turned(index, hidden, token_rows, (clock,))
    late = (clock,)
    if paired:
        *third_xy, clock = tie((*third_xy, clock))
        third_far = fsdp_swap(third_xy[0], 4)
        late = (*third_xy, clock)
    activated, slope, clock = up(index, hidden, bias_up, mid_pieces, late)
    if paired:
        down_pieces = both_cores(own_pieces(w_down, *third_xy))
        third_far, clock = tie((third_far, clock))
        down_pieces += both_cores([(third_far, 6, 0)])
    result, normed2, root2, payload, pooled, stats, _ = down(
        index, activated, normed1, rows, seg_rows, pos_col, down_pieces, (clock,)
    )

    wd_full, clock = hold_weights(index, down_pieces, (inner, width), 0, (payload,))
    if paired:
        line = [payload] + [swap(payload, "batch", planes, bit) for bit in (1, 2, 3)]
        *line, clock = tie((*line, clock))
        line = jnp.concatenate(line, axis=0)
        plane = [line] + [fsdp_swap(line, bit) for bit in (2, 4, 6)]
        wu_full, clock = hold_weights(index, mid_pieces, (width, inner), width, (line, clock))
        *plane, clock = tie((*plane, clock))
        everyone = list(plane) + [fsdp_swap(value, 1) for value in plane]
        layout = (2, ring // 2, planes)
        flip = me * own
    else:
        wu_full, clock = hold_weights(index, mid_pieces, (width, inner), width)
        everyone = [lax.all_gather(payload, ("batch", "fsdp"), axis=0, tiled=True)]
        layout = (1, planes * ring, 1)
        flip = jnp.zeros_like(me)
    place = jnp.stack([flip, me * own]).astype(jnp.int32)
    pair_loss, d_pool, _ = contrast(
        place, layout, everyone, payload, pos_col, pooled, stats, (clock,)
    )

    def start(keeps, sends, line, axis=None):
        return Sum(index, planes, keeps, sends, line, axis) if paired else None

    def go(results, *sums):
        sent, clock = [], results[0]
        for one in sums:
            if one is not None:
                stage = one.next(clock)
                clock = stage[0]
                sent += stage
        if sent:
            results = tie((*results, *sent))[: len(results)]
        return results, tuple(sent)

    d_summed, d_down, sums2, keep_down, send_down, _ = norm2(
        index,
        out_grad.reshape(count, width),
        normed2,
        root2,
        seg_rows,
        rows,
        d_pool,
        activated,
    )
    sum_down = start([keep_down], [send_down], True)
    half, sent = (), ()
    for first in (0, 2):
        half = up_back(
            index, d_down, slope, hidden_turned, wd_full, wu_full, first, 2, tuple(half), sent
        )[:4]
        half, sent = go(half, sum_down)
    d_hidden, sums_up, keep_up, send_up = half
    sum_up = start([keep_up], [send_up], False)
    *first_norm, _ = norm1(
        index,
        [d_hidden],
        d_summed,
        normed1,
        root1,
        rows,
        context,
        sums2,
        sums_up,
        mid_pieces,
        sent,
    )
    (d_attn, d_context, keep_out, send_out), sent = go(first_norm, sum_up)
    pairs = HEADS // 2
    cuts = 3
    backs = []
    for cut in range(cuts):
        *back, _ = attend_back(
            index,
            qkv,
            d_context,
            lse,
            seg_rows,
            tokens_turned,
            cut * pairs // cuts,
            pairs // cuts,
            sent,
        )
        if cut == 0:
            back, sent = go(back, sum_down, sum_up)
            sum_left = start([keep_out, back[3]], [send_out, back[4]], True, 2)
        if cut == 1:
            back, sent = go(back, sum_left)
        if cut == 2:
            sum_right = start([backs[1][3], back[3]], [backs[1][4], back[4]], False, 4)
            back, sent = go(back, sum_down, sum_up, sum_left, sum_right)
        backs.append(back)
    grads = [backs[cut][kind] for kind in range(3) for cut in range(cuts)]
    grad_tokens, _ = input_grad(index, d_attn, grads, qkv_pieces, sent)

    lanes = width // pairs

    part = width // BLOCKS
    if paired:
        (grad_tokens,), sent = go((grad_tokens,), sum_right, sum_down, sum_up)
        _, sent = go(sent, sum_left)
        _, sent = go(sent, sum_right)
        _, sent = go(sent, sum_up, sum_left)
        _, sent = go(sent, sum_right, sum_left)
        go(sent, sum_right)
        grad_down, grad_up = sum_down.result().T, sum_up.result()
        left, right = sum_left.result(), sum_right.result()
        grad_out = left[:part, :width]
        joined = [left[:, width:], right[:, :width], right[:, width:]]
        own_vectors = [left[part, i * TILE : i * TILE + part] for i in range(6)]
        own_vectors.append(left[part + 1, : sizes[-1]])
    else:

        def scatter(keep, send):
            full = lax.psum(jnp.stack([keep, send], axis=1).astype(f32), "batch")
            return full.reshape((BLOCKS,) + full.shape[2:])

        def own_rows(full):
            full = full.reshape((-1,) + full.shape[2:])
            return lax.psum_scatter(full, "fsdp", scatter_dimension=0, tiled=True)

        def own_values(full):
            return lax.psum_scatter(full.reshape(-1), "fsdp", scatter_dimension=0, tiled=True)

        grad_down = own_rows(scatter(keep_down, send_down).transpose(0, 2, 1))
        grad_up = own_rows(scatter(keep_up, send_up))
        left = scatter(keep_out, send_out)
        grad_out = own_rows(left[:, :part])
        own_vectors = [own_values(left[:, part, i * TILE : i * TILE + part]) for i in range(6)]
        own_vectors.append(own_values(left[:, part + 1, : sizes[-1]]))
        whole_grads = [scatter(back[3], back[4]) for back in backs]
        joined = []
        for grads in whole_grads:
            line = lax.psum(jnp.sum(grads[:, part], axis=0), "fsdp")
            joined.append(jnp.concatenate([own_rows(grads[:, :part]), line[None]], axis=0))

    span = width // cuts
    ordered = [
        group[:, kind * span : (kind + 1) * span] for kind in range(3) for group in joined
    ]
    depth = joined[0].shape[0] - 1 if not paired else part
    grad_qkv = jnp.concatenate([group[:depth] for group in ordered], axis=1)
    vector = jnp.concatenate([group[depth] for group in ordered[:cuts] + ordered[2 * cuts :]])
    shard = vector.shape[0] // ring
    grad_bqv = lax.dynamic_slice(vector, (fsdp * shard,), (shard,))
    grad_bout, grad_g1, grad_s1, grad_bdown, grad_g2, grad_s2, grad_bup = own_vectors
    return (
        result.reshape(tokens.shape),
        pair_loss.reshape(own),
        grad_tokens.reshape(tokens.shape),
        grad_qkv,
        grad_bqv,
        grad_out,
        grad_bout,
        grad_g1,
        grad_s1,
        grad_up,
        grad_bup,
        grad_down,
        grad_bdown,
        grad_g2,
        grad_s2,
    )


def solution(mesh):
    rows = P(("batch", "fsdp"), None, None)
    matrix = P("fsdp", None)
    vector = P("fsdp")
    placed = (
        rows,
        P(("batch", "fsdp"), None),
        P(("batch", "fsdp")),
        rows,
        matrix,
        vector,
        matrix,
        vector,
        vector,
        vector,
        matrix,
        vector,
        matrix,
        vector,
        vector,
        vector,
    )
    given = (
        rows,
        P(("batch", "fsdp")),
        rows,
        matrix,
        vector,
        matrix,
        vector,
        vector,
        vector,
        matrix,
        vector,
        matrix,
        vector,
        vector,
        vector,
    )
    return jax.shard_map(
        functools.partial(layer, mesh.shape["batch"], mesh.shape["fsdp"]),
        mesh=mesh,
        in_specs=placed,
        out_specs=given,
        check_vma=False,
    )
```
